32 devices in a mesh: rep: 4 (over y, x), shard: 8 (over z, core).
Axes of the slice: x: 2, y: 2, z: 4, core: 2. Of those that a mesh axis runs over, the one named last changes fastest.
Arguments:
- tokens: bfloat16 [16384, 1024], P(('rep', 'shard')), may hold values from -6 to 6
- lengths: int32 [32, 4], P(('rep', 'shard')), may hold values from 1 to 256, 512 in all within a row
- group_live: int32 [4], P('rep'), may hold values from 128 to 512, as said below
- w_query: bfloat16 [1024, 1024], P('shard'), may hold values from -0.1875 to 0.1875
- w_key: bfloat16 [1024, 512], P('shard'), may hold values from -0.1875 to 0.1875
- w_value: bfloat16 [1024, 512], P('shard'), may hold values from -0.1875 to 0.1875
- w_out: bfloat16 [1024, 1024], P('shard'), may hold values from -0.75 to 0.75
- w_gate: bfloat16 [1024, 4608], P('shard'), may hold values from -0.1875 to 0.1875
- w_up: bfloat16 [1024, 4608], P('shard'), may hold values from -0.1875 to 0.1875
- w_down: bfloat16 [4608, 1024], P('shard'), may hold values from -0.09375 to 0.09375
- g_attn: bfloat16 [1024], P('shard'), may hold values from 0.099609375 to 1.8984375
- g_query: bfloat16 [64], P('shard'), may hold values from 0.099609375 to 1.8984375
- g_key: bfloat16 [64], P('shard'), may hold values from 0.099609375 to 1.8984375
- g_ffn: bfloat16 [1024], P('shard'), may hold values from 0.099609375 to 1.8984375
- cotangent: bfloat16 [16384, 1024], P(('rep', 'shard')), may hold values from -6 to 6
Outputs:
- block_out: bfloat16 [16384, 1024], P(('rep', 'shard'))
- grad_tokens: bfloat16 [16384, 1024], P(('rep', 'shard'))
- grad_w_query: float32 [1024, 1024], P('shard')
- grad_w_key: float32 [1024, 512], P('shard')
- grad_w_value: float32 [1024, 512], P('shard')
- grad_w_out: float32 [1024, 1024], P('shard')
- grad_w_gate: float32 [1024, 4608], P('shard')
- grad_w_up: float32 [1024, 4608], P('shard')
- grad_w_down: float32 [4608, 1024], P('shard')
- grad_g_attn: float32 [1024], P('shard')
- grad_g_query: float32 [64], P('shard')
- grad_g_key: float32 [64], P('shard')
- grad_g_ffn: float32 [1024], P('shard')
The draws below stay inside these ranges and needn't reach their ends.
Inputs may be any that keep to these rules, and one draw needn't show every extreme that they name: Each device's row holds 4 sequence lengths that sum to 512, the largest exactly 256. `group_live`: slots of a device at or past its group's count are padding; one group is full and one holds 128.
All inputs are finite; a program needn't handle non-finite values.
Results may differ from the reference program's by a relative error of at most 0.028.
Values may be sent and summed in bfloat16 or wider, within the bound.
No kernel may reach another device: no remote copies, remote signals or barrier semaphores. Data moves between devices by JAX's collectives and lax.ppermute only.
A program may use at most 256 MiB of HBM per device.

```python
import math
import jax
import jax.numpy as jnp
import numpy as np
from jax import lax

D = 1024
H = 16
KV = 8
HD = 64
FF = 4608
TOK_DEV = 512
LONGEST = 256
SLOTS = 4
GROUPS = 4
GROUP_RANKS = 8
RANKS = 32
TOKENS = 16384


def draw_group_live(key, part):
    key = jax.random.fold_in(key, 11)
    key_counts, key_fullest, key_offset = jax.random.split(key, 3)
    counts = jax.random.randint(key_counts, (GROUPS,), TOK_DEV // 4, TOK_DEV + 1, dtype=jnp.int32)
    fullest = jax.random.randint(key_fullest, (), 0, GROUPS, dtype=jnp.int32)
    offset = jax.random.randint(key_offset, (), 1, GROUPS, dtype=jnp.int32)
    lightest = (fullest + offset) % GROUPS
    group_index = jnp.arange(GROUPS, dtype=jnp.int32)
    counts = jnp.where(group_index == fullest, TOK_DEV, counts)
    counts = jnp.where(group_index == lightest, TOK_DEV // 4, counts)
    return counts.astype(jnp.int32)


def steps_of(key, extent, pieces, smallest, largest):
    level = 1.0
    for axis_at, shards_of in pieces:
        draws = jax.random.uniform(jax.random.fold_in(jax.random.fold_in(key, 6), axis_at), (shards_of,), jnp.float32, smallest / len(pieces), largest / len(pieces))
        level = level * jnp.repeat(jnp.exp(draws), extent[axis_at] // shards_of).reshape((-1,) + (1,) * (len(extent) - 1 - axis_at))
    return level


def split_up(amount, total, limit, slope):
    weights = [(1 << 20) // math.isqrt(rank ** slope) + 1 for rank in range(2, amount + 1)]
    surplus, given = total - limit - (amount - 1), [1] * (amount - 1)
    while surplus > 0:
        candidates = [i for i in range(amount - 1) if given[i] < limit]
        pool, budget = sum([weights[i] for i in candidates]), surplus
        for i in candidates:
            extra = min(limit - given[i], max(1, budget * weights[i] // pool), surplus)
            given[i] = given[i] + extra
            surplus = surplus - extra
    return np.array([limit] + given)


def ragged(key, count, total, bound, slope):
    if count == 2:
        one = jax.random.randint(key, (), max(1, total - bound), min(bound, total - 1) + 1)
        return jnp.stack([one, total - one])
    tallies = jnp.asarray(split_up(count, total, bound, slope), jnp.int32)
    couples = (count - 1) // 2
    donor, sink = tallies[1:1 + 2 * couples:2], tallies[2:2 + 2 * couples:2]
    room = jnp.minimum(donor - 1, bound - sink)
    passed = jax.random.randint(jax.random.fold_in(key, 1), (couples,), 0, 1 << 20) % (room + 1)
    tallies = tallies.at[1:1 + 2 * couples:2].set(donor - passed).at[2:2 + 2 * couples:2].set(sink + passed)
    return tallies[jax.random.permutation(jax.random.fold_in(key, 2), count)]


def scatter_about(own_key, extent, spread, most, pieces=(), kind=jnp.bfloat16):
    result = jax.random.normal(own_key, extent, jnp.float32) * spread
    if len(pieces) > 0:
        result = steps_of(own_key, extent, pieces, -0.22, 0.18) * result
    return jnp.clip(result, min=-most, max=most).astype(kind)


def setup_inputs(seed: int = 0) -> dict:
    arg_keys = jax.random.split(jax.random.key(seed), 16)
    return {
        "tokens": scatter_about(arg_keys[0], (TOKENS, D), 1.0, 6.0, ((0, 32),)),
        "lengths": jax.vmap(lambda own: ragged(own, SLOTS, TOK_DEV, LONGEST, 1))(jax.random.split(arg_keys[1], RANKS)).reshape((RANKS, SLOTS)).astype(jnp.int32),
        "group_live": draw_group_live(jax.random.fold_in(arg_keys[15], 71), 0),
        "w_query": scatter_about(arg_keys[3], (D, H * HD), D ** -0.5, 0.1875, ((0, 8),)),
        "w_key": scatter_about(arg_keys[4], (D, KV * HD), D ** -0.5, 0.1875, ((0, 8),)),
        "w_value": scatter_about(arg_keys[5], (D, KV * HD), D ** -0.5, 0.1875, ((0, 8),)),
        "w_out": scatter_about(arg_keys[6], (H * HD, D), (H * HD // 16) ** -0.5, 0.75, ((0, 8),)),
        "w_gate": scatter_about(arg_keys[7], (D, FF), D ** -0.5, 0.1875, ((0, 8),)),
        "w_up": scatter_about(arg_keys[8], (D, FF), D ** -0.5, 0.1875, ((0, 8),)),
        "w_down": scatter_about(arg_keys[9], (FF, D), FF ** -0.5, 0.09375, ((0, 8),)),
        "g_attn": jnp.clip(1.0 + 0.18 * jax.random.normal(arg_keys[10], (D,), jnp.float32), 0.099609375, 1.8984375).astype(jnp.bfloat16),
        "g_query": jnp.clip(1.0 + 0.18 * jax.random.normal(arg_keys[11], (HD,), jnp.float32), 0.099609375, 1.8984375).astype(jnp.bfloat16),
        "g_key": jnp.clip(1.0 + 0.18 * jax.random.normal(arg_keys[12], (HD,), jnp.float32), 0.099609375, 1.8984375).astype(jnp.bfloat16),
        "g_ffn": jnp.clip(1.0 + 0.18 * jax.random.normal(arg_keys[13], (D,), jnp.float32), 0.099609375, 1.8984375).astype(jnp.bfloat16),
        "cotangent": scatter_about(arg_keys[14], (TOKENS, D), 1.0, 6.0, ((0, 32),)),
    }


@jax.custom_vjp
def low(v):
    return lax.optimization_barrier(v.astype(jnp.bfloat16)).astype(jnp.float32)

@jax.custom_vjp
def low_back(v):
    return v

def low_keep(v):
    return (low(v), None)

def low_pass(kept, grad):
    return (grad,)

def back_keep(v):
    return (v, None)

def back_low(kept, grad):
    return (low(grad),)
low.defvjp(low_keep, low_pass)
low_back.defvjp(back_keep, back_low)
epsilon = 1e-05
theta_base = 1000000.0
masked_score = -1e+30

def matmul(left, right):
    return jnp.dot(left, right, precision=lax.Precision.HIGHEST, preferred_element_type=jnp.float32)

def rms_norm(values, gain):
    return values * lax.rsqrt(lax.optimization_barrier(jnp.mean(values * values, axis=-1, keepdims=True)) + epsilon) * gain

def layout(seq_lengths, live_rows, row_count):
    row_index = jnp.arange(row_count, dtype=jnp.int32)
    seq_ends = jnp.cumsum(seq_lengths).astype(jnp.int32)
    passed_ends = row_index[:, None] >= seq_ends[None, :]
    segment = lax.optimization_barrier(jnp.sum(passed_ends.astype(jnp.int32), axis=1, dtype=jnp.int32))
    begins = lax.optimization_barrier(jnp.sum(jnp.where(passed_ends, seq_lengths[None, :], 0), axis=1, dtype=jnp.int32))
    live_mask = row_index < live_rows
    segment = jnp.where(live_mask, segment, -1).astype(jnp.int32)
    position = (row_index - begins).astype(jnp.float32)
    return (row_index, segment, position, live_mask.astype(jnp.float32))

def rotary_tables(position, head_width):
    half_width = head_width // 2
    frequency = theta_base ** (-2.0 * jnp.arange(half_width, dtype=jnp.float32) / head_width)
    angles = position[:, None] * frequency[None, :]
    return (jnp.cos(angles)[:, None, :], jnp.sin(angles)[:, None, :])

def rotate(values, cosine, sine):
    half_width = values.shape[-1] // 2
    front_part = values[..., :half_width]
    back_part = values[..., half_width:]
    return jnp.concatenate([front_part * cosine - back_part * sine, back_part * cosine + front_part * sine], axis=-1)

def attend(query, keys, values, segment, row_index):
    row_count, kv_heads, head_width = keys.shape
    groups = query.shape[1] // kv_heads
    grouped = query.reshape(row_count, kv_heads, groups, head_width)
    raw_scores = jnp.einsum('qkgd,tkd->kgqt', grouped, keys, precision=lax.Precision.HIGHEST) * head_width ** (-0.5)
    raw_scores = low_back(raw_scores)
    allowed = (segment[:, None] == segment[None, :]) & (row_index[None, :] <= row_index[:, None])
    scores = jnp.where(allowed, raw_scores, masked_score)
    top_score = lax.optimization_barrier(jnp.max(scores, axis=-1, keepdims=True))
    weights = jnp.exp(scores - top_score)
    probability = weights / lax.optimization_barrier(jnp.sum(weights, axis=-1, keepdims=True))
    attended = jnp.einsum('kgqt,tkd->qkgd', low(probability), values, precision=lax.Precision.HIGHEST)
    return attended.reshape(row_count, query.shape[1] * head_width)

def layer_rows(x_rows, seq_lengths, live_rows, params):
    w_query, w_key, w_value, w_out, w_gate, w_up, w_down, g_attn, g_query, g_key, g_ffn = params
    row_index, segment, position, keep_mask = layout(seq_lengths, live_rows, x_rows.shape[0])
    cosine, sine = rotary_tables(position, HD)
    attn_input = low(rms_norm(x_rows, g_attn))
    q_raw = low_back(matmul(attn_input, w_query)).reshape(-1, H, HD)
    k_raw = low_back(matmul(attn_input, w_key)).reshape(-1, KV, HD)
    v_low = low(low_back(matmul(attn_input, w_value))).reshape(-1, KV, HD)
    q_low = low(rotate(rms_norm(q_raw, g_query), cosine, sine))
    k_low = low(rotate(rms_norm(k_raw, g_key), cosine, sine))
    attended = low(low_back(attend(q_low, k_low, v_low, segment, row_index)))
    attn_result = low_back(matmul(attended, w_out))
    hidden = x_rows + keep_mask[:, None] * attn_result
    ffn_input = low(rms_norm(hidden, g_ffn))
    gate_proj = low_back(matmul(ffn_input, w_gate))
    up_proj = low_back(matmul(ffn_input, w_up))
    inner_low = low(jax.nn.silu(gate_proj) * up_proj)
    ffn_result = low_back(matmul(inner_low, w_down))
    return hidden + keep_mask[:, None] * ffn_result

def reference(tokens, lengths, group_live, w_query, w_key, w_value, w_out, w_gate, w_up, w_down, g_attn, g_query, g_key, g_ffn, cotangent):
    params = (w_query.astype(jnp.float32), w_key.astype(jnp.float32), w_value.astype(jnp.float32), w_out.astype(jnp.float32), w_gate.astype(jnp.float32), w_up.astype(jnp.float32), w_down.astype(jnp.float32), g_attn.astype(jnp.float32), g_query.astype(jnp.float32), g_key.astype(jnp.float32), g_ffn.astype(jnp.float32))
    x_blocks = tokens.astype(jnp.float32).reshape(RANKS, TOK_DEV, D)
    live_blocks = jnp.repeat(group_live, GROUP_RANKS, total_repeat_length=RANKS).astype(jnp.int32)

    def forward(x_all, weights_all):

        def device_layer(device_item):
            return layer_rows(device_item[0], device_item[1], device_item[2], weights_all)
        return lax.map(jax.checkpoint(device_layer), (x_all, lengths, live_blocks))
    block_rows, pullback = jax.vjp(forward, x_blocks, params)
    grad_x, weight_grads = pullback(cotangent.astype(jnp.float32).reshape(RANKS, TOK_DEV, D))
    return (block_rows.reshape(TOKENS, D).astype(jnp.bfloat16), grad_x.reshape(TOKENS, D).astype(jnp.bfloat16), weight_grads[0], weight_grads[1], weight_grads[2], weight_grads[3], weight_grads[4], weight_grads[5], weight_grads[6], weight_grads[7], weight_grads[8], weight_grads[9], weight_grads[10])
```

```python
import functools

import jax
import jax.numpy as jnp
from jax import lax
from jax.experimental import pallas as pl
from jax.experimental.pallas import tpu as pltpu
from jax.sharding import PartitionSpec as P

H = 16
KV = 8
HD = 64


epsilon = 1e-05
theta_base = 1000000.0
masked_score = -1e30


def layout(seq_lengths, live_rows, row_count):
    row_index = jnp.arange(row_count, dtype=jnp.int32)
    seq_ends = jnp.cumsum(seq_lengths)
    passed_ends = row_index[:, None] >= seq_ends[None, :]
    segment = jnp.sum(passed_ends.astype(jnp.int32), axis=1, dtype=jnp.int32)
    begins = jnp.sum(jnp.where(passed_ends, seq_lengths[None, :], 0), axis=1, dtype=jnp.int32)
    live_mask = row_index < live_rows
    segment = jnp.where(live_mask, segment, -1)
    position = (row_index - begins).astype(jnp.float32)
    return (row_index, segment, position, live_mask.astype(jnp.float32))


def rotary_tables(position):
    half_width = HD // 2
    frequency = theta_base ** (-2.0 * jnp.arange(half_width, dtype=jnp.float32) / HD)
    angles = position[:, None] * frequency[None, :]
    cosine, sine = jnp.cos(angles), jnp.sin(angles)
    return (
        jnp.concatenate([cosine] * 4, axis=1),
        jnp.concatenate([-sine, sine, -sine, sine], axis=1),
    )


def normalize(values):
    inverse_rms = lax.rsqrt(jnp.mean(values * values, axis=-1, keepdims=True) + epsilon)
    return (values * inverse_rms, inverse_rms)


def norm_back(incoming, unit_values, inverse_rms, gain):
    grad_unit = incoming * gain
    grad_values = inverse_rms * (
        grad_unit - unit_values * jnp.mean(unit_values * grad_unit, axis=-1, keepdims=True)
    )
    grad_gain = jnp.sum((incoming * unit_values).reshape(-1, unit_values.shape[-1]), axis=0)
    return (grad_values, grad_gain)


def rows_product(left, right):
    return lax.dot_general(
        left, right, (((0,), (0,)), ((), ())), preferred_element_type=jnp.float32
    )


def back_product(left, right):
    return lax.dot_general(
        left, right, (((1,), (1,)), ((), ())), preferred_element_type=jnp.float32
    )


def lane_index(shape):
    return lax.broadcasted_iota(jnp.int32, shape, len(shape) - 1)


def head_mean(values):
    first = lane_index(values.shape) < HD
    low = jnp.sum(jnp.where(first, values, 0.0), axis=-1, keepdims=True)
    high = jnp.sum(jnp.where(first, 0.0, values), axis=-1, keepdims=True)
    return jnp.where(first, low, high) * (1.0 / HD)


def swap_halves(values):
    front = lane_index(values.shape) % HD < HD // 2
    return jnp.where(
        front, pltpu.roll(values, 2 * HD - HD // 2, 1), pltpu.roll(values, HD // 2, 1)
    )


def head_unit(raw):
    inverse = lax.rsqrt(head_mean(raw * raw) + epsilon)
    return raw * inverse, inverse


def head_norm_back(incoming, unit_values, inverse, gain):
    grad_unit = incoming * gain
    return inverse * (grad_unit - unit_values * head_mean(unit_values * grad_unit))


def pair_of(values, which):
    first = lane_index(values.shape) < HD
    kept = jnp.where(first, values, 0.0) if which == 0 else jnp.where(first, 0.0, values)
    moved = pltpu.roll(kept, HD, 1)
    pair = (kept, moved) if which == 0 else (moved, kept)
    return tuple(value.astype(jnp.bfloat16) for value in pair)


def dot_rows(left, right):
    return lax.dot_general(
        left, right, (((0,), (0,)), ((), ())), preferred_element_type=jnp.float32
    )


def dot_back(left, right):
    return lax.dot_general(
        left, right, (((1,), (1,)), ((), ())), preferred_element_type=jnp.float32
    )


def dot_plain(left, right):
    return lax.dot_general(
        left, right, (((1,), (0,)), ((), ())), preferred_element_type=jnp.float32
    )


def attend_kernel(block, q_ref, k_ref, v_ref, cos_ref, sin_ref, gain_ref, bias_ref, out_ref, log_ref):
    rows = q_ref.shape[0]
    tile = 2 * HD
    cosine, sine = cos_ref[...], sin_ref[...]
    first = lane_index((block, tile)) < HD

    def turned(raw, gain):
        unit_values, _ = head_unit(raw)
        scaled = unit_values * gain
        return cosine * scaled + sine * swap_halves(scaled)

    k_turned = turned(k_ref[...], gain_ref[1:2, :])
    v_values = v_ref[...]
    for which in range(2):
        lanes = slice(which * tile, (which + 1) * tile)
        query = (turned(q_ref[:, lanes], gain_ref[0:1, :]).astype(jnp.bfloat16)) * HD ** (-0.5)
        query = query.astype(jnp.bfloat16)
        keys = pair_of(k_turned, which)
        values = pair_of(v_values, which)
        for start in range(0, rows, block):
            stop = start + block
            bias = bias_ref[start:stop, :stop]
            result = jnp.zeros((block, tile), jnp.float32)
            logs = []
            for head in range(2):
                scores = dot_back(query[start:stop], keys[head][:stop]) + bias
                top = jnp.max(scores, axis=-1, keepdims=True)
                weights = jnp.exp(scores - top)
                totals = jnp.sum(weights, axis=-1, keepdims=True)
                low = (weights * (1.0 / totals)).astype(jnp.bfloat16)
                result += dot_plain(low, values[head][:stop])
                logs.append(top + jnp.log(totals))
            out_ref[start:stop, lanes] = result.astype(jnp.bfloat16)
            log_ref[start:stop, lanes] = jnp.where(first, logs[0], logs[1])


def attend_back_kernel(
    block,
    q_ref,
    k_ref,
    v_ref,
    cos_ref,
    sin_ref,
    gain_ref,
    bias_ref,
    log_ref,
    grad_ref,
    dq_ref,
    dk_ref,
    dv_ref,
    gain_grad_ref,
    key_sum,
    value_sum,
):
    rows = q_ref.shape[0]
    tile = 2 * HD
    cosine, sine = cos_ref[...], sin_ref[...]
    query_gain, key_gain = gain_ref[0:1, :], gain_ref[1:2, :]
    first = lane_index((rows, tile)) < HD
    scale = HD ** (-0.5)

    @pl.when(pl.program_id(0) == 0)
    def _():
        gain_grad_ref[...] = jnp.zeros_like(gain_grad_ref)

    def turned(scaled):
        return cosine * scaled + sine * swap_halves(scaled)

    def back(incoming, unit_values, inverse, gain, row):
        flat = cosine * incoming - sine * swap_halves(incoming)
        gain_grad_ref[row:row + 1, :] += jnp.sum(flat * unit_values, axis=0, keepdims=True)
        return head_norm_back(flat, unit_values, inverse, gain).astype(jnp.bfloat16)

    k_unit, k_inverse = head_unit(k_ref[...])
    k_turned = turned(k_unit * key_gain)
    v_values = v_ref[...]
    key_parts, value_parts = [], []
    for which in range(2):
        lanes = slice(which * tile, (which + 1) * tile)
        q_unit, q_inverse = head_unit(q_ref[:, lanes])
        query = (turned(q_unit * query_gain)).astype(jnp.bfloat16)
        query = (query * scale).astype(jnp.bfloat16)
        keys = pair_of(k_turned, which)
        values = pair_of(v_values, which)
        key_sum[...] = jnp.zeros_like(key_sum)
        value_sum[...] = jnp.zeros_like(value_sum)
        d_query = []
        for start in range(0, rows, block):
            stop = start + block
            bias = bias_ref[start:stop, :stop]
            grad = grad_ref[start:stop, lanes]
            part = jnp.zeros((block, tile), jnp.float32)
            for head in range(2):
                column = which * tile + head * HD
                logs = log_ref[start:stop, column:column + 1]
                scores = dot_back(query[start:stop], keys[head][:stop]) + bias
                probability = jnp.exp(scores - logs)
                grad_prob = dot_back(grad, values[head][:stop])
                terms = jnp.sum(probability * grad_prob, axis=-1, keepdims=True)
                grad_scores = (probability * (grad_prob - terms)).astype(jnp.bfloat16)
                part += dot_plain(grad_scores, keys[head][:stop])
                key_sum[head, :stop, :] += dot_rows(grad_scores, query[start:stop])
                value_sum[head, :stop, :] += dot_rows(probability.astype(jnp.bfloat16), grad)
            d_query.append(part * scale)
        dq_ref[:, lanes] = back(
            jnp.concatenate(d_query, axis=0), q_unit, q_inverse, query_gain, 0
        )
        for total, parts in ((key_sum, key_parts), (value_sum, value_parts)):
            joined = jnp.where(first, total[0], total[1])
            parts.append(joined + pltpu.roll(joined, HD, 1))
    d_key = jnp.where(first, key_parts[0], key_parts[1])
    dk_ref[...] = back(d_key, k_unit, k_inverse, key_gain, 1)
    dv_ref[...] = jnp.where(first, value_parts[0], value_parts[1]).astype(jnp.bfloat16)


def attention_specs(rows, first=0):
    tile = 2 * HD
    queries, keys = H // 2 + first, KV // 2
    fixed = lambda i: (0, 0)
    return [
        pl.BlockSpec((rows, 2 * tile), lambda i: (0, first + i)),
        pl.BlockSpec((rows, tile), lambda i: (0, queries + i)),
        pl.BlockSpec((rows, tile), lambda i: (0, queries + keys + i)),
        pl.BlockSpec((rows, tile), fixed),
        pl.BlockSpec((rows, tile), fixed),
        pl.BlockSpec((8, tile), fixed),
        pl.BlockSpec((rows, rows), fixed),
    ]


def attend(qkv, tables, first, count):
    rows = qkv.shape[0]
    wide = pl.BlockSpec((rows, 4 * HD), lambda i: (0, i))
    return pl.pallas_call(
        functools.partial(attend_kernel, rows // 2),
        grid=(count,),
        out_shape=[
            jax.ShapeDtypeStruct((rows, 4 * HD * count), jnp.bfloat16),
            jax.ShapeDtypeStruct((rows, 4 * HD * count), jnp.float32),
        ],
        in_specs=attention_specs(rows, first),
        out_specs=[wide, wide],
        compiler_params=pltpu.CompilerParams(vmem_limit_bytes=48 << 20),
        cost_estimate=pl.CostEstimate(
            flops=16 * count * rows * rows * 2 * HD,
            bytes_accessed=rows * 4096 * count,
            transcendentals=4 * count * rows * rows,
        ),
        name="attend",
    )(qkv, qkv, qkv, *tables)


def attend_back(qkv, tables, logs, grad, first, count):
    rows = qkv.shape[0]
    tile = 2 * HD
    wide = pl.BlockSpec((rows, 2 * tile), lambda i: (0, i))
    taken = pl.BlockSpec((rows, 2 * tile), lambda i: (0, first + i))
    narrow = pl.BlockSpec((rows, tile), lambda i: (0, i))
    return pl.pallas_call(
        functools.partial(attend_back_kernel, rows // 2),
        grid=(count,),
        out_shape=[
            jax.ShapeDtypeStruct((rows, 2 * tile * count), jnp.bfloat16),
            jax.ShapeDtypeStruct((rows, tile * count), jnp.bfloat16),
            jax.ShapeDtypeStruct((rows, tile * count), jnp.bfloat16),
            jax.ShapeDtypeStruct((8, tile), jnp.float32),
        ],
        in_specs=attention_specs(rows, first) + [wide, taken],
        out_specs=[wide, narrow, narrow, pl.BlockSpec((8, tile), lambda i: (0, 0))],
        scratch_shapes=[
            pltpu.VMEM((2, rows, tile), jnp.float32),
            pltpu.VMEM((2, rows, tile), jnp.float32),
        ],
        compiler_params=pltpu.CompilerParams(vmem_limit_bytes=48 << 20),
        cost_estimate=pl.CostEstimate(
            flops=40 * count * rows * rows * 2 * HD,
            bytes_accessed=rows * 5120 * count,
            transcendentals=4 * count * rows * rows,
        ),
        name="attend_back",
    )(qkv, qkv, qkv, *tables, logs, grad)


class Links:
    def __init__(self, groups, shards):
        self.groups = groups
        self.shards = shards
        self.depth = shards // 2
        rep = lax.axis_index("rep")
        shard = lax.axis_index("shard")
        self.rep = rep
        self.z = shard // 2
        self.core = shard % 2
        self.index = jnp.stack([rep, self.z, self.core]).astype(jnp.int32)

    def across_core(self, value):
        return lax.ppermute(value, "shard", [(s, s ^ 1) for s in range(self.shards)])

    def across_rep(self, value, bit):
        return lax.ppermute(value, "rep", [(r, r ^ bit) for r in range(self.groups)])

    def along_z(self, value):
        pairs = [(s, (s + 2) % self.shards) for s in range(self.shards)]
        return lax.ppermute(value, "shard", pairs)

    def fits(self, rows):
        return self.groups == 4 and self.shards % 2 == 0 and rows % 64 == 0

    def gather_of(self, shard, widths):
        kind = Gather if self.fits(shard.shape[0]) else PlainGather
        return kind(self, shard, widths)

    def sum_of(self, left, right, extra=None):
        kind = Sum if self.fits(left.shape[1] // self.shards) else PlainSum
        return kind(self, left, right, extra)


def add(*values):
    return functools.reduce(jnp.add, [value.astype(jnp.float32) for value in values])


def advance(moves, *others):
    states = [(move.held, move.flying) for move in moves]
    states, others = lax.optimization_barrier((states, others))
    for move, (held, flying) in zip(moves, states):
        move.held, move.flying = held, flying
        move.held, move.flying = next(move.work)
    return others[0] if len(others) == 1 else others


class Moves:
    held = ()
    flying = ()

    def still(self):
        while True:
            yield (), ()

    def finish(self):
        for self.held, self.flying in self.work:
            pass


class PlainGather(Moves):
    def __init__(self, links, shard, widths):
        self.shard, self.widths = shard, widths
        self.work = self.still()

    def result(self):
        whole = lax.all_gather(self.shard, "shard", axis=0, tiled=True)
        cuts = [sum(self.widths[:i]) for i in range(1, len(self.widths))]
        return jnp.split(whole, cuts, axis=1)


class PlainSum(Moves):
    def __init__(self, links, left, right, extra):
        low = rows_product(left, right).astype(jnp.bfloat16)
        self.low = low if extra is None else jnp.concatenate([low, extra], axis=1)
        self.work = self.still()

    def result(self):
        owned = lax.psum_scatter(self.low, "shard", scatter_dimension=0, tiled=True)
        return lax.psum(owned, "rep").astype(jnp.float32)


class Gather(Moves):
    def __init__(self, links, shard, widths):
        self.links, self.shard, self.widths = links, shard, widths
        rows, self.columns = shard.shape
        self.part = rows // links.groups
        self.middle = self.columns // 256 * 128
        self.held = (lax.dynamic_slice_in_dim(shard, links.rep * self.part, self.part, axis=0),)
        self.work = self.stages()

    def stages(self):
        links, middle = self.links, self.middle
        moving, pieces = self.held[0], ()
        for _ in range(links.depth - 1):
            yield pieces, (links.along_z(moving),)
            moving = self.flying[0]
            pieces = self.held + (moving,)
        mine = jnp.concatenate(pieces, axis=0)
        yield (mine,), (
            links.across_rep(mine, 1),
            links.across_rep(mine, 2),
            links.across_core(self.shard),
        )
        (mine,), (from_x, from_y, other) = self.held, self.flying
        yield (mine, from_x, from_y, other), (
            links.across_rep(from_x[:, :middle], 2),
            links.across_rep(from_y[:, middle:], 1),
            links.across_core(mine),
            links.across_core(from_x),
            links.across_core(from_y),
        )
        yield self.held + self.flying, (
            links.across_core(self.flying[0]),
            links.across_core(self.flying[1]),
        )

    def result(self):
        self.finish()
        mine, from_x, from_y, other, left, right, *core = self.held
        here = (self.shard, mine, from_x, from_y, left, right)
        there = (other, *core, *self.flying)
        links = self.links
        return assemble(
            links.index, here, there, links.depth, self.part, self.middle, self.widths
        )


class Sum(Moves):
    def __init__(self, links, left, right, extra):
        self.links = links
        self.rows = left.shape[1] // links.shards
        self.part = self.rows // links.groups
        self.held = product(links.index, left, right, extra, links.depth)
        self.columns = self.held[0].shape[1]
        self.middle = self.columns // 256 * 128
        self.work = self.stages()

    def result(self):
        self.finish()
        return place(self.links.index, self.flying + self.held, self.part, self.middle)

    def stages(self):
        links, middle, part = self.links, self.middle, self.part
        depth, rep = links.depth, links.rep
        yield (self.held[1],), (links.across_core(self.held[0]),)
        self.held = self.held + self.flying

        def block(offset, first):
            cuts = []
            for value in self.held[:2]:
                cut = value.reshape(depth, links.groups, part, self.columns)
                cut = lax.dynamic_index_in_dim(cut, rep ^ offset, axis=1, keepdims=False)
                cuts.append(cut[..., :middle] if first else cut[..., middle:])
            return add(*cuts)

        def two(near, far):
            return jnp.stack([near, far]).astype(jnp.bfloat16)

        yield self.held, (
            links.across_rep(two(block(1, True), block(3, True)), 1),
            links.across_rep(two(block(2, False), block(3, False)), 2),
        )
        one = self.flying
        yield (
            add(block(0, True), one[0][0]).astype(jnp.bfloat16),
            add(block(0, False), one[1][0]).astype(jnp.bfloat16),
        ), (
            links.across_rep(add(block(2, True), one[0][1]).astype(jnp.bfloat16), 2),
            links.across_rep(add(block(1, False), one[1][1]).astype(jnp.bfloat16), 1),
        )
        self.held = self.held + self.flying

        def at(step):
            index = (links.z + 2 * depth - 1 - step) % depth
            cut = [
                lax.dynamic_index_in_dim(value, index, axis=0, keepdims=False)
                for value in self.held
            ]
            return jnp.concatenate([add(cut[0], cut[2]), add(cut[1], cut[3])], axis=1)

        moving = at(0).astype(jnp.bfloat16)
        for step in range(1, depth):
            yield self.held, (links.along_z(moving),)
            moving = add(self.flying[0], at(step)).astype(jnp.bfloat16)
        yield (moving,), (links.across_rep(moving, 1), links.across_rep(moving, 2))
        from_x, from_y = self.flying
        yield self.held + (from_x, from_y), (
            links.across_rep(from_x[:, :middle], 2),
            links.across_rep(from_y[:, middle:], 1),
        )


def product_kernel(chunk, index_ref, left_ref, right_ref, *refs):
    extra_ref = refs[0] if len(refs) == 3 else None
    send_ref, keep_ref = refs[-2:]
    rows = send_ref.shape[0]
    core = index_ref[2]

    def put(lanes, whole):
        low, high = whole[:rows], whole[rows:]
        send_ref[:, lanes] = jnp.where(core == 0, high, low).astype(jnp.bfloat16)
        keep_ref[:, lanes] = jnp.where(core == 0, low, high).astype(jnp.bfloat16)

    left = left_ref[...]
    columns = right_ref.shape[1]
    for start in range(0, columns, chunk):
        lanes = slice(start, start + chunk)
        put(lanes, dot_rows(left, right_ref[:, lanes]))
    if extra_ref is not None:
        put(slice(columns, None), extra_ref[...])


def product(index, left, right, extra, depth):
    tokens, rows = left.shape[0], left.shape[1] // depth
    columns = right.shape[1]
    inputs = [left, right]
    specs = [
        pl.BlockSpec(memory_space=pltpu.SMEM),
        pl.BlockSpec((tokens, rows), lambda i: (0, i)),
        pl.BlockSpec((tokens, columns), lambda i: (0, 0)),
    ]
    wide = columns
    if extra is not None:
        inputs.append(extra)
        specs.append(pl.BlockSpec((rows, extra.shape[1]), lambda i: (i, 0)))
        wide += extra.shape[1]
    half = pl.BlockSpec((rows // 2, wide), lambda i: (i, 0))
    shape = jax.ShapeDtypeStruct((depth * rows // 2, wide), jnp.bfloat16)
    return tuple(
        pl.pallas_call(
            functools.partial(product_kernel, 512),
            grid=(depth,),
            out_shape=[shape, shape],
            in_specs=specs,
            out_specs=[half, half],
            compiler_params=pltpu.CompilerParams(vmem_limit_bytes=48 << 20),
            cost_estimate=pl.CostEstimate(
                flops=2 * tokens * depth * rows * columns,
                bytes_accessed=2 * (tokens * (depth * rows + columns) + depth * rows * wide),
                transcendentals=0,
            ),
            name="product",
        )(index, *inputs)
    )


def place_kernel(part, middle, index_ref, left, right, mine, from_x, from_y, out_ref):
    rep = index_ref[0]

    def put(offset, lanes, value):
        start = pl.multiple_of((rep ^ offset) * part, 16)
        out_ref[pl.ds(start, part), lanes] = value[...].astype(jnp.float32)

    put(0, slice(None), mine)
    put(1, slice(None), from_x)
    put(2, slice(None), from_y)
    put(3, slice(0, middle), left)
    put(3, slice(middle, None), right)


def place(index, values, part, middle):
    columns = values[2].shape[1]
    whole = pl.BlockSpec(memory_space=pltpu.VMEM)
    return pl.pallas_call(
        functools.partial(place_kernel, part, middle),
        out_shape=jax.ShapeDtypeStruct((4 * part, columns), jnp.float32),
        in_specs=[pl.BlockSpec(memory_space=pltpu.SMEM)] + [whole] * 5,
        out_specs=whole,
        compiler_params=pltpu.CompilerParams(vmem_limit_bytes=32 << 20),
        cost_estimate=pl.CostEstimate(
            flops=0, bytes_accessed=24 * part * columns, transcendentals=0
        ),
        name="place",
    )(index, *values)


def assemble_kernel(depth, part, middle, widths, index_ref, *refs):
    sources = refs[:12]
    count = len(widths)
    outputs = refs[12:12 + count]
    held = refs[12 + count:12 + 2 * count]
    arrived, left_here = refs[12 + 2 * count:]
    rows = part * 4
    columns = sum(widths)
    rep, z, core = index_ref[0], index_ref[1], index_ref[2]
    blocks = []
    for step in range(depth):
        for side in range(2):
            own, mine, from_x, from_y, left, right = sources[6 * side:6 * side + 6]
            which = core if side == 0 else 1 - core
            base = pl.multiple_of((lax.rem(z + depth - step, depth) * 2 + which) * rows, rows)
            if step == 0:
                blocks.append((base, [(own, 0, rows, 0, 0, columns)]))
                continue
            start = (step - 1) * part
            moves = [
                (mine, start, part, rep * part, 0, columns),
                (from_x, start, part, (rep ^ 1) * part, 0, columns),
                (from_y, start, part, (rep ^ 2) * part, 0, columns),
                (left, start, part, (rep ^ 3) * part, 0, middle),
                (right, start, part, (rep ^ 3) * part, middle, columns),
            ]
            blocks.append((base, moves))
    used = 0
    plan = []
    for base, moves in blocks:
        copies = []
        for source, start, height, offset, first, last in moves:
            edge = 0
            for buffer, width in zip(held, widths):
                low, high = max(first, edge), min(last, edge + width)
                if low < high:
                    copies.append(
                        pltpu.make_async_copy(
                            source.at[pl.ds(start, height), pl.ds(low - first, high - low)],
                            buffer.at[
                                pl.ds(pl.multiple_of(base + offset, 16), height),
                                pl.ds(low - edge, high - low),
                            ],
                            arrived.at[used],
                        )
                    )
                    used += 1
                edge += width
        plan.append((base, copies))
    for _, copies in plan:
        for copy in copies:
            copy.start()
    stores = []
    for base, copies in plan:
        for copy in copies:
            copy.wait()
        for buffer, output in zip(held, outputs):
            place = pl.ds(base, rows)
            stores.append(
                pltpu.make_async_copy(
                    buffer.at[place, :], output.at[place, :], left_here.at[len(stores)]
                )
            )
            stores[-1].start()
    for store in stores:
        store.wait()


def assemble(index, here, there, depth, part, middle, widths):
    rows = here[0].shape[0] * 2 * depth
    total = sum(widths) * rows
    count = 2 * (1 + 5 * (depth - 1)) * len(widths)
    return pl.pallas_call(
        functools.partial(assemble_kernel, depth, part, middle, widths),
        out_shape=[jax.ShapeDtypeStruct((rows, width), jnp.bfloat16) for width in widths],
        in_specs=[pl.BlockSpec(memory_space=pltpu.SMEM)] + [pl.BlockSpec(memory_space=pl.ANY)] * 12,
        out_specs=[pl.BlockSpec(memory_space=pl.ANY)] * len(widths),
        scratch_shapes=[pltpu.VMEM((rows, width), jnp.bfloat16) for width in widths]
        + [
            pltpu.SemaphoreType.DMA((count,)),
            pltpu.SemaphoreType.DMA((2 * depth * len(widths),)),
        ],
        compiler_params=pltpu.CompilerParams(vmem_limit_bytes=2 * total + (8 << 20)),
        cost_estimate=pl.CostEstimate(flops=0, bytes_accessed=4 * total, transcendentals=0),
        name="assemble",
    )(index, *here, *there)


def body(
    groups,
    shards,
    tokens,
    lengths,
    group_live,
    w_query,
    w_key,
    w_value,
    w_out,
    w_gate,
    w_up,
    w_down,
    g_attn,
    g_query,
    g_key,
    g_ffn,
    cotangent,
):
    links = Links(groups, shards)
    shard_rows = w_query.shape[0]
    width = HD * (H + 2 * KV)

    def column(values):
        return jnp.pad(values, (0, shard_rows - values.shape[0]))[:, None]

    gains = jnp.concatenate([column(g) for g in (g_attn, g_ffn, g_query, g_key)], axis=1)
    gains = jnp.pad(gains, ((0, 0), (0, 124)))
    packed = jnp.concatenate([w_query, w_key, w_value, w_out, gains], axis=1)
    first_move = links.gather_of(packed, (width, w_out.shape[1], 128))
    gate_move = links.gather_of(w_gate, (w_gate.shape[1],))
    up_move = links.gather_of(w_up, (w_up.shape[1],))
    down_move = links.gather_of(w_down, (w_down.shape[1],))
    for _ in range(3):
        advance([first_move])
    for _ in range(3):
        advance([first_move, gate_move])
    full_qkv, full_out, full_gains = first_move.result()
    head_rows = g_query.shape[0]
    all_gains = full_gains[:, :4].astype(jnp.float32)
    gain_attn = all_gains[:, 0]
    gain_ffn = all_gains[:, 1]
    gain_query = all_gains[:, 2].reshape(shards, shard_rows)[:, :head_rows].reshape(HD)
    gain_key = all_gains[:, 3].reshape(shards, shard_rows)[:, :head_rows].reshape(HD)

    row_count = tokens.shape[0]
    x_float = tokens.astype(jnp.float32)
    row_index, segment, position, keep_mask = layout(lengths[0], group_live[0], row_count)
    allowed = (segment[:, None] == segment[None, :]) & (row_index[None, :] <= row_index[:, None])
    bias = jnp.where(allowed, 0.0, masked_score).astype(jnp.float32)
    gain_rows = jnp.stack([jnp.tile(gain_query, 2), jnp.tile(gain_key, 2)])
    tables = (*rotary_tables(position), jnp.pad(gain_rows, ((0, 6), (0, 0))), bias)
    unit_one, inverse_one = normalize(x_float)
    attn_input = (unit_one * gain_attn).astype(jnp.bfloat16)
    qkv = jnp.dot(attn_input, full_qkv, preferred_element_type=jnp.float32)
    qkv = advance([gate_move, up_move], qkv)
    parts, logs = [], []
    for first in range(KV // 2):
        part, log = attend(qkv, tables, first, 1)
        if first == 1:
            qkv, part = advance([up_move], qkv, part)
        parts.append(part)
        logs.append(log)
    attended = jnp.concatenate(parts, axis=1)
    attended = advance([gate_move, up_move], attended)
    hidden = x_float + keep_mask[:, None] * jnp.dot(
        attended, full_out, preferred_element_type=jnp.float32
    )
    unit_two, inverse_two = normalize(hidden)
    ffn_input = (unit_two * gain_ffn).astype(jnp.bfloat16)
    ffn_input = advance([gate_move, up_move, down_move], ffn_input)
    (full_gate,) = gate_move.result()
    gate_proj = jnp.dot(ffn_input, full_gate, preferred_element_type=jnp.float32)
    gate_proj = advance([up_move, down_move], gate_proj)
    gate_proj = advance([up_move, down_move], gate_proj)
    (full_up,) = up_move.result()
    up_proj = jnp.dot(ffn_input, full_up, preferred_element_type=jnp.float32)
    inner_low = (jax.nn.silu(gate_proj) * up_proj).astype(jnp.bfloat16)
    inner_low = advance([down_move], inner_low)

    d_final = cotangent.astype(jnp.float32)
    d_ffn = (keep_mask[:, None] * d_final).astype(jnp.bfloat16)
    down_sum = links.sum_of(inner_low, d_ffn)
    d_ffn = advance([down_move, down_sum], d_ffn)
    d_ffn = advance([down_move], d_ffn)
    (full_down,) = down_move.result()
    d_inner = back_product(d_ffn, full_down)
    sigmoid_gate = jax.nn.sigmoid(gate_proj)
    d_gate = (d_inner * up_proj * sigmoid_gate * (1.0 + gate_proj * (1.0 - sigmoid_gate))).astype(
        jnp.bfloat16
    )
    d_up = (d_inner * gate_proj * sigmoid_gate).astype(jnp.bfloat16)
    d_gate, d_up = advance([down_sum], d_gate, d_up)
    gate_sum = links.sum_of(ffn_input, d_gate)
    d_up = advance([gate_sum], d_up)
    up_sum = links.sum_of(ffn_input, d_up)
    d_gate, d_up = advance([up_sum], d_gate, d_up)
    d_ffn_input = back_product(d_gate, full_gate)
    d_up, d_ffn_input = advance([down_sum, gate_sum], d_up, d_ffn_input)
    d_ffn_input = d_ffn_input + back_product(d_up, full_up)
    d_ffn_input = advance([down_sum], d_ffn_input)
    d_hidden_norm, grad_gain_ffn = norm_back(d_ffn_input, unit_two, inverse_two, gain_ffn)
    d_hidden = d_final + d_hidden_norm
    d_attn = (keep_mask[:, None] * d_hidden).astype(jnp.bfloat16)
    out_sum = links.sum_of(attended, d_attn)
    d_attn = advance([out_sum], d_attn)
    d_attended = back_product(d_attn, full_out).astype(jnp.bfloat16)
    d_attended, qkv = advance([down_sum, gate_sum, up_sum], d_attended, qkv)
    pieces = []
    plans = ([down_sum, out_sum], [down_sum, gate_sum, up_sum], [down_sum, gate_sum, out_sum])
    for first in range(KV // 2):
        piece = attend_back(qkv, tables, logs[first], d_attended, first, 1)
        if first < len(plans):
            d_attended, qkv, *piece = advance(plans[first], d_attended, qkv, *piece)
        pieces.append(piece)
    gain_sums = sum(piece[3] for piece in pieces)
    d_qkv = jnp.concatenate([piece[i] for i in range(3) for piece in pieces], axis=1)
    d_qkv = advance([gate_sum, up_sum, out_sum], d_qkv)
    grad_gain_query = gain_sums[0, :HD] + gain_sums[0, HD:]
    grad_gain_key = gain_sums[1, :HD] + gain_sums[1, HD:]
    d_attn_input = back_product(d_qkv, full_qkv)
    d_x_norm, grad_gain_attn = norm_back(d_attn_input, unit_one, inverse_one, gain_attn)
    grad_tokens = (d_hidden + d_x_norm).astype(jnp.bfloat16)

    def spread(values):
        blocks = jnp.pad(
            values.reshape(shards, head_rows), ((0, 0), (0, shard_rows - head_rows))
        )
        return blocks.reshape(shards * shard_rows)

    gain_grads = jnp.stack(
        [grad_gain_attn, grad_gain_ffn, spread(grad_gain_query), spread(grad_gain_key)], axis=1
    )
    gain_grads = jnp.pad(gain_grads, ((0, 0), (0, 124))).astype(jnp.bfloat16)
    qkv_sum = links.sum_of(attn_input, d_qkv, gain_grads)
    inner_low = advance([qkv_sum, gate_sum, up_sum, out_sum], inner_low)
    block_out = (
        hidden
        + keep_mask[:, None] * jnp.dot(inner_low, full_down, preferred_element_type=jnp.float32)
    ).astype(jnp.bfloat16)
    advance([qkv_sum, gate_sum, up_sum, out_sum])
    block_out = advance([qkv_sum, up_sum, out_sum], block_out)
    advance([qkv_sum, up_sum, out_sum])
    for _ in range(4):
        advance([qkv_sum])
    owned = qkv_sum.result()
    grad_down, grad_gate = down_sum.result(), gate_sum.result()
    grad_up, grad_out = up_sum.result(), out_sum.result()
    return (
        block_out,
        grad_tokens,
        owned[:, : H * HD],
        owned[:, H * HD : (H + KV) * HD],
        owned[:, (H + KV) * HD : width],
        grad_out,
        grad_gate,
        grad_up,
        grad_down,
        owned[:, width],
        owned[:head_rows, width + 2],
        owned[:head_rows, width + 3],
        owned[:, width + 1],
    )


def solution(mesh):
    in_specs = (
        P(("rep", "shard"), None),
        P(("rep", "shard"), None),
        P("rep"),
        P("shard", None),
        P("shard", None),
        P("shard", None),
        P("shard", None),
        P("shard", None),
        P("shard", None),
        P("shard", None),
        P("shard"),
        P("shard"),
        P("shard"),
        P("shard"),
        P(("rep", "shard"), None),
    )
    out_specs = (
        P(("rep", "shard"), None),
        P(("rep", "shard"), None),
        P("shard", None),
        P("shard", None),
        P("shard", None),
        P("shard", None),
        P("shard", None),
        P("shard", None),
        P("shard", None),
        P("shard"),
        P("shard"),
        P("shard"),
        P("shard"),
    )
    return jax.shard_map(
        functools.partial(body, mesh.shape["rep"], mesh.shape["shard"]),
        mesh=mesh,
        in_specs=in_specs,
        out_specs=out_specs,
        check_vma=False,
    )
```

```python
import functools

import jax
import jax.numpy as jnp
from jax import lax
from jax.experimental import pallas as pl
from jax.experimental.pallas import tpu as pltpu
from jax.sharding import PartitionSpec as P

H = 16
KV = 8
HD = 64


epsilon = 1e-05
theta_base = 1000000.0
masked_score = -1e30


def layout(seq_lengths, live_rows, row_count):
    row_index = jnp.arange(row_count, dtype=jnp.int32)
    seq_ends = jnp.cumsum(seq_lengths)
    passed_ends = row_index[:, None] >= seq_ends[None, :]
    segment = jnp.sum(passed_ends.astype(jnp.int32), axis=1, dtype=jnp.int32)
    begins = jnp.sum(jnp.where(passed_ends, seq_lengths[None, :], 0), axis=1, dtype=jnp.int32)
    live_mask = row_index < live_rows
    segment = jnp.where(live_mask, segment, -1)
    position = (row_index - begins).astype(jnp.float32)
    return (row_index, segment, position, live_mask.astype(jnp.float32))


def rotary_tables(position):
    half_width = HD // 2
    frequency = theta_base ** (-2.0 * jnp.arange(half_width, dtype=jnp.float32) / HD)
    angles = position[:, None] * frequency[None, :]
    cosine, sine = jnp.cos(angles), jnp.sin(angles)
    return (
        jnp.concatenate([cosine] * 4, axis=1),
        jnp.concatenate([-sine, sine, -sine, sine], axis=1),
    )


def normalize(values):
    inverse_rms = lax.rsqrt(jnp.mean(values * values, axis=-1, keepdims=True) + epsilon)
    return (values * inverse_rms, inverse_rms)


def norm_back(incoming, unit_values, inverse_rms, gain):
    grad_unit = incoming * gain
    grad_values = inverse_rms * (
        grad_unit - unit_values * jnp.mean(unit_values * grad_unit, axis=-1, keepdims=True)
    )
    grad_gain = jnp.sum((incoming * unit_values).reshape(-1, unit_values.shape[-1]), axis=0)
    return (grad_values, grad_gain)


def rows_product(left, right):
    return lax.dot_general(
        left, right, (((0,), (0,)), ((), ())), preferred_element_type=jnp.float32
    )


def back_product(left, right):
    return lax.dot_general(
        left, right, (((1,), (1,)), ((), ())), preferred_element_type=jnp.float32
    )


def lane_index(shape):
    return lax.broadcasted_iota(jnp.int32, shape, len(shape) - 1)


def head_mean(values):
    first = lane_index(values.shape) < HD
    low = jnp.sum(jnp.where(first, values, 0.0), axis=-1, keepdims=True)
    high = jnp.sum(jnp.where(first, 0.0, values), axis=-1, keepdims=True)
    return jnp.where(first, low, high) * (1.0 / HD)


def swap_halves(values):
    front = lane_index(values.shape) % HD < HD // 2
    return jnp.where(
        front, pltpu.roll(values, 2 * HD - HD // 2, 1), pltpu.roll(values, HD // 2, 1)
    )


def head_unit(raw):
    inverse = lax.rsqrt(head_mean(raw * raw) + epsilon)
    return raw * inverse, inverse


def head_norm_back(incoming, unit_values, inverse, gain):
    grad_unit = incoming * gain
    return inverse * (grad_unit - unit_values * head_mean(unit_values * grad_unit))


def pair_of(values, which):
    first = lane_index(values.shape) < HD
    kept = jnp.where(first, values, 0.0) if which == 0 else jnp.where(first, 0.0, values)
    moved = pltpu.roll(kept, HD, 1)
    pair = (kept, moved) if which == 0 else (moved, kept)
    return tuple(value.astype(jnp.bfloat16) for value in pair)


def dot_rows(left, right):
    return lax.dot_general(
        left, right, (((0,), (0,)), ((), ())), preferred_element_type=jnp.float32
    )


def dot_back(left, right):
    return lax.dot_general(
        left, right, (((1,), (1,)), ((), ())), preferred_element_type=jnp.float32
    )


def dot_plain(left, right):
    return lax.dot_general(
        left, right, (((1,), (0,)), ((), ())), preferred_element_type=jnp.float32
    )


def attend_kernel(block, q_ref, k_ref, v_ref, cos_ref, sin_ref, gain_ref, bias_ref, out_ref, log_ref):
    rows = q_ref.shape[0]
    tile = 2 * HD
    cosine, sine = cos_ref[...], sin_ref[...]
    first = lane_index((block, tile)) < HD

    def turned(raw, gain):
        unit_values, _ = head_unit(raw)
        scaled = unit_values * gain
        return cosine * scaled + sine * swap_halves(scaled)

    k_turned = turned(k_ref[...], gain_ref[1:2, :])
    v_values = v_ref[...]
    for which in range(2):
        lanes = slice(which * tile, (which + 1) * tile)
        query = (turned(q_ref[:, lanes], gain_ref[0:1, :]).astype(jnp.bfloat16)) * HD ** (-0.5)
        query = query.astype(jnp.bfloat16)
        keys = pair_of(k_turned, which)
        values = pair_of(v_values, which)
        for start in range(0, rows, block):
            stop = start + block
            bias = bias_ref[start:stop, :stop]
            result = jnp.zeros((block, tile), jnp.float32)
            logs = []
            for head in range(2):
                scores = dot_back(query[start:stop], keys[head][:stop]) + bias
                top = jnp.max(scores, axis=-1, keepdims=True)
                weights = jnp.exp(scores - top)
                totals = jnp.sum(weights, axis=-1, keepdims=True)
                low = (weights * (1.0 / totals)).astype(jnp.bfloat16)
                result += dot_plain(low, values[head][:stop])
                logs.append(top + jnp.log(totals))
            out_ref[start:stop, lanes] = result.astype(jnp.bfloat16)
            log_ref[start:stop, lanes] = jnp.where(first, logs[0], logs[1])


def attend_back_kernel(
    block,
    q_ref,
    k_ref,
    v_ref,
    cos_ref,
    sin_ref,
    gain_ref,
    bias_ref,
    log_ref,
    grad_ref,
    *refs,
):
    rows = q_ref.shape[0]
    tile = 2 * HD
    cosine, sine = cos_ref[...], sin_ref[...]
    dq_ref, dk_ref, dv_ref, gain_grad_ref, key_sum, value_sum = refs[-6:]
    query_gain, key_gain = gain_ref[0:1, :], gain_ref[1:2, :]
    first = lane_index((rows, tile)) < HD
    scale = HD ** (-0.5)

    @pl.when(pl.program_id(0) == 0)
    def _():
        gain_grad_ref[...] = jnp.zeros_like(gain_grad_ref)

    def turned(scaled):
        return cosine * scaled + sine * swap_halves(scaled)

    def back(incoming, unit_values, inverse, gain, row):
        flat = cosine * incoming - sine * swap_halves(incoming)
        gain_grad_ref[row:row + 1, :] += jnp.sum(flat * unit_values, axis=0, keepdims=True)
        return head_norm_back(flat, unit_values, inverse, gain).astype(jnp.bfloat16)

    k_unit, k_inverse = head_unit(k_ref[...])
    k_turned = turned(k_unit * key_gain)
    v_values = v_ref[...]
    key_parts, value_parts = [], []
    for which in range(2):
        lanes = slice(which * tile, (which + 1) * tile)
        q_unit, q_inverse = head_unit(q_ref[:, lanes])
        query = (turned(q_unit * query_gain)).astype(jnp.bfloat16)
        query = (query * scale).astype(jnp.bfloat16)
        keys = pair_of(k_turned, which)
        values = pair_of(v_values, which)
        key_sum[...] = jnp.zeros_like(key_sum)
        value_sum[...] = jnp.zeros_like(value_sum)
        d_query = []
        for start in range(0, rows, block):
            stop = start + block
            bias = bias_ref[start:stop, :stop]
            grad = grad_ref[start:stop, lanes]
            part = jnp.zeros((block, tile), jnp.float32)
            for head in range(2):
                column = which * tile + head * HD
                logs = log_ref[start:stop, column:column + 1]
                scores = dot_back(query[start:stop], keys[head][:stop]) + bias
                probability = jnp.exp(scores - logs)
                grad_prob = dot_back(grad, values[head][:stop])
                terms = jnp.sum(probability * grad_prob, axis=-1, keepdims=True)
                grad_scores = (probability * (grad_prob - terms)).astype(jnp.bfloat16)
                part += dot_plain(grad_scores, keys[head][:stop])
                key_sum[head, :stop, :] += dot_rows(grad_scores, query[start:stop])
                value_sum[head, :stop, :] += dot_rows(probability.astype(jnp.bfloat16), grad)
            d_query.append(part * scale)
        dq_ref[:, lanes] = back(
            jnp.concatenate(d_query, axis=0), q_unit, q_inverse, query_gain, 0
        )
        for total, parts in ((key_sum, key_parts), (value_sum, value_parts)):
            joined = jnp.where(first, total[0], total[1])
            parts.append(joined + pltpu.roll(joined, HD, 1))
    d_key = jnp.where(first, key_parts[0], key_parts[1])
    dk_ref[...] = back(d_key, k_unit, k_inverse, key_gain, 1)
    dv_ref[...] = jnp.where(first, value_parts[0], value_parts[1]).astype(jnp.bfloat16)


def attention_specs(rows, first=0):
    tile = 2 * HD
    fixed = lambda i: (0, 0)
    return [
        pl.BlockSpec((rows, 2 * tile), lambda i: (0, first + i)),
        pl.BlockSpec((rows, tile), lambda i: (0, H // 2 + first + i)),
        pl.BlockSpec((rows, tile), lambda i: (0, H // 2 + KV // 2 + first + i)),
        pl.BlockSpec((rows, tile), fixed),
        pl.BlockSpec((rows, tile), fixed),
        pl.BlockSpec((8, tile), fixed),
        pl.BlockSpec((rows, rows), fixed),
    ]


def attend(qkv, tables, first, count):
    rows = qkv.shape[0]
    wide = pl.BlockSpec((rows, 4 * HD), lambda i: (0, i))
    return pl.pallas_call(
        functools.partial(attend_kernel, rows // 2),
        grid=(count,),
        out_shape=[
            jax.ShapeDtypeStruct((rows, 4 * HD * count), jnp.bfloat16),
            jax.ShapeDtypeStruct((rows, 4 * HD * count), jnp.float32),
        ],
        in_specs=attention_specs(rows, first),
        out_specs=[wide, wide],
        compiler_params=pltpu.CompilerParams(vmem_limit_bytes=48 << 20),
        cost_estimate=pl.CostEstimate(flops=0, bytes_accessed=0, transcendentals=0),
        name="attend",
    )(qkv, qkv, qkv, *tables)


def attend_back(qkv, tables, logs, grad, first, count, before=()):
    rows = qkv.shape[0]
    tile = 2 * HD
    wide = pl.BlockSpec((rows, 2 * tile), lambda i: (0, i))
    taken = pl.BlockSpec((rows, 2 * tile), lambda i: (0, first + i))
    narrow = pl.BlockSpec((rows, tile), lambda i: (0, first + i))
    specs = attention_specs(rows, first) + [wide, taken]
    return pl.pallas_call(
        functools.partial(attend_back_kernel, rows // 2),
        grid=(count,),
        out_shape=[
            jax.ShapeDtypeStruct((rows, H * HD), jnp.bfloat16),
            jax.ShapeDtypeStruct((rows, KV * HD), jnp.bfloat16),
            jax.ShapeDtypeStruct((rows, KV * HD), jnp.bfloat16),
            jax.ShapeDtypeStruct((8, tile), jnp.float32),
        ],
        in_specs=specs + [pl.BlockSpec(memory_space=pl.ANY)] * len(before),
        input_output_aliases={len(specs) + i: i for i in range(len(before))},
        out_specs=[taken, narrow, narrow, pl.BlockSpec((8, tile), lambda i: (0, 0))],
        scratch_shapes=[
            pltpu.VMEM((2, rows, tile), jnp.float32),
            pltpu.VMEM((2, rows, tile), jnp.float32),
        ],
        compiler_params=pltpu.CompilerParams(vmem_limit_bytes=48 << 20),
        cost_estimate=pl.CostEstimate(flops=0, bytes_accessed=0, transcendentals=0),
        name="attend_back",
    )(qkv, qkv, qkv, *tables, logs, grad, *before)


def inner_back_kernel(d_ref, down_ref, gate_ref, up_ref, d_gate_ref, d_up_ref):
    d_inner = dot_back(d_ref[...], down_ref[...])
    gate = gate_ref[...]
    sigmoid = jax.nn.sigmoid(gate)
    d_gate = d_inner * up_ref[...] * sigmoid * (1.0 + gate * (1.0 - sigmoid))
    d_gate_ref[...] = d_gate.astype(jnp.bfloat16)
    d_up_ref[...] = (d_inner * gate * sigmoid).astype(jnp.bfloat16)


def inner_back(d_ffn, full_down, gate_proj, up_proj):
    (rows, width), units = d_ffn.shape, full_down.shape[0]
    tile = 512
    columns = pl.BlockSpec((rows, tile), lambda i: (0, i))
    shape = jax.ShapeDtypeStruct((rows, units), jnp.bfloat16)
    return pl.pallas_call(
        inner_back_kernel,
        grid=(units // tile,),
        out_shape=[shape, shape],
        in_specs=[
            pl.BlockSpec((rows, width), lambda i: (0, 0)),
            pl.BlockSpec((tile, width), lambda i: (i, 0)),
            columns,
            columns,
        ],
        out_specs=[columns, columns],
        compiler_params=pltpu.CompilerParams(vmem_limit_bytes=48 << 20),
        cost_estimate=pl.CostEstimate(flops=0, bytes_accessed=0, transcendentals=0),
        name="inner_back",
    )(d_ffn, full_down, gate_proj, up_proj)


def ffn_out_kernel(inner_ref, down_ref, hidden_ref, keep_ref, out_ref, total):
    step = pl.program_id(0)
    part = dot_plain(inner_ref[...], down_ref[...])

    @pl.when(step == 0)
    def _():
        total[...] = part

    @pl.when(step > 0)
    def _():
        total[...] += part

    @pl.when(step == pl.num_programs(0) - 1)
    def _():
        out_ref[...] = (hidden_ref[...] + keep_ref[...] * total[...]).astype(jnp.bfloat16)


def ffn_out(inner_low, full_down, hidden, keep_column):
    (rows, units), width = inner_low.shape, full_down.shape[1]
    tile = 512
    fixed = lambda i: (0, 0)
    return pl.pallas_call(
        ffn_out_kernel,
        grid=(units // tile,),
        out_shape=jax.ShapeDtypeStruct((rows, width), jnp.bfloat16),
        in_specs=[
            pl.BlockSpec((rows, tile), lambda i: (0, i)),
            pl.BlockSpec((tile, width), lambda i: (i, 0)),
            pl.BlockSpec((rows, width), fixed),
            pl.BlockSpec((rows, 1), fixed),
        ],
        out_specs=pl.BlockSpec((rows, width), fixed),
        scratch_shapes=[pltpu.VMEM((rows, width), jnp.float32)],
        compiler_params=pltpu.CompilerParams(vmem_limit_bytes=48 << 20),
        cost_estimate=pl.CostEstimate(flops=0, bytes_accessed=0, transcendentals=0),
        name="ffn_out",
    )(inner_low, full_down, hidden, keep_column)


def ffn_back_kernel(d_gate_ref, d_up_ref, gate_ref, up_ref, out_ref):
    part = dot_back(d_gate_ref[...], gate_ref[...]) + dot_back(d_up_ref[...], up_ref[...])

    @pl.when(pl.program_id(0) == 0)
    def _():
        out_ref[...] = part

    @pl.when(pl.program_id(0) > 0)
    def _():
        out_ref[...] += part


def ffn_back(d_gate, d_up, full_gate, full_up):
    (rows, units), width = d_gate.shape, full_gate.shape[0]
    tile = 512
    left = pl.BlockSpec((rows, tile), lambda i: (0, i))
    right = pl.BlockSpec((width, tile), lambda i: (0, i))
    return pl.pallas_call(
        ffn_back_kernel,
        grid=(units // tile,),
        out_shape=jax.ShapeDtypeStruct((rows, width), jnp.float32),
        in_specs=[left, left, right, right],
        out_specs=pl.BlockSpec((rows, width), lambda i: (0, 0)),
        compiler_params=pltpu.CompilerParams(vmem_limit_bytes=48 << 20),
        cost_estimate=pl.CostEstimate(flops=0, bytes_accessed=0, transcendentals=0),
        name="ffn_back",
    )(d_gate, d_up, full_gate, full_up)


class Links:
    def __init__(self, groups, shards):
        self.groups = groups
        self.shards = shards
        self.depth = shards // 2
        rep = lax.axis_index("rep")
        shard = lax.axis_index("shard")
        self.rep = rep
        self.z = shard // 2
        self.core = shard % 2
        self.index = jnp.stack([rep, self.z, self.core]).astype(jnp.int32)

    def across_core(self, value):
        return lax.ppermute(value, "shard", [(s, s ^ 1) for s in range(self.shards)])

    def across_x(self, value):
        return lax.ppermute(value, "rep", [(r, r ^ 1) for r in range(self.groups)])

    def across_y(self, value):
        return lax.ppermute(value, "rep", [(r, r ^ 2) for r in range(self.groups)])

    def along_z(self, value):
        pairs = [(s, (s + 2) % self.shards) for s in range(self.shards)]
        return lax.ppermute(value, "shard", pairs)

    def fits(self, rows):
        return self.groups == 4 and self.shards % 2 == 0 and rows % 64 == 0

    def gather_of(self, shard, widths):
        kind = Gather if self.fits(shard.shape[0]) else PlainGather
        return kind(self, shard, widths)

    def sum_of(self, pairs, extra=None, depth_first=False):
        kind = Sum if self.fits(pairs[0][0].shape[1] // self.shards) else PlainSum
        return kind(self, pairs, extra, depth_first)


def add(*values):
    return functools.reduce(jnp.add, [value.astype(jnp.float32) for value in values])


def advance(moves, *others):
    states = [(move.held, move.flying) for move in moves]
    states, others = lax.optimization_barrier((states, others))
    sends = []
    for move, (held, flying) in zip(moves, states):
        move.held, move.flying = held, flying
        move.held, move.sends = next(move.work)
        sends.append([value for _, value in move.sends])
    sends, others = lax.optimization_barrier((sends, others))
    for move, values in zip(moves, sends):
        move.flying = tuple(link(value) for (link, _), value in zip(move.sends, values))
    return others[0] if len(others) == 1 else others


def settle(moves, *others):
    states = [(move.held, move.flying) for move in moves]
    states, others = lax.optimization_barrier((states, others))
    for move, (held, flying) in zip(moves, states):
        move.held, move.flying = held, flying
    return others[0] if len(others) == 1 else others


class Moves:
    held = ()
    flying = ()

    def still(self):
        while True:
            yield (), ()

    def finish(self):
        for self.held, sends in self.work:
            self.flying = tuple(link(value) for link, value in sends)


class PlainGather(Moves):
    def __init__(self, links, shard, widths):
        self.shard, self.widths = shard, widths
        self.work = self.still()

    def result(self):
        whole = lax.all_gather(self.shard, "shard", axis=0, tiled=True)
        cuts = [sum(self.widths[:i]) for i in range(1, len(self.widths))]
        return jnp.split(whole, cuts, axis=1)


class PlainSum(Moves):
    def __init__(self, links, pairs, extra, depth_first):
        parts = [rows_product(left, right).astype(jnp.bfloat16) for left, right in pairs]
        self.low = jnp.concatenate(parts + ([] if extra is None else [extra]), axis=1)
        self.work = self.still()

    def result(self):
        owned = lax.psum_scatter(self.low, "shard", scatter_dimension=0, tiled=True)
        return lax.psum(owned, "rep").astype(jnp.float32)


class Gather(Moves):
    def __init__(self, links, shard, widths):
        self.links, self.shard, self.widths = links, shard, widths
        rows, self.columns = shard.shape
        self.part = rows // links.groups
        self.middle = self.columns // 256 * 128
        self.held = (lax.dynamic_slice_in_dim(shard, links.rep * self.part, self.part, axis=0),)
        self.work = self.stages()

    def stages(self):
        links, middle = self.links, self.middle
        moving, pieces = self.held[0], ()
        for step in range(links.depth - 1):
            moves = ((links.along_z, moving),)
            if step == 0:
                moves += ((links.across_core, self.shard),)
            yield pieces, moves
            moving = self.flying[0]
            pieces = self.held + self.flying
        first, other, *rest = pieces
        mine = jnp.concatenate([first, *rest], axis=0)
        yield (mine, other), (
            (links.across_x, mine),
            (links.across_y, mine),
            (links.across_core, mine),
        )
        from_x, from_y, _ = self.flying
        yield self.held + self.flying, (
            (links.across_y, from_x[:, :middle]),
            (links.across_x, from_y[:, middle:]),
            (links.across_core, from_x),
            (links.across_core, from_y),
        )
        yield self.held + self.flying, (
            (links.across_core, self.flying[0]),
            (links.across_core, self.flying[1]),
        )

    def result(self):
        self.finish()
        mine, other, from_x, from_y, mine_core, left, right, x_core, y_core = self.held
        here = (self.shard, mine, from_x, from_y, left, right)
        there = (other, mine_core, x_core, y_core, *self.flying)
        links = self.links
        return assemble(
            links.index, here, there, links.depth, self.part, self.middle, self.widths
        )


class Sum(Moves):
    def __init__(self, links, pairs, extra, depth_first):
        self.links = links
        self.part = pairs[0][0].shape[1] // links.shards // links.groups
        self.held = product(links.index, pairs, extra, links.depth)
        self.work = self.stages(depth_first)

    def result(self):
        self.finish()
        return place(self.links.index, self.flying + self.held, self.part)

    def stages(self, depth_first):
        links, part = self.links, self.part
        yield (self.held[1],), ((links.across_core, self.held[0]),)
        pair = self.held + self.flying
        if depth_first:
            yield from self.along(pair, links.groups * part)
            yield from self.across((self.held[0], self.flying[0]), 1)
            own, left, right = self.held + self.flying
            mine = jnp.concatenate(
                [add(own[:, : left.shape[1]], left), add(own[:, left.shape[1] :], right)], axis=1
            )
        else:
            yield from self.across(pair, links.depth)
            yield from self.along(self.held + self.flying, part)
            mine = add(self.held[0], self.flying[0])
        mine = mine.astype(jnp.bfloat16)
        middle = mine.shape[1] // 2
        yield (mine,), ((links.across_x, mine), (links.across_y, mine))
        from_x, from_y = self.flying
        yield self.held + (from_x, from_y), (
            (links.across_y, from_x[:, :middle]),
            (links.across_x, from_y[:, middle:]),
        )

    def across(self, pair, depth):
        links, part = self.links, self.part
        left, right = sum_first(links.index, pair, part, depth)
        yield pair, ((links.across_x, left), (links.across_y, right))
        left, right, own = sum_second(links.index, self.held, self.flying, part, depth)
        yield (own,), ((links.across_y, left), (links.across_x, right))

    def along(self, values, rows):
        links = self.links
        moving, *terms = ring_terms(links.index, values, rows, links.depth)
        yield tuple(terms), ((links.along_z, moving),)
        for _ in range(links.depth - 2):
            moving = add(self.held[0], self.flying[0]).astype(jnp.bfloat16)
            yield self.held[1:], ((links.along_z, moving),)


def sum_first_kernel(index_ref, *refs):
    keep, received = refs[0:3], refs[3:6]
    left_ref, right_ref = refs[6:]

    def total(place):
        return keep[place][...].astype(jnp.float32) + received[place][...].astype(jnp.float32)

    both = total(2).astype(jnp.bfloat16)
    middle = left_ref.shape[2]
    left_ref[0] = total(0).astype(jnp.bfloat16)
    left_ref[1] = both[:, :middle]
    right_ref[0] = total(1).astype(jnp.bfloat16)
    right_ref[1] = both[:, middle:]


def sum_first(index, pair, part, depth):
    columns = pair[0].shape[1]
    middle = columns // 2
    specs = [
        pl.BlockSpec((part, middle), lambda i, index: (4 * i + (index[0] ^ 1), 0)),
        pl.BlockSpec((part, middle), lambda i, index: (4 * i + (index[0] ^ 2), 1)),
        pl.BlockSpec((part, columns), lambda i, index: (4 * i + (index[0] ^ 3), 0)),
    ]
    half = pl.BlockSpec((2, part, middle), lambda i, index: (0, i, 0))
    shape = jax.ShapeDtypeStruct((2, depth * part, middle), jnp.bfloat16)
    return pl.pallas_call(
        sum_first_kernel,
        grid_spec=pltpu.PrefetchScalarGridSpec(
            num_scalar_prefetch=1, grid=(depth,), in_specs=specs * 2, out_specs=[half, half]
        ),
        out_shape=[shape, shape],
        compiler_params=pltpu.CompilerParams(vmem_limit_bytes=48 << 20),
        cost_estimate=pl.CostEstimate(flops=0, bytes_accessed=0, transcendentals=0),
        name="sum_first",
    )(index, *([pair[0]] * 3 + [pair[1]] * 3))


def sum_second_kernel(index_ref, *refs):
    keep, received = refs[0:3], refs[3:6]
    from_left, from_right, left_ref, right_ref, own_ref = refs[6:]
    middle = left_ref.shape[1]

    def total(place):
        return keep[place][...].astype(jnp.float32) + received[place][...].astype(jnp.float32)

    left_ref[...] = (total(0) + from_left[1].astype(jnp.float32)).astype(jnp.bfloat16)
    right_ref[...] = (total(1) + from_right[1].astype(jnp.float32)).astype(jnp.bfloat16)
    own = total(2)
    own_ref[:, :middle] = (own[:, :middle] + from_left[0].astype(jnp.float32)).astype(jnp.bfloat16)
    own_ref[:, middle:] = (own[:, middle:] + from_right[0].astype(jnp.float32)).astype(jnp.bfloat16)


def sum_second(index, pair, arrived, part, depth):
    columns = pair[0].shape[1]
    middle = columns // 2
    specs = [
        pl.BlockSpec((part, middle), lambda i, index: (4 * i + (index[0] ^ 2), 0)),
        pl.BlockSpec((part, middle), lambda i, index: (4 * i + (index[0] ^ 1), 1)),
        pl.BlockSpec((part, columns), lambda i, index: (4 * i + index[0], 0)),
    ]
    two = pl.BlockSpec((2, part, middle), lambda i, index: (0, i, 0))
    half = pl.BlockSpec((part, middle), lambda i, index: (i, 0))
    shape = jax.ShapeDtypeStruct((depth * part, middle), jnp.bfloat16)
    return pl.pallas_call(
        sum_second_kernel,
        grid_spec=pltpu.PrefetchScalarGridSpec(
            num_scalar_prefetch=1,
            grid=(depth,),
            in_specs=specs * 2 + [two, two],
            out_specs=[half, half, pl.BlockSpec((part, columns), lambda i, index: (i, 0))],
        ),
        out_shape=[shape, shape, jax.ShapeDtypeStruct((depth * part, columns), jnp.bfloat16)],
        compiler_params=pltpu.CompilerParams(vmem_limit_bytes=48 << 20),
        cost_estimate=pl.CostEstimate(flops=0, bytes_accessed=0, transcendentals=0),
        name="sum_second",
    )(index, *([pair[0]] * 3 + [pair[1]] * 3), *arrived)


def ring_terms_kernel(depth, index_ref, own_ref, *refs):
    others, outputs = refs[:-depth], refs[-depth:]
    own = own_ref[...].astype(jnp.float32)
    rest = [other[...].astype(jnp.float32) for other in others]
    total = own + (rest[0] if len(rest) == 1 else jnp.concatenate(rest, axis=1))
    for step in range(depth):

        @pl.when(pl.program_id(0) == step)
        def _(step=step):
            outputs[step][...] = total.astype(jnp.bfloat16)


def ring_terms(index, values, rows, depth):
    columns = values[0].shape[1]
    at = lambda i, index: (lax.rem(index[1] + 2 * depth - 1 - i, depth), 0)
    shape = jax.ShapeDtypeStruct((rows, columns), jnp.bfloat16)
    return pl.pallas_call(
        functools.partial(ring_terms_kernel, depth),
        grid_spec=pltpu.PrefetchScalarGridSpec(
            num_scalar_prefetch=1,
            grid=(depth,),
            in_specs=[pl.BlockSpec((rows, value.shape[1]), at) for value in values],
            out_specs=[pl.BlockSpec((rows, columns), lambda i, index: (0, 0))] * depth,
        ),
        out_shape=[shape] * depth,
        compiler_params=pltpu.CompilerParams(vmem_limit_bytes=48 << 20),
        cost_estimate=pl.CostEstimate(flops=0, bytes_accessed=0, transcendentals=0),
        name="ring_terms",
    )(index, *values)


def back_kernel(left_ref, right_ref, out_ref):
    out_ref[...] = dot_back(left_ref[...], right_ref[...]).astype(jnp.bfloat16)


def back_low(left, right):
    whole = pl.BlockSpec(memory_space=pltpu.VMEM)
    return pl.pallas_call(
        back_kernel,
        out_shape=jax.ShapeDtypeStruct((left.shape[0], right.shape[0]), jnp.bfloat16),
        in_specs=[whole, whole],
        out_specs=whole,
        compiler_params=pltpu.CompilerParams(vmem_limit_bytes=48 << 20),
        cost_estimate=pl.CostEstimate(flops=0, bytes_accessed=0, transcendentals=0),
        name="back_low",
    )(left, right)


def product_kernel(chunk, pairs, index_ref, *refs):
    extra_ref = refs[2 * pairs] if len(refs) > 2 * pairs + 2 else None
    send_ref, keep_ref = refs[-2:]
    rows = send_ref.shape[0]
    core = index_ref[2]

    def put(lanes, whole):
        low, high = whole[:rows], whole[rows:]
        send_ref[:, lanes] = jnp.where(core == 0, high, low).astype(jnp.bfloat16)
        keep_ref[:, lanes] = jnp.where(core == 0, low, high).astype(jnp.bfloat16)

    base = 0
    for pair in range(pairs):
        left_ref, right_ref = refs[2 * pair : 2 * pair + 2]
        left = left_ref[...]
        for start in range(0, right_ref.shape[1], chunk):
            put(
                slice(base + start, base + start + chunk),
                dot_rows(left, right_ref[:, start : start + chunk]),
            )
        base += right_ref.shape[1]
    if extra_ref is not None:
        put(slice(base, None), extra_ref[...].astype(jnp.float32))


def product(index, pairs, extra, depth):
    tokens, rows = pairs[0][0].shape[0], pairs[0][0].shape[1] // depth
    inputs, specs = [index], [pl.BlockSpec(memory_space=pltpu.SMEM)]
    columns = 0
    for left, right in pairs:
        inputs += [left, right]
        specs += [
            pl.BlockSpec((tokens, rows), lambda i: (0, i)),
            pl.BlockSpec((tokens, right.shape[1]), lambda i: (0, 0)),
        ]
        columns += right.shape[1]
    wide = columns
    if extra is not None:
        inputs.append(extra)
        specs.append(pl.BlockSpec((rows, extra.shape[1]), lambda i: (i, 0)))
        wide += extra.shape[1]
    half = pl.BlockSpec((rows // 2, wide), lambda i: (i, 0))
    shape = jax.ShapeDtypeStruct((depth * rows // 2, wide), jnp.bfloat16)
    return tuple(
        pl.pallas_call(
            functools.partial(product_kernel, 512, len(pairs)),
            grid=(depth,),
            out_shape=[shape, shape],
            in_specs=specs,
            out_specs=[half, half],
            compiler_params=pltpu.CompilerParams(vmem_limit_bytes=48 << 20),
            cost_estimate=pl.CostEstimate(flops=0, bytes_accessed=0, transcendentals=0),
            name="product",
        )(*inputs)
    )


def place_kernel(part, middle, index_ref, *refs):
    *far, mine, from_x, from_y, out_ref = refs
    rep = index_ref[0]

    def put(offset, lanes, value):
        start = pl.multiple_of((rep ^ offset) * part, 16)
        out_ref[pl.ds(start, part), lanes] = value[...].astype(jnp.float32)

    put(0, slice(None), mine)
    put(1, slice(None), from_x)
    put(2, slice(None), from_y)
    if len(far) == 1:
        put(3, slice(None), far[0])
    else:
        put(3, slice(0, middle), far[0])
        put(3, slice(middle, None), far[1])


def place(index, values, part):
    columns = values[-1].shape[1]
    middle = columns // 2
    whole = pl.BlockSpec(memory_space=pltpu.VMEM)
    return pl.pallas_call(
        functools.partial(place_kernel, part, middle),
        out_shape=jax.ShapeDtypeStruct((4 * part, columns), jnp.float32),
        in_specs=[pl.BlockSpec(memory_space=pltpu.SMEM)] + [whole] * len(values),
        out_specs=whole,
        compiler_params=pltpu.CompilerParams(vmem_limit_bytes=32 << 20),
        cost_estimate=pl.CostEstimate(flops=0, bytes_accessed=0, transcendentals=0),
        name="place",
    )(index, *values)


def assemble_kernel(depth, part, middle, widths, index_ref, *refs):
    sources = refs[:12]
    count = len(widths)
    outputs = refs[12:12 + count]
    held = refs[12 + count:12 + 2 * count]
    arrived, left_here = refs[12 + 2 * count:]
    rows = part * 4
    columns = sum(widths)
    rep, z, core = index_ref[0], index_ref[1], index_ref[2]
    blocks = []
    for step in range(depth):
        for side in range(2):
            own, mine, from_x, from_y, left, right = sources[6 * side:6 * side + 6]
            which = core if side == 0 else 1 - core
            base = pl.multiple_of((lax.rem(z + depth - step, depth) * 2 + which) * rows, rows)
            if step == 0:
                blocks.append((base, [(own, 0, rows, 0, 0, columns)]))
                continue
            start = (step - 1) * part
            moves = [
                (mine, start, part, rep * part, 0, columns),
                (from_x, start, part, (rep ^ 1) * part, 0, columns),
                (from_y, start, part, (rep ^ 2) * part, 0, columns),
                (left, start, part, (rep ^ 3) * part, 0, middle),
                (right, start, part, (rep ^ 3) * part, middle, columns),
            ]
            blocks.append((base, moves))
    used = 0
    plan = []
    for base, moves in blocks:
        copies = []
        for source, start, height, offset, first, last in moves:
            edge = 0
            for buffer, width in zip(held, widths):
                low, high = max(first, edge), min(last, edge + width)
                if low < high:
                    copies.append(
                        pltpu.make_async_copy(
                            source.at[pl.ds(start, height), pl.ds(low - first, high - low)],
                            buffer.at[
                                pl.ds(pl.multiple_of(base + offset, 16), height),
                                pl.ds(low - edge, high - low),
                            ],
                            arrived.at[used],
                        )
                    )
                    used += 1
                edge += width
        plan.append((base, copies))
    for _, copies in plan:
        for copy in copies:
            copy.start()
    stores = []
    for base, copies in plan:
        for copy in copies:
            copy.wait()
        for buffer, output in zip(held, outputs):
            place = pl.ds(base, rows)
            stores.append(
                pltpu.make_async_copy(
                    buffer.at[place, :], output.at[place, :], left_here.at[len(stores)]
                )
            )
            stores[-1].start()
    for store in stores:
        store.wait()


def assemble(index, here, there, depth, part, middle, widths):
    rows = here[0].shape[0] * 2 * depth
    total = sum(widths) * rows
    count = 2 * (1 + 5 * (depth - 1)) * len(widths)
    return pl.pallas_call(
        functools.partial(assemble_kernel, depth, part, middle, widths),
        out_shape=[jax.ShapeDtypeStruct((rows, width), jnp.bfloat16) for width in widths],
        in_specs=[pl.BlockSpec(memory_space=pltpu.SMEM)] + [pl.BlockSpec(memory_space=pl.ANY)] * 12,
        out_specs=[pl.BlockSpec(memory_space=pl.ANY)] * len(widths),
        scratch_shapes=[pltpu.VMEM((rows, width), jnp.bfloat16) for width in widths]
        + [
            pltpu.SemaphoreType.DMA((count,)),
            pltpu.SemaphoreType.DMA((2 * depth * len(widths),)),
        ],
        compiler_params=pltpu.CompilerParams(vmem_limit_bytes=2 * total + (8 << 20)),
        cost_estimate=pl.CostEstimate(flops=0, bytes_accessed=0, transcendentals=0),
        name="assemble",
    )(index, *here, *there)


def body(
    groups,
    shards,
    tokens,
    lengths,
    group_live,
    w_query,
    w_key,
    w_value,
    w_out,
    w_gate,
    w_up,
    w_down,
    g_attn,
    g_query,
    g_key,
    g_ffn,
    cotangent,
):
    links = Links(groups, shards)
    shard_rows = w_query.shape[0]
    width = HD * (H + 2 * KV)

    def column(values):
        return jnp.pad(values, (0, shard_rows - values.shape[0]))[:, None]

    gains = jnp.concatenate([column(g) for g in (g_attn, g_ffn, g_query, g_key)], axis=1)
    gains = jnp.pad(gains, ((0, 0), (0, 124)))
    packed = jnp.concatenate([w_query, w_key, w_value, w_out, gains], axis=1)
    first_move = links.gather_of(packed, (width, w_out.shape[1], 128))
    gate_move = links.gather_of(w_gate, (w_gate.shape[1],))
    up_move = links.gather_of(w_up, (w_up.shape[1],))
    down_move = links.gather_of(w_down, (w_down.shape[1],))
    for _ in range(3):
        advance([first_move])
    for _ in range(3):
        advance([first_move, gate_move])
    full_qkv, full_out, full_gains = first_move.result()
    full_qkv = advance([gate_move], full_qkv)
    full_qkv = advance([up_move], full_qkv)
    head_rows = g_query.shape[0]
    all_gains = full_gains[:, :4].astype(jnp.float32)
    gain_attn = all_gains[:, 0]
    gain_ffn = all_gains[:, 1]
    gain_query = all_gains[:, 2].reshape(shards, shard_rows)[:, :head_rows].reshape(HD)
    gain_key = all_gains[:, 3].reshape(shards, shard_rows)[:, :head_rows].reshape(HD)

    row_count = tokens.shape[0]
    x_float = tokens.astype(jnp.float32)
    row_index, segment, position, keep_mask = layout(lengths[0], group_live[0], row_count)
    allowed = (segment[:, None] == segment[None, :]) & (row_index[None, :] <= row_index[:, None])
    bias = jnp.where(allowed, 0.0, masked_score).astype(jnp.float32)
    gain_rows = jnp.stack([jnp.tile(gain_query, 2), jnp.tile(gain_key, 2)])
    tables = (*rotary_tables(position), jnp.pad(gain_rows, ((0, 6), (0, 0))), bias)
    unit_one, inverse_one = normalize(x_float)
    attn_input = (unit_one * gain_attn).astype(jnp.bfloat16)
    qkv = jnp.dot(attn_input, full_qkv, preferred_element_type=jnp.float32)
    parts, logs = [], []
    for first in range(KV // 2):
        part, log = attend(qkv, tables, first, 1)
        if first == 0:
            qkv, part = advance([up_move], qkv, part)
        if first == 1:
            qkv, part = advance([gate_move], qkv, part)
        if first == 2:
            qkv, part = advance([up_move], qkv, part)
        if first == 3:
            part = advance([gate_move], part)
            part = advance([up_move], part)
            part = advance([down_move], part)
        parts.append(part)
        logs.append(log)
    attended = jnp.concatenate(parts, axis=1)
    hidden = x_float + keep_mask[:, None] * jnp.dot(
        attended, full_out, preferred_element_type=jnp.float32
    )
    unit_two, inverse_two = normalize(hidden)
    ffn_input = (unit_two * gain_ffn).astype(jnp.bfloat16)
    (full_gate,) = gate_move.result()
    full_gate = advance([down_move], full_gate)
    gate_proj = jnp.dot(ffn_input, full_gate, preferred_element_type=jnp.float32)
    gate_proj = advance([up_move], gate_proj)
    gate_proj = advance([down_move], gate_proj)
    gate_proj = advance([up_move], gate_proj)
    gate_proj = advance([down_move], gate_proj)
    (full_up,) = up_move.result()
    up_proj = jnp.dot(ffn_input, full_up, preferred_element_type=jnp.float32)
    inner_low = (jax.nn.silu(gate_proj) * up_proj).astype(jnp.bfloat16)
    inner_low = advance([down_move], inner_low)

    d_final = cotangent.astype(jnp.float32)
    d_ffn = (keep_mask[:, None] * d_final).astype(jnp.bfloat16)
    down_sum = links.sum_of([(inner_low, d_ffn)])
    d_ffn = advance([down_move], d_ffn)
    (full_down,) = down_move.result()
    full_down = advance([down_sum], full_down)
    d_gate, d_up = inner_back(d_ffn, full_down, gate_proj, up_proj)
    d_gate, d_up = advance([down_sum], d_gate, d_up)
    gate_sum = links.sum_of([(ffn_input, d_gate)], depth_first=True)
    d_gate, d_up = advance([gate_sum], d_gate, d_up)
    up_sum = links.sum_of([(ffn_input, d_up)])
    d_gate, d_up = advance([up_sum], d_gate, d_up)
    d_gate, d_up = advance([gate_sum], d_gate, d_up)
    d_ffn_input = ffn_back(d_gate, d_up, full_gate, full_up)
    d_hidden_norm, grad_gain_ffn = norm_back(d_ffn_input, unit_two, inverse_two, gain_ffn)
    d_hidden = d_final + d_hidden_norm
    d_attn = (keep_mask[:, None] * d_hidden).astype(jnp.bfloat16)
    d_attn = advance([down_sum], d_attn)
    d_attn = advance([up_sum], d_attn)
    d_attended = back_low(d_attn, full_out)
    plans = ([gate_sum], [down_sum], [up_sum], [up_sum, gate_sum, down_sum])
    gain_sums, outputs = 0.0, ()
    for first in range(KV // 2):
        *outputs, gain_sum = attend_back(qkv, tables, logs[first], d_attended, first, 1, outputs)
        if plans[first]:
            d_attended, *outputs = advance(plans[first], d_attended, *outputs)
        gain_sums = gain_sums + gain_sum
    d_query, d_key, d_value = outputs
    grad_gain_query = gain_sums[0, :HD] + gain_sums[0, HD:]
    grad_gain_key = gain_sums[1, :HD] + gain_sums[1, HD:]
    d_attn_input = (
        back_product(d_query, full_qkv[:, : H * HD])
        + back_product(d_key, full_qkv[:, H * HD : (H + KV) * HD])
        + back_product(d_value, full_qkv[:, (H + KV) * HD :])
    )
    d_x_norm, grad_gain_attn = norm_back(d_attn_input, unit_one, inverse_one, gain_attn)
    grad_tokens = (d_hidden + d_x_norm).astype(jnp.bfloat16)

    def spread(values):
        blocks = jnp.pad(
            values.reshape(shards, head_rows), ((0, 0), (0, shard_rows - head_rows))
        )
        return blocks.reshape(shards * shard_rows)

    gain_grads = jnp.stack(
        [grad_gain_attn, grad_gain_ffn, spread(grad_gain_query), spread(grad_gain_key)], axis=1
    )
    gain_grads = jnp.pad(gain_grads, ((0, 0), (0, 252))).astype(jnp.bfloat16)
    qkv_sum = links.sum_of(
        [(attn_input, value) for value in (d_query, d_key, d_value)] + [(attended, d_attn)],
        gain_grads,
    )
    inner_low = advance([qkv_sum], inner_low)
    block_out = ffn_out(inner_low, full_down, hidden, keep_mask[:, None])
    plans = (
        [qkv_sum],
        [up_sum],
        [down_sum],
        [gate_sum],
        [qkv_sum],
        [up_sum],
        [down_sum],
        [gate_sum],
        [qkv_sum],
        [up_sum],
        [gate_sum],
        [qkv_sum, down_sum],
        [up_sum, gate_sum],
        [qkv_sum],
        [qkv_sum],
        [qkv_sum],
    )
    for plan in plans:
        block_out = advance(plan, block_out)
    owned = qkv_sum.result()
    grad_down, grad_gate, grad_up = down_sum.result(), gate_sum.result(), up_sum.result()
    last = width + w_out.shape[1]
    return (
        block_out,
        grad_tokens,
        owned[:, : H * HD],
        owned[:, H * HD : (H + KV) * HD],
        owned[:, (H + KV) * HD : width],
        owned[:, width : width + w_out.shape[1]],
        grad_gate,
        grad_up,
        grad_down,
        owned[:, last],
        owned[:head_rows, last + 2],
        owned[:head_rows, last + 3],
        owned[:, last + 1],
    )


def solution(mesh):
    in_specs = (
        P(("rep", "shard"), None),
        P(("rep", "shard"), None),
        P("rep"),
        P("shard", None),
        P("shard", None),
        P("shard", None),
        P("shard", None),
        P("shard", None),
        P("shard", None),
        P("shard", None),
        P("shard"),
        P("shard"),
        P("shard"),
        P("shard"),
        P(("rep", "shard"), None),
    )
    out_specs = (
        P(("rep", "shard"), None),
        P(("rep", "shard"), None),
        P("shard", None),
        P("shard", None),
        P("shard", None),
        P("shard", None),
        P("shard", None),
        P("shard", None),
        P("shard", None),
        P("shard"),
        P("shard"),
        P("shard"),
        P("shard"),
    )
    return jax.shard_map(
        functools.partial(body, mesh.shape["rep"], mesh.shape["shard"]),
        mesh=mesh,
        in_specs=in_specs,
        out_specs=out_specs,
        check_vma=False,
    )
```

```python
import functools

import jax
import jax.numpy as jnp
from jax import lax
from jax.experimental import pallas as pl
from jax.experimental.pallas import tpu as pltpu
from jax.sharding import PartitionSpec as P

H = 16
KV = 8
HD = 64


epsilon = 1e-05
theta_base = 1000000.0
masked_score = -1e30


def layout(seq_lengths, live_rows, row_count):
    row_index = jnp.arange(row_count, dtype=jnp.int32)
    seq_ends = jnp.cumsum(seq_lengths)
    passed_ends = row_index[:, None] >= seq_ends[None, :]
    segment = jnp.sum(passed_ends.astype(jnp.int32), axis=1, dtype=jnp.int32)
    begins = jnp.sum(jnp.where(passed_ends, seq_lengths[None, :], 0), axis=1, dtype=jnp.int32)
    live_mask = row_index < live_rows
    segment = jnp.where(live_mask, segment, -1)
    position = (row_index - begins).astype(jnp.float32)
    return (row_index, segment, position, live_mask.astype(jnp.float32))


def rotary_tables(position):
    half_width = HD // 2
    frequency = theta_base ** (-2.0 * jnp.arange(half_width, dtype=jnp.float32) / HD)
    angles = position[:, None] * frequency[None, :]
    cosine, sine = jnp.cos(angles), jnp.sin(angles)
    return (
        jnp.concatenate([cosine] * 4, axis=1),
        jnp.concatenate([-sine, sine, -sine, sine], axis=1),
    )


def normalize(values):
    inverse_rms = lax.rsqrt(jnp.mean(values * values, axis=-1, keepdims=True) + epsilon)
    return (values * inverse_rms, inverse_rms)


def norm_back(incoming, unit_values, inverse_rms, gain):
    grad_unit = incoming * gain
    grad_values = inverse_rms * (
        grad_unit - unit_values * jnp.mean(unit_values * grad_unit, axis=-1, keepdims=True)
    )
    grad_gain = jnp.sum((incoming * unit_values).reshape(-1, unit_values.shape[-1]), axis=0)
    return (grad_values, grad_gain)


def rows_product(left, right):
    return lax.dot_general(
        left, right, (((0,), (0,)), ((), ())), preferred_element_type=jnp.float32
    )


def back_product(left, right):
    return lax.dot_general(
        left, right, (((1,), (1,)), ((), ())), preferred_element_type=jnp.float32
    )


def lane_index(shape):
    return lax.broadcasted_iota(jnp.int32, shape, len(shape) - 1)


def head_mean(values):
    first = lane_index(values.shape) < HD
    low = jnp.sum(jnp.where(first, values, 0.0), axis=-1, keepdims=True)
    high = jnp.sum(jnp.where(first, 0.0, values), axis=-1, keepdims=True)
    return jnp.where(first, low, high) * (1.0 / HD)


def swap_halves(values):
    front = lane_index(values.shape) % HD < HD // 2
    return jnp.where(
        front, pltpu.roll(values, 2 * HD - HD // 2, 1), pltpu.roll(values, HD // 2, 1)
    )


def head_unit(raw):
    inverse = lax.rsqrt(head_mean(raw * raw) + epsilon)
    return raw * inverse, inverse


def head_norm_back(incoming, unit_values, inverse, gain):
    grad_unit = incoming * gain
    return inverse * (grad_unit - unit_values * head_mean(unit_values * grad_unit))


def pair_of(values, which):
    first = lane_index(values.shape) < HD
    kept = jnp.where(first, values, 0.0) if which == 0 else jnp.where(first, 0.0, values)
    moved = pltpu.roll(kept, HD, 1)
    pair = (kept, moved) if which == 0 else (moved, kept)
    return tuple(value.astype(jnp.bfloat16) for value in pair)


def dot_rows(left, right):
    return lax.dot_general(
        left, right, (((0,), (0,)), ((), ())), preferred_element_type=jnp.float32
    )


def dot_back(left, right):
    return lax.dot_general(
        left, right, (((1,), (1,)), ((), ())), preferred_element_type=jnp.float32
    )


def dot_plain(left, right):
    return lax.dot_general(
        left, right, (((1,), (0,)), ((), ())), preferred_element_type=jnp.float32
    )


def attend_kernel(block, q_ref, k_ref, v_ref, cos_ref, sin_ref, gain_ref, bias_ref, out_ref, log_ref):
    rows = q_ref.shape[0]
    tile = 2 * HD
    cosine, sine = cos_ref[...], sin_ref[...]
    first = lane_index((block, tile)) < HD

    def turned(raw, gain):
        unit_values, _ = head_unit(raw)
        scaled = unit_values * gain
        return cosine * scaled + sine * swap_halves(scaled)

    k_turned = turned(k_ref[...], gain_ref[1:2, :])
    v_values = v_ref[...]
    for which in range(2):
        lanes = slice(which * tile, (which + 1) * tile)
        query = (turned(q_ref[:, lanes], gain_ref[0:1, :]).astype(jnp.bfloat16)) * HD ** (-0.5)
        query = query.astype(jnp.bfloat16)
        keys = pair_of(k_turned, which)
        values = pair_of(v_values, which)
        for start in range(0, rows, block):
            stop = start + block
            bias = bias_ref[start:stop, :stop]
            result = jnp.zeros((block, tile), jnp.float32)
            logs = []
            for head in range(2):
                scores = dot_back(query[start:stop], keys[head][:stop]) + bias
                top = jnp.max(scores, axis=-1, keepdims=True)
                weights = jnp.exp(scores - top)
                totals = jnp.sum(weights, axis=-1, keepdims=True)
                low = (weights * (1.0 / totals)).astype(jnp.bfloat16)
                result += dot_plain(low, values[head][:stop])
                logs.append(top + jnp.log(totals))
            out_ref[start:stop, lanes] = result.astype(jnp.bfloat16)
            log_ref[start:stop, lanes] = jnp.where(first, logs[0], logs[1])


def attend_back_kernel(
    block,
    q_ref,
    k_ref,
    v_ref,
    cos_ref,
    sin_ref,
    gain_ref,
    bias_ref,
    log_ref,
    grad_ref,
    *refs,
):
    rows = q_ref.shape[0]
    tile = 2 * HD
    cosine, sine = cos_ref[...], sin_ref[...]
    dq_ref, dk_ref, dv_ref, gain_grad_ref, key_sum, value_sum = refs[-6:]
    query_gain, key_gain = gain_ref[0:1, :], gain_ref[1:2, :]
    first = lane_index((rows, tile)) < HD
    scale = HD ** (-0.5)

    @pl.when(pl.program_id(0) == 0)
    def _():
        gain_grad_ref[...] = jnp.zeros_like(gain_grad_ref)

    def turned(scaled):
        return cosine * scaled + sine * swap_halves(scaled)

    def back(incoming, unit_values, inverse, gain, row):
        flat = cosine * incoming - sine * swap_halves(incoming)
        gain_grad_ref[row:row + 1, :] += jnp.sum(flat * unit_values, axis=0, keepdims=True)
        return head_norm_back(flat, unit_values, inverse, gain).astype(jnp.bfloat16)

    k_unit, k_inverse = head_unit(k_ref[...])
    k_turned = turned(k_unit * key_gain)
    v_values = v_ref[...]
    key_parts, value_parts = [], []
    for which in range(2):
        lanes = slice(which * tile, (which + 1) * tile)
        q_unit, q_inverse = head_unit(q_ref[:, lanes])
        query = (turned(q_unit * query_gain)).astype(jnp.bfloat16)
        query = (query * scale).astype(jnp.bfloat16)
        keys = pair_of(k_turned, which)
        values = pair_of(v_values, which)
        key_sum[...] = jnp.zeros_like(key_sum)
        value_sum[...] = jnp.zeros_like(value_sum)
        d_query = []
        for start in range(0, rows, block):
            stop = start + block
            bias = bias_ref[start:stop, :stop]
            grad = grad_ref[start:stop, lanes]
            part = jnp.zeros((block, tile), jnp.float32)
            for head in range(2):
                column = which * tile + head * HD
                logs = log_ref[start:stop, column:column + 1]
                scores = dot_back(query[start:stop], keys[head][:stop]) + bias
                probability = jnp.exp(scores - logs)
                grad_prob = dot_back(grad, values[head][:stop])
                terms = jnp.sum(probability * grad_prob, axis=-1, keepdims=True)
                grad_scores = (probability * (grad_prob - terms)).astype(jnp.bfloat16)
                part += dot_plain(grad_scores, keys[head][:stop])
                key_sum[head, :stop, :] += dot_rows(grad_scores, query[start:stop])
                value_sum[head, :stop, :] += dot_rows(probability.astype(jnp.bfloat16), grad)
            d_query.append(part * scale)
        dq_ref[:, lanes] = back(
            jnp.concatenate(d_query, axis=0), q_unit, q_inverse, query_gain, 0
        )
        for total, parts in ((key_sum, key_parts), (value_sum, value_parts)):
            joined = jnp.where(first, total[0], total[1])
            parts.append(joined + pltpu.roll(joined, HD, 1))
    d_key = jnp.where(first, key_parts[0], key_parts[1])
    dk_ref[...] = back(d_key, k_unit, k_inverse, key_gain, 1)
    dv_ref[...] = jnp.where(first, value_parts[0], value_parts[1]).astype(jnp.bfloat16)


def attention_specs(rows, first=0):
    tile = 2 * HD
    fixed = lambda i: (0, 0)
    return [
        pl.BlockSpec((rows, 2 * tile), lambda i: (0, first + i)),
        pl.BlockSpec((rows, tile), lambda i: (0, H // 2 + first + i)),
        pl.BlockSpec((rows, tile), lambda i: (0, H // 2 + KV // 2 + first + i)),
        pl.BlockSpec((rows, tile), fixed),
        pl.BlockSpec((rows, tile), fixed),
        pl.BlockSpec((8, tile), fixed),
        pl.BlockSpec((rows, rows), fixed),
    ]


def attend(qkv, tables, first, count):
    rows = qkv.shape[0]
    wide = pl.BlockSpec((rows, 4 * HD), lambda i: (0, i))
    return pl.pallas_call(
        functools.partial(attend_kernel, rows // 2),
        grid=(count,),
        out_shape=[
            jax.ShapeDtypeStruct((rows, 4 * HD * count), jnp.bfloat16),
            jax.ShapeDtypeStruct((rows, 4 * HD * count), jnp.float32),
        ],
        in_specs=attention_specs(rows, first),
        out_specs=[wide, wide],
        compiler_params=pltpu.CompilerParams(vmem_limit_bytes=48 << 20),
        cost_estimate=pl.CostEstimate(flops=0, bytes_accessed=0, transcendentals=0),
        name="attend",
    )(qkv, qkv, qkv, *tables)


def attend_back(qkv, tables, logs, grad, first, count, before=()):
    rows = qkv.shape[0]
    tile = 2 * HD
    wide = pl.BlockSpec((rows, 2 * tile), lambda i: (0, i))
    taken = pl.BlockSpec((rows, 2 * tile), lambda i: (0, first + i))
    narrow = pl.BlockSpec((rows, tile), lambda i: (0, first + i))
    specs = attention_specs(rows, first) + [wide, taken]
    return pl.pallas_call(
        functools.partial(attend_back_kernel, rows // 2),
        grid=(count,),
        out_shape=[
            jax.ShapeDtypeStruct((rows, H * HD), jnp.bfloat16),
            jax.ShapeDtypeStruct((rows, KV * HD), jnp.bfloat16),
            jax.ShapeDtypeStruct((rows, KV * HD), jnp.bfloat16),
            jax.ShapeDtypeStruct((8, tile), jnp.float32),
        ],
        in_specs=specs + [pl.BlockSpec(memory_space=pl.ANY)] * len(before),
        input_output_aliases={len(specs) + i: i for i in range(len(before))},
        out_specs=[taken, narrow, narrow, pl.BlockSpec((8, tile), lambda i: (0, 0))],
        scratch_shapes=[
            pltpu.VMEM((2, rows, tile), jnp.float32),
            pltpu.VMEM((2, rows, tile), jnp.float32),
        ],
        compiler_params=pltpu.CompilerParams(vmem_limit_bytes=48 << 20),
        cost_estimate=pl.CostEstimate(flops=0, bytes_accessed=0, transcendentals=0),
        name="attend_back",
    )(qkv, qkv, qkv, *tables, logs, grad, *before)


def inner_back_kernel(d_ref, down_ref, gate_ref, up_ref, d_gate_ref, d_up_ref):
    d_inner = dot_back(d_ref[...], down_ref[...])
    gate = gate_ref[...]
    sigmoid = jax.nn.sigmoid(gate)
    d_gate = d_inner * up_ref[...] * sigmoid * (1.0 + gate * (1.0 - sigmoid))
    d_gate_ref[...] = d_gate.astype(jnp.bfloat16)
    d_up_ref[...] = (d_inner * gate * sigmoid).astype(jnp.bfloat16)


def inner_back(d_ffn, full_down, gate_proj, up_proj):
    (rows, width), units = d_ffn.shape, full_down.shape[0]
    tile = 512
    columns = pl.BlockSpec((rows, tile), lambda i: (0, i))
    shape = jax.ShapeDtypeStruct((rows, units), jnp.bfloat16)
    return pl.pallas_call(
        inner_back_kernel,
        grid=(units // tile,),
        out_shape=[shape, shape],
        in_specs=[
            pl.BlockSpec((rows, width), lambda i: (0, 0)),
            pl.BlockSpec((tile, width), lambda i: (i, 0)),
            columns,
            columns,
        ],
        out_specs=[columns, columns],
        compiler_params=pltpu.CompilerParams(vmem_limit_bytes=48 << 20),
        cost_estimate=pl.CostEstimate(flops=0, bytes_accessed=0, transcendentals=0),
        name="inner_back",
    )(d_ffn, full_down, gate_proj, up_proj)


def ffn_out_kernel(inner_ref, down_ref, hidden_ref, keep_ref, out_ref, total):
    step = pl.program_id(0)
    part = dot_plain(inner_ref[...], down_ref[...])

    @pl.when(step == 0)
    def _():
        total[...] = part

    @pl.when(step > 0)
    def _():
        total[...] += part

    @pl.when(step == pl.num_programs(0) - 1)
    def _():
        out_ref[...] = (hidden_ref[...] + keep_ref[...] * total[...]).astype(jnp.bfloat16)


def ffn_out(inner_low, full_down, hidden, keep_column):
    (rows, units), width = inner_low.shape, full_down.shape[1]
    tile = 512
    fixed = lambda i: (0, 0)
    return pl.pallas_call(
        ffn_out_kernel,
        grid=(units // tile,),
        out_shape=jax.ShapeDtypeStruct((rows, width), jnp.bfloat16),
        in_specs=[
            pl.BlockSpec((rows, tile), lambda i: (0, i)),
            pl.BlockSpec((tile, width), lambda i: (i, 0)),
            pl.BlockSpec((rows, width), fixed),
            pl.BlockSpec((rows, 1), fixed),
        ],
        out_specs=pl.BlockSpec((rows, width), fixed),
        scratch_shapes=[pltpu.VMEM((rows, width), jnp.float32)],
        compiler_params=pltpu.CompilerParams(vmem_limit_bytes=48 << 20),
        cost_estimate=pl.CostEstimate(flops=0, bytes_accessed=0, transcendentals=0),
        name="ffn_out",
    )(inner_low, full_down, hidden, keep_column)


def ffn_back_kernel(d_gate_ref, d_up_ref, gate_ref, up_ref, out_ref):
    part = dot_back(d_gate_ref[...], gate_ref[...]) + dot_back(d_up_ref[...], up_ref[...])

    @pl.when(pl.program_id(0) == 0)
    def _():
        out_ref[...] = part

    @pl.when(pl.program_id(0) > 0)
    def _():
        out_ref[...] += part


def ffn_back(d_gate, d_up, full_gate, full_up):
    (rows, units), width = d_gate.shape, full_gate.shape[0]
    tile = 512
    left = pl.BlockSpec((rows, tile), lambda i: (0, i))
    right = pl.BlockSpec((width, tile), lambda i: (0, i))
    return pl.pallas_call(
        ffn_back_kernel,
        grid=(units // tile,),
        out_shape=jax.ShapeDtypeStruct((rows, width), jnp.float32),
        in_specs=[left, left, right, right],
        out_specs=pl.BlockSpec((rows, width), lambda i: (0, 0)),
        compiler_params=pltpu.CompilerParams(vmem_limit_bytes=48 << 20),
        cost_estimate=pl.CostEstimate(flops=0, bytes_accessed=0, transcendentals=0),
        name="ffn_back",
    )(d_gate, d_up, full_gate, full_up)


class Links:
    def __init__(self, groups, shards):
        self.groups = groups
        self.shards = shards
        self.depth = shards // 2
        rep = lax.axis_index("rep")
        shard = lax.axis_index("shard")
        self.rep = rep
        self.z = shard // 2
        self.core = shard % 2
        self.index = jnp.stack([rep, self.z, self.core]).astype(jnp.int32)

    def across_core(self, value):
        return lax.ppermute(value, "shard", [(s, s ^ 1) for s in range(self.shards)])

    def across_x(self, value):
        return lax.ppermute(value, "rep", [(r, r ^ 1) for r in range(self.groups)])

    def across_y(self, value):
        return lax.ppermute(value, "rep", [(r, r ^ 2) for r in range(self.groups)])

    def along_z(self, value):
        pairs = [(s, (s + 2) % self.shards) for s in range(self.shards)]
        return lax.ppermute(value, "shard", pairs)

    def fits(self, rows):
        return self.groups == 4 and self.shards % 2 == 0 and rows % 64 == 0

    def gather_of(self, shard, widths):
        kind = Gather if self.fits(shard.shape[0]) else PlainGather
        return kind(self, shard, widths)

    def sum_of(self, pairs, extra=None, depth_first=False):
        kind = Sum if self.fits(pairs[0][0].shape[1] // self.shards) else PlainSum
        return kind(self, pairs, extra, depth_first)


def add(*values):
    return functools.reduce(jnp.add, [value.astype(jnp.float32) for value in values])


def advance(moves, *others):
    states = [(move.held, move.flying) for move in moves]
    states, others = lax.optimization_barrier((states, others))
    sends = []
    for move, (held, flying) in zip(moves, states):
        move.held, move.flying = held, flying
        move.held, move.sends = next(move.work)
        sends.append([value for _, value in move.sends])
    sends, others = lax.optimization_barrier((sends, others))
    for move, values in zip(moves, sends):
        move.flying = tuple(link(value) for (link, _), value in zip(move.sends, values))
    return others[0] if len(others) == 1 else others


def settle(moves, *others):
    states = [(move.held, move.flying) for move in moves]
    states, others = lax.optimization_barrier((states, others))
    for move, (held, flying) in zip(moves, states):
        move.held, move.flying = held, flying
    return others[0] if len(others) == 1 else others


class Moves:
    held = ()
    flying = ()

    def still(self):
        while True:
            yield (), ()

    def finish(self):
        for self.held, sends in self.work:
            self.flying = tuple(link(value) for link, value in sends)


class PlainGather(Moves):
    def __init__(self, links, shard, widths):
        self.shard, self.widths = shard, widths
        self.work = self.still()

    def result(self):
        whole = lax.all_gather(self.shard, "shard", axis=0, tiled=True)
        cuts = [sum(self.widths[:i]) for i in range(1, len(self.widths))]
        return jnp.split(whole, cuts, axis=1)


class PlainSum(Moves):
    def __init__(self, links, pairs, extra, depth_first):
        parts = [rows_product(left, right).astype(jnp.bfloat16) for left, right in pairs]
        self.low = jnp.concatenate(parts + ([] if extra is None else [extra]), axis=1)
        self.work = self.still()

    def result(self):
        owned = lax.psum_scatter(self.low, "shard", scatter_dimension=0, tiled=True)
        return lax.psum(owned, "rep").astype(jnp.float32)


class Gather(Moves):
    def __init__(self, links, shard, widths):
        self.links, self.shard, self.widths = links, shard, widths
        rows, self.columns = shard.shape
        self.part = rows // links.groups
        self.middle = self.columns // 256 * 128
        self.held = (lax.dynamic_slice_in_dim(shard, links.rep * self.part, self.part, axis=0),)
        self.work = self.stages()

    def stages(self):
        links, middle = self.links, self.middle
        moving, pieces = self.held[0], ()
        for step in range(links.depth - 1):
            moves = ((links.along_z, moving),)
            if step == 0:
                moves += ((links.across_core, self.shard),)
            yield pieces, moves
            moving = self.flying[0]
            pieces = self.held + self.flying
        first, other, *rest = pieces
        mine = jnp.concatenate([first, *rest], axis=0)
        yield (mine, other), (
            (links.across_x, mine),
            (links.across_y, mine),
            (links.across_core, mine),
        )
        from_x, from_y, _ = self.flying
        yield self.held + self.flying, (
            (links.across_y, from_x[:, :middle]),
            (links.across_x, from_y[:, middle:]),
            (links.across_core, from_x),
            (links.across_core, from_y),
        )
        yield self.held + self.flying, (
            (links.across_core, self.flying[0]),
            (links.across_core, self.flying[1]),
        )

    def result(self):
        self.finish()
        mine, other, from_x, from_y, mine_core, left, right, x_core, y_core = self.held
        here = (self.shard, mine, from_x, from_y, left, right)
        there = (other, mine_core, x_core, y_core, *self.flying)
        links = self.links
        return assemble(
            links.index, here, there, links.depth, self.part, self.middle, self.widths
        )


class Sum(Moves):
    def __init__(self, links, pairs, extra, depth_first):
        self.links = links
        self.part = pairs[0][0].shape[1] // links.shards // links.groups
        self.held = product(links.index, pairs, extra, links.depth)
        self.work = self.stages(depth_first)

    def result(self):
        self.finish()
        return place(self.links.index, self.flying + self.held, self.part)

    def stages(self, depth_first):
        links, part = self.links, self.part
        yield (self.held[1],), ((links.across_core, self.held[0]),)
        pair = self.held + self.flying
        if depth_first:
            yield from self.along(pair, links.groups * part)
            yield from self.across((self.held[0], self.flying[0]), 1)
            own, left, right = self.held + self.flying
            mine = jnp.concatenate(
                [add(own[:, : left.shape[1]], left), add(own[:, left.shape[1] :], right)], axis=1
            )
        else:
            yield from self.across(pair, links.depth)
            yield from self.along(self.held + self.flying, part)
            mine = add(self.held[0], self.flying[0])
        mine = mine.astype(jnp.bfloat16)
        middle = mine.shape[1] // 2
        yield (mine,), ((links.across_x, mine), (links.across_y, mine))
        from_x, from_y = self.flying
        yield self.held + (from_x, from_y), (
            (links.across_y, from_x[:, :middle]),
            (links.across_x, from_y[:, middle:]),
        )

    def across(self, pair, depth):
        links, part = self.links, self.part
        left, right = sum_first(links.index, pair, part, depth)
        yield pair, ((links.across_x, left), (links.across_y, right))
        left, right, own = sum_second(links.index, self.held, self.flying, part, depth)
        yield (own,), ((links.across_y, left), (links.across_x, right))

    def along(self, values, rows):
        links = self.links
        moving, *terms = ring_terms(links.index, values, rows, links.depth)
        yield tuple(terms), ((links.along_z, moving),)
        for _ in range(links.depth - 2):
            moving = add(self.held[0], self.flying[0]).astype(jnp.bfloat16)
            yield self.held[1:], ((links.along_z, moving),)


def sum_first_kernel(index_ref, *refs):
    keep, received = refs[0:3], refs[3:6]
    left_ref, right_ref = refs[6:]

    def total(place):
        return keep[place][...].astype(jnp.float32) + received[place][...].astype(jnp.float32)

    both = total(2).astype(jnp.bfloat16)
    middle = left_ref.shape[2]
    left_ref[0] = total(0).astype(jnp.bfloat16)
    left_ref[1] = both[:, :middle]
    right_ref[0] = total(1).astype(jnp.bfloat16)
    right_ref[1] = both[:, middle:]


def sum_first(index, pair, part, depth):
    columns = pair[0].shape[1]
    middle = columns // 2
    specs = [
        pl.BlockSpec((part, middle), lambda i, index: (4 * i + (index[0] ^ 1), 0)),
        pl.BlockSpec((part, middle), lambda i, index: (4 * i + (index[0] ^ 2), 1)),
        pl.BlockSpec((part, columns), lambda i, index: (4 * i + (index[0] ^ 3), 0)),
    ]
    half = pl.BlockSpec((2, part, middle), lambda i, index: (0, i, 0))
    shape = jax.ShapeDtypeStruct((2, depth * part, middle), jnp.bfloat16)
    return pl.pallas_call(
        sum_first_kernel,
        grid_spec=pltpu.PrefetchScalarGridSpec(
            num_scalar_prefetch=1, grid=(depth,), in_specs=specs * 2, out_specs=[half, half]
        ),
        out_shape=[shape, shape],
        compiler_params=pltpu.CompilerParams(vmem_limit_bytes=48 << 20),
        cost_estimate=pl.CostEstimate(flops=0, bytes_accessed=0, transcendentals=0),
        name="sum_first",
    )(index, *([pair[0]] * 3 + [pair[1]] * 3))


def sum_second_kernel(index_ref, *refs):
    keep, received = refs[0:3], refs[3:6]
    from_left, from_right, left_ref, right_ref, own_ref = refs[6:]
    middle = left_ref.shape[1]

    def total(place):
        return keep[place][...].astype(jnp.float32) + received[place][...].astype(jnp.float32)

    left_ref[...] = (total(0) + from_left[1].astype(jnp.float32)).astype(jnp.bfloat16)
    right_ref[...] = (total(1) + from_right[1].astype(jnp.float32)).astype(jnp.bfloat16)
    own = total(2)
    own_ref[:, :middle] = (own[:, :middle] + from_left[0].astype(jnp.float32)).astype(jnp.bfloat16)
    own_ref[:, middle:] = (own[:, middle:] + from_right[0].astype(jnp.float32)).astype(jnp.bfloat16)


def sum_second(index, pair, arrived, part, depth):
    columns = pair[0].shape[1]
    middle = columns // 2
    specs = [
        pl.BlockSpec((part, middle), lambda i, index: (4 * i + (index[0] ^ 2), 0)),
        pl.BlockSpec((part, middle), lambda i, index: (4 * i + (index[0] ^ 1), 1)),
        pl.BlockSpec((part, columns), lambda i, index: (4 * i + index[0], 0)),
    ]
    two = pl.BlockSpec((2, part, middle), lambda i, index: (0, i, 0))
    half = pl.BlockSpec((part, middle), lambda i, index: (i, 0))
    shape = jax.ShapeDtypeStruct((depth * part, middle), jnp.bfloat16)
    return pl.pallas_call(
        sum_second_kernel,
        grid_spec=pltpu.PrefetchScalarGridSpec(
            num_scalar_prefetch=1,
            grid=(depth,),
            in_specs=specs * 2 + [two, two],
            out_specs=[half, half, pl.BlockSpec((part, columns), lambda i, index: (i, 0))],
        ),
        out_shape=[shape, shape, jax.ShapeDtypeStruct((depth * part, columns), jnp.bfloat16)],
        compiler_params=pltpu.CompilerParams(vmem_limit_bytes=48 << 20),
        cost_estimate=pl.CostEstimate(flops=0, bytes_accessed=0, transcendentals=0),
        name="sum_second",
    )(index, *([pair[0]] * 3 + [pair[1]] * 3), *arrived)


def ring_terms_kernel(depth, index_ref, own_ref, *refs):
    others, outputs = refs[:-depth], refs[-depth:]
    own = own_ref[...].astype(jnp.float32)
    rest = [other[...].astype(jnp.float32) for other in others]
    total = own + (rest[0] if len(rest) == 1 else jnp.concatenate(rest, axis=1))
    for step in range(depth):

        @pl.when(pl.program_id(0) == step)
        def _(step=step):
            outputs[step][...] = total.astype(jnp.bfloat16)


def ring_terms(index, values, rows, depth):
    columns = values[0].shape[1]
    at = lambda i, index: (lax.rem(index[1] + 2 * depth - 1 - i, depth), 0)
    shape = jax.ShapeDtypeStruct((rows, columns), jnp.bfloat16)
    return pl.pallas_call(
        functools.partial(ring_terms_kernel, depth),
        grid_spec=pltpu.PrefetchScalarGridSpec(
            num_scalar_prefetch=1,
            grid=(depth,),
            in_specs=[pl.BlockSpec((rows, value.shape[1]), at) for value in values],
            out_specs=[pl.BlockSpec((rows, columns), lambda i, index: (0, 0))] * depth,
        ),
        out_shape=[shape] * depth,
        compiler_params=pltpu.CompilerParams(vmem_limit_bytes=48 << 20),
        cost_estimate=pl.CostEstimate(flops=0, bytes_accessed=0, transcendentals=0),
        name="ring_terms",
    )(index, *values)


def back_kernel(left_ref, right_ref, out_ref):
    out_ref[...] = dot_back(left_ref[...], right_ref[...]).astype(jnp.bfloat16)


def back_low(left, right):
    whole = pl.BlockSpec(memory_space=pltpu.VMEM)
    return pl.pallas_call(
        back_kernel,
        out_shape=jax.ShapeDtypeStruct((left.shape[0], right.shape[0]), jnp.bfloat16),
        in_specs=[whole, whole],
        out_specs=whole,
        compiler_params=pltpu.CompilerParams(vmem_limit_bytes=48 << 20),
        cost_estimate=pl.CostEstimate(flops=0, bytes_accessed=0, transcendentals=0),
        name="back_low",
    )(left, right)


def product_kernel(chunk, pairs, index_ref, *refs):
    extra_ref = refs[2 * pairs] if len(refs) > 2 * pairs + 2 else None
    send_ref, keep_ref = refs[-2:]
    rows = send_ref.shape[0]
    core = index_ref[2]

    def put(lanes, whole):
        low, high = whole[:rows], whole[rows:]
        send_ref[:, lanes] = jnp.where(core == 0, high, low).astype(jnp.bfloat16)
        keep_ref[:, lanes] = jnp.where(core == 0, low, high).astype(jnp.bfloat16)

    base = 0
    for pair in range(pairs):
        left_ref, right_ref = refs[2 * pair : 2 * pair + 2]
        left = left_ref[...]
        for start in range(0, right_ref.shape[1], chunk):
            put(
                slice(base + start, base + start + chunk),
                dot_rows(left, right_ref[:, start : start + chunk]),
            )
        base += right_ref.shape[1]
    if extra_ref is not None:
        put(slice(base, None), extra_ref[...].astype(jnp.float32))


def product(index, pairs, extra, depth):
    tokens, rows = pairs[0][0].shape[0], pairs[0][0].shape[1] // depth
    inputs, specs = [index], [pl.BlockSpec(memory_space=pltpu.SMEM)]
    columns = 0
    for left, right in pairs:
        inputs += [left, right]
        specs += [
            pl.BlockSpec((tokens, rows), lambda i: (0, i)),
            pl.BlockSpec((tokens, right.shape[1]), lambda i: (0, 0)),
        ]
        columns += right.shape[1]
    wide = columns
    if extra is not None:
        inputs.append(extra)
        specs.append(pl.BlockSpec((rows, extra.shape[1]), lambda i: (i, 0)))
        wide += extra.shape[1]
    half = pl.BlockSpec((rows // 2, wide), lambda i: (i, 0))
    shape = jax.ShapeDtypeStruct((depth * rows // 2, wide), jnp.bfloat16)
    return tuple(
        pl.pallas_call(
            functools.partial(product_kernel, 512, len(pairs)),
            grid=(depth,),
            out_shape=[shape, shape],
            in_specs=specs,
            out_specs=[half, half],
            compiler_params=pltpu.CompilerParams(vmem_limit_bytes=48 << 20),
            cost_estimate=pl.CostEstimate(flops=0, bytes_accessed=0, transcendentals=0),
            name="product",
        )(*inputs)
    )


def place_kernel(part, middle, index_ref, *refs):
    *far, mine, from_x, from_y, out_ref = refs
    rep = index_ref[0]

    def put(offset, lanes, value):
        start = pl.multiple_of((rep ^ offset) * part, 16)
        out_ref[pl.ds(start, part), lanes] = value[...].astype(jnp.float32)

    put(0, slice(None), mine)
    put(1, slice(None), from_x)
    put(2, slice(None), from_y)
    if len(far) == 1:
        put(3, slice(None), far[0])
    else:
        put(3, slice(0, middle), far[0])
        put(3, slice(middle, None), far[1])


def place(index, values, part):
    columns = values[-1].shape[1]
    middle = columns // 2
    whole = pl.BlockSpec(memory_space=pltpu.VMEM)
    return pl.pallas_call(
        functools.partial(place_kernel, part, middle),
        out_shape=jax.ShapeDtypeStruct((4 * part, columns), jnp.float32),
        in_specs=[pl.BlockSpec(memory_space=pltpu.SMEM)] + [whole] * len(values),
        out_specs=whole,
        compiler_params=pltpu.CompilerParams(vmem_limit_bytes=32 << 20),
        cost_estimate=pl.CostEstimate(flops=0, bytes_accessed=0, transcendentals=0),
        name="place",
    )(index, *values)


def assemble_kernel(depth, part, middle, widths, index_ref, *refs):
    sources = refs[:12]
    count = len(widths)
    outputs = refs[12:12 + count]
    held = refs[12 + count:12 + 2 * count]
    arrived, left_here = refs[12 + 2 * count:]
    rows = part * 4
    columns = sum(widths)
    rep, z, core = index_ref[0], index_ref[1], index_ref[2]
    blocks = []
    for step in range(depth):
        for side in range(2):
            own, mine, from_x, from_y, left, right = sources[6 * side:6 * side + 6]
            which = core if side == 0 else 1 - core
            base = pl.multiple_of((lax.rem(z + depth - step, depth) * 2 + which) * rows, rows)
            if step == 0:
                blocks.append((base, [(own, 0, rows, 0, 0, columns)]))
                continue
            start = (step - 1) * part
            moves = [
                (mine, start, part, rep * part, 0, columns),
                (from_x, start, part, (rep ^ 1) * part, 0, columns),
                (from_y, start, part, (rep ^ 2) * part, 0, columns),
                (left, start, part, (rep ^ 3) * part, 0, middle),
                (right, start, part, (rep ^ 3) * part, middle, columns),
            ]
            blocks.append((base, moves))
    used = 0
    plan = []
    for base, moves in blocks:
        copies = []
        for source, start, height, offset, first, last in moves:
            edge = 0
            for buffer, width in zip(held, widths):
                low, high = max(first, edge), min(last, edge + width)
                if low < high:
                    copies.append(
                        pltpu.make_async_copy(
                            source.at[pl.ds(start, height), pl.ds(low - first, high - low)],
                            buffer.at[
                                pl.ds(pl.multiple_of(base + offset, 16), height),
                                pl.ds(low - edge, high - low),
                            ],
                            arrived.at[used],
                        )
                    )
                    used += 1
                edge += width
        plan.append((base, copies))
    for _, copies in plan:
        for copy in copies:
            copy.start()
    stores = []
    for base, copies in plan:
        for copy in copies:
            copy.wait()
        for buffer, output in zip(held, outputs):
            place = pl.ds(base, rows)
            stores.append(
                pltpu.make_async_copy(
                    buffer.at[place, :], output.at[place, :], left_here.at[len(stores)]
                )
            )
            stores[-1].start()
    for store in stores:
        store.wait()


def assemble(index, here, there, depth, part, middle, widths):
    rows = here[0].shape[0] * 2 * depth
    total = sum(widths) * rows
    count = 2 * (1 + 5 * (depth - 1)) * len(widths)
    return pl.pallas_call(
        functools.partial(assemble_kernel, depth, part, middle, widths),
        out_shape=[jax.ShapeDtypeStruct((rows, width), jnp.bfloat16) for width in widths],
        in_specs=[pl.BlockSpec(memory_space=pltpu.SMEM)] + [pl.BlockSpec(memory_space=pl.ANY)] * 12,
        out_specs=[pl.BlockSpec(memory_space=pl.ANY)] * len(widths),
        scratch_shapes=[pltpu.VMEM((rows, width), jnp.bfloat16) for width in widths]
        + [
            pltpu.SemaphoreType.DMA((count,)),
            pltpu.SemaphoreType.DMA((2 * depth * len(widths),)),
        ],
        compiler_params=pltpu.CompilerParams(vmem_limit_bytes=2 * total + (8 << 20)),
        cost_estimate=pl.CostEstimate(flops=0, bytes_accessed=0, transcendentals=0),
        name="assemble",
    )(index, *here, *there)


def body(
    groups,
    shards,
    tokens,
    lengths,
    group_live,
    w_query,
    w_key,
    w_value,
    w_out,
    w_gate,
    w_up,
    w_down,
    g_attn,
    g_query,
    g_key,
    g_ffn,
    cotangent,
):
    links = Links(groups, shards)
    shard_rows = w_query.shape[0]
    width = HD * (H + 2 * KV)

    def column(values):
        return jnp.pad(values, (0, shard_rows - values.shape[0]))[:, None]

    gains = jnp.concatenate([column(g) for g in (g_attn, g_ffn, g_query, g_key)], axis=1)
    gains = jnp.pad(gains, ((0, 0), (0, 124)))
    packed = jnp.concatenate([w_query, w_key, w_value, w_out, gains], axis=1)
    first_move = links.gather_of(packed, (width, w_out.shape[1], 128))
    gate_move = links.gather_of(w_gate, (w_gate.shape[1],))
    up_move = links.gather_of(w_up, (w_up.shape[1],))
    down_move = links.gather_of(w_down, (w_down.shape[1],))
    for _ in range(3):
        advance([first_move])
    for _ in range(3):
        advance([first_move, gate_move])
    full_qkv, full_out, full_gains = first_move.result()
    full_qkv = advance([gate_move], full_qkv)
    full_qkv = advance([up_move], full_qkv)
    head_rows = g_query.shape[0]
    all_gains = full_gains[:, :4].astype(jnp.float32)
    gain_attn = all_gains[:, 0]
    gain_ffn = all_gains[:, 1]
    gain_query = all_gains[:, 2].reshape(shards, shard_rows)[:, :head_rows].reshape(HD)
    gain_key = all_gains[:, 3].reshape(shards, shard_rows)[:, :head_rows].reshape(HD)

    row_count = tokens.shape[0]
    x_float = tokens.astype(jnp.float32)
    row_index, segment, position, keep_mask = layout(lengths[0], group_live[0], row_count)
    allowed = (segment[:, None] == segment[None, :]) & (row_index[None, :] <= row_index[:, None])
    bias = jnp.where(allowed, 0.0, masked_score).astype(jnp.float32)
    gain_rows = jnp.stack([jnp.tile(gain_query, 2), jnp.tile(gain_key, 2)])
    tables = (*rotary_tables(position), jnp.pad(gain_rows, ((0, 6), (0, 0))), bias)
    unit_one, inverse_one = normalize(x_float)
    attn_input = (unit_one * gain_attn).astype(jnp.bfloat16)
    qkv = jnp.dot(attn_input, full_qkv, preferred_element_type=jnp.float32)
    parts, logs = [], []
    for first in range(KV // 2):
        part, log = attend(qkv, tables, first, 1)
        if first == 0:
            qkv, part = advance([up_move], qkv, part)
        if first == 1:
            qkv, part = advance([gate_move], qkv, part)
        if first == 2:
            qkv, part = advance([up_move], qkv, part)
        if first == 3:
            part = advance([gate_move], part)
            part = advance([up_move], part)
            part = advance([down_move], part)
        parts.append(part)
        logs.append(log)
    attended = jnp.concatenate(parts, axis=1)
    hidden = x_float + keep_mask[:, None] * jnp.dot(
        attended, full_out, preferred_element_type=jnp.float32
    )
    unit_two, inverse_two = normalize(hidden)
    ffn_input = (unit_two * gain_ffn).astype(jnp.bfloat16)
    (full_gate,) = gate_move.result()
    full_gate = advance([down_move], full_gate)
    gate_proj = jnp.dot(ffn_input, full_gate, preferred_element_type=jnp.float32)
    gate_proj = advance([down_move], gate_proj)
    gate_proj = advance([up_move], gate_proj)
    gate_proj = advance([up_move], gate_proj)
    gate_proj = advance([down_move], gate_proj)
    (full_up,) = up_move.result()
    up_proj = jnp.dot(ffn_input, full_up, preferred_element_type=jnp.float32)
    inner_low = (jax.nn.silu(gate_proj) * up_proj).astype(jnp.bfloat16)
    inner_low = advance([down_move], inner_low)

    d_final = cotangent.astype(jnp.float32)
    d_ffn = (keep_mask[:, None] * d_final).astype(jnp.bfloat16)
    down_sum = links.sum_of([(inner_low, d_ffn)])
    d_ffn, down_sum.held = advance([down_move], d_ffn, down_sum.held)
    (full_down,) = down_move.result()
    full_down = advance([down_sum], full_down)
    d_gate, d_up = inner_back(d_ffn, full_down, gate_proj, up_proj)
    d_gate, d_up = advance([down_sum], d_gate, d_up)
    gate_sum = links.sum_of([(ffn_input, d_gate)], depth_first=True)
    d_gate, d_up = advance([gate_sum], d_gate, d_up)
    up_sum = links.sum_of([(ffn_input, d_up)])
    d_gate, d_up = advance([up_sum], d_gate, d_up)
    d_gate, d_up = advance([gate_sum], d_gate, d_up)
    d_ffn_input = ffn_back(d_gate, d_up, full_gate, full_up)
    d_hidden_norm, grad_gain_ffn = norm_back(d_ffn_input, unit_two, inverse_two, gain_ffn)
    d_hidden = d_final + d_hidden_norm
    d_attn = (keep_mask[:, None] * d_hidden).astype(jnp.bfloat16)
    d_attn = advance([down_sum], d_attn)
    d_attn = advance([up_sum], d_attn)
    d_attended = back_low(d_attn, full_out)
    plans = ([gate_sum], [down_sum], [up_sum], [gate_sum, down_sum])
    gain_sums, outputs = 0.0, ()
    for first in range(KV // 2):
        *outputs, gain_sum = attend_back(qkv, tables, logs[first], d_attended, first, 1, outputs)
        if plans[first]:
            d_attended, *outputs = advance(plans[first], d_attended, *outputs)
        gain_sums = gain_sums + gain_sum
    d_query, d_key, d_value = outputs
    grad_gain_query = gain_sums[0, :HD] + gain_sums[0, HD:]
    grad_gain_key = gain_sums[1, :HD] + gain_sums[1, HD:]
    d_attn_input = (
        back_product(d_query, full_qkv[:, : H * HD])
        + back_product(d_key, full_qkv[:, H * HD : (H + KV) * HD])
        + back_product(d_value, full_qkv[:, (H + KV) * HD :])
    )
    d_x_norm, grad_gain_attn = norm_back(d_attn_input, unit_one, inverse_one, gain_attn)
    grad_tokens = (d_hidden + d_x_norm).astype(jnp.bfloat16)

    def spread(values):
        blocks = jnp.pad(
            values.reshape(shards, head_rows), ((0, 0), (0, shard_rows - head_rows))
        )
        return blocks.reshape(shards * shard_rows)

    gain_grads = jnp.stack(
        [grad_gain_attn, grad_gain_ffn, spread(grad_gain_query), spread(grad_gain_key)], axis=1
    )
    gain_grads = jnp.pad(gain_grads, ((0, 0), (0, 252))).astype(jnp.bfloat16)
    gain_grads = settle([up_sum], gain_grads)
    qkv_sum = links.sum_of(
        [(attn_input, value) for value in (d_query, d_key, d_value)] + [(attended, d_attn)],
        gain_grads,
    )
    for plan in ([qkv_sum], [up_sum], [qkv_sum]):
        inner_low = advance(plan, inner_low)
    block_out = ffn_out(inner_low, full_down, hidden, keep_mask[:, None])
    plans = (
        [up_sum],
        [down_sum],
        [gate_sum],
        [qkv_sum],
        [up_sum],
        [down_sum],
        [gate_sum],
        [qkv_sum],
        [up_sum],
        [gate_sum],
        [qkv_sum, down_sum],
        [up_sum, gate_sum],
        [qkv_sum],
        [qkv_sum],
        [qkv_sum],
    )
    for plan in plans:
        block_out = advance(plan, block_out)
    owned = qkv_sum.result()
    grad_down, grad_gate, grad_up = down_sum.result(), gate_sum.result(), up_sum.result()
    last = width + w_out.shape[1]
    return (
        block_out,
        grad_tokens,
        owned[:, : H * HD],
        owned[:, H * HD : (H + KV) * HD],
        owned[:, (H + KV) * HD : width],
        owned[:, width : width + w_out.shape[1]],
        grad_gate,
        grad_up,
        grad_down,
        owned[:, last],
        owned[:head_rows, last + 2],
        owned[:head_rows, last + 3],
        owned[:, last + 1],
    )


def solution(mesh):
    in_specs = (
        P(("rep", "shard"), None),
        P(("rep", "shard"), None),
        P("rep"),
        P("shard", None),
        P("shard", None),
        P("shard", None),
        P("shard", None),
        P("shard", None),
        P("shard", None),
        P("shard", None),
        P("shard"),
        P("shard"),
        P("shard"),
        P("shard"),
        P(("rep", "shard"), None),
    )
    out_specs = (
        P(("rep", "shard"), None),
        P(("rep", "shard"), None),
        P("shard", None),
        P("shard", None),
        P("shard", None),
        P("shard", None),
        P("shard", None),
        P("shard", None),
        P("shard", None),
        P("shard"),
        P("shard"),
        P("shard"),
        P("shard"),
    )
    return jax.shard_map(
        functools.partial(body, mesh.shape["rep"], mesh.shape["shard"]),
        mesh=mesh,
        in_specs=in_specs,
        out_specs=out_specs,
        check_vma=False,
    )
```

```python
import functools

import jax
import jax.numpy as jnp
from jax import lax
from jax.experimental import pallas as pl
from jax.experimental.pallas import tpu as pltpu
from jax.sharding import PartitionSpec as P

H = 16
KV = 8
HD = 64


epsilon = 1e-05
theta_base = 1000000.0
masked_score = -1e30


def layout(seq_lengths, live_rows, row_count):
    row_index = jnp.arange(row_count, dtype=jnp.int32)
    seq_ends = jnp.cumsum(seq_lengths)
    passed_ends = row_index[:, None] >= seq_ends[None, :]
    segment = jnp.sum(passed_ends.astype(jnp.int32), axis=1, dtype=jnp.int32)
    begins = jnp.sum(jnp.where(passed_ends, seq_lengths[None, :], 0), axis=1, dtype=jnp.int32)
    live_mask = row_index < live_rows
    segment = jnp.where(live_mask, segment, -1)
    position = (row_index - begins).astype(jnp.float32)
    return (row_index, segment, position, live_mask.astype(jnp.float32))


def rotary_tables(position):
    half_width = HD // 2
    frequency = theta_base ** (-2.0 * jnp.arange(half_width, dtype=jnp.float32) / HD)
    angles = position[:, None] * frequency[None, :]
    cosine, sine = jnp.cos(angles), jnp.sin(angles)
    return (
        jnp.concatenate([cosine] * 4, axis=1),
        jnp.concatenate([-sine, sine, -sine, sine], axis=1),
    )


def normalize(values):
    inverse_rms = lax.rsqrt(jnp.mean(values * values, axis=-1, keepdims=True) + epsilon)
    return (values * inverse_rms, inverse_rms)


def norm_back(incoming, unit_values, inverse_rms, gain):
    grad_unit = incoming * gain
    grad_values = inverse_rms * (
        grad_unit - unit_values * jnp.mean(unit_values * grad_unit, axis=-1, keepdims=True)
    )
    grad_gain = jnp.sum((incoming * unit_values).reshape(-1, unit_values.shape[-1]), axis=0)
    return (grad_values, grad_gain)


def rows_product(left, right):
    return lax.dot_general(
        left, right, (((0,), (0,)), ((), ())), preferred_element_type=jnp.float32
    )


def back_product(left, right):
    return lax.dot_general(
        left, right, (((1,), (1,)), ((), ())), preferred_element_type=jnp.float32
    )


def lane_index(shape):
    return lax.broadcasted_iota(jnp.int32, shape, len(shape) - 1)


def head_mean(values):
    first = lane_index(values.shape) < HD
    low = jnp.sum(jnp.where(first, values, 0.0), axis=-1, keepdims=True)
    high = jnp.sum(jnp.where(first, 0.0, values), axis=-1, keepdims=True)
    return jnp.where(first, low, high) * (1.0 / HD)


def swap_halves(values):
    front = lane_index(values.shape) % HD < HD // 2
    return jnp.where(
        front, pltpu.roll(values, 2 * HD - HD // 2, 1), pltpu.roll(values, HD // 2, 1)
    )


def head_unit(raw):
    inverse = lax.rsqrt(head_mean(raw * raw) + epsilon)
    return raw * inverse, inverse


def head_norm_back(incoming, unit_values, inverse, gain):
    grad_unit = incoming * gain
    return inverse * (grad_unit - unit_values * head_mean(unit_values * grad_unit))


def pair_of(values, which):
    first = lane_index(values.shape) < HD
    kept = jnp.where(first, values, 0.0) if which == 0 else jnp.where(first, 0.0, values)
    moved = pltpu.roll(kept, HD, 1)
    pair = (kept, moved) if which == 0 else (moved, kept)
    return tuple(value.astype(jnp.bfloat16) for value in pair)


def dot_rows(left, right):
    return lax.dot_general(
        left, right, (((0,), (0,)), ((), ())), preferred_element_type=jnp.float32
    )


def dot_back(left, right):
    return lax.dot_general(
        left, right, (((1,), (1,)), ((), ())), preferred_element_type=jnp.float32
    )


def dot_plain(left, right):
    return lax.dot_general(
        left, right, (((1,), (0,)), ((), ())), preferred_element_type=jnp.float32
    )


def attend_kernel(block, q_ref, k_ref, v_ref, cos_ref, sin_ref, gain_ref, bias_ref, out_ref, log_ref):
    rows = q_ref.shape[0]
    tile = 2 * HD
    cosine, sine = cos_ref[...], sin_ref[...]
    first = lane_index((block, tile)) < HD

    def turned(raw, gain):
        unit_values, _ = head_unit(raw)
        scaled = unit_values * gain
        return cosine * scaled + sine * swap_halves(scaled)

    k_turned = turned(k_ref[...], gain_ref[1:2, :])
    v_values = v_ref[...]
    for which in range(2):
        lanes = slice(which * tile, (which + 1) * tile)
        query = (turned(q_ref[:, lanes], gain_ref[0:1, :]).astype(jnp.bfloat16)) * HD ** (-0.5)
        query = query.astype(jnp.bfloat16)
        keys = pair_of(k_turned, which)
        values = pair_of(v_values, which)
        for start in range(0, rows, block):
            stop = start + block
            bias = bias_ref[start:stop, :stop]
            result = jnp.zeros((block, tile), jnp.float32)
            logs = []
            for head in range(2):
                scores = dot_back(query[start:stop], keys[head][:stop]) + bias
                top = jnp.max(scores, axis=-1, keepdims=True)
                weights = jnp.exp(scores - top)
                totals = jnp.sum(weights, axis=-1, keepdims=True)
                low = (weights * (1.0 / totals)).astype(jnp.bfloat16)
                result += dot_plain(low, values[head][:stop])
                logs.append(top + jnp.log(totals))
            out_ref[start:stop, lanes] = result.astype(jnp.bfloat16)
            log_ref[start:stop, lanes] = jnp.where(first, logs[0], logs[1])


def attend_back_kernel(
    block,
    q_ref,
    k_ref,
    v_ref,
    cos_ref,
    sin_ref,
    gain_ref,
    bias_ref,
    log_ref,
    grad_ref,
    *refs,
):
    rows = q_ref.shape[0]
    tile = 2 * HD
    cosine, sine = cos_ref[...], sin_ref[...]
    dq_ref, dk_ref, dv_ref, gain_grad_ref, key_sum, value_sum = refs[-6:]
    query_gain, key_gain = gain_ref[0:1, :], gain_ref[1:2, :]
    first = lane_index((rows, tile)) < HD
    scale = HD ** (-0.5)

    @pl.when(pl.program_id(0) == 0)
    def _():
        gain_grad_ref[...] = jnp.zeros_like(gain_grad_ref)

    def turned(scaled):
        return cosine * scaled + sine * swap_halves(scaled)

    def back(incoming, unit_values, inverse, gain, row):
        flat = cosine * incoming - sine * swap_halves(incoming)
        gain_grad_ref[row:row + 1, :] += jnp.sum(flat * unit_values, axis=0, keepdims=True)
        return head_norm_back(flat, unit_values, inverse, gain).astype(jnp.bfloat16)

    k_unit, k_inverse = head_unit(k_ref[...])
    k_turned = turned(k_unit * key_gain)
    v_values = v_ref[...]
    key_parts, value_parts = [], []
    for which in range(2):
        lanes = slice(which * tile, (which + 1) * tile)
        q_unit, q_inverse = head_unit(q_ref[:, lanes])
        query = (turned(q_unit * query_gain)).astype(jnp.bfloat16)
        query = (query * scale).astype(jnp.bfloat16)
        keys = pair_of(k_turned, which)
        values = pair_of(v_values, which)
        key_sum[...] = jnp.zeros_like(key_sum)
        value_sum[...] = jnp.zeros_like(value_sum)
        d_query = []
        for start in range(0, rows, block):
            stop = start + block
            bias = bias_ref[start:stop, :stop]
            grad = grad_ref[start:stop, lanes]
            part = jnp.zeros((block, tile), jnp.float32)
            for head in range(2):
                column = which * tile + head * HD
                logs = log_ref[start:stop, column:column + 1]
                scores = dot_back(query[start:stop], keys[head][:stop]) + bias
                probability = jnp.exp(scores - logs)
                grad_prob = dot_back(grad, values[head][:stop])
                terms = jnp.sum(probability * grad_prob, axis=-1, keepdims=True)
                grad_scores = (probability * (grad_prob - terms)).astype(jnp.bfloat16)
                part += dot_plain(grad_scores, keys[head][:stop])
                key_sum[head, :stop, :] += dot_rows(grad_scores, query[start:stop])
                value_sum[head, :stop, :] += dot_rows(probability.astype(jnp.bfloat16), grad)
            d_query.append(part * scale)
        dq_ref[:, lanes] = back(
            jnp.concatenate(d_query, axis=0), q_unit, q_inverse, query_gain, 0
        )
        for total, parts in ((key_sum, key_parts), (value_sum, value_parts)):
            joined = jnp.where(first, total[0], total[1])
            parts.append(joined + pltpu.roll(joined, HD, 1))
    d_key = jnp.where(first, key_parts[0], key_parts[1])
    dk_ref[...] = back(d_key, k_unit, k_inverse, key_gain, 1)
    dv_ref[...] = jnp.where(first, value_parts[0], value_parts[1]).astype(jnp.bfloat16)


def attention_specs(rows, first=0):
    tile = 2 * HD
    fixed = lambda i: (0, 0)
    return [
        pl.BlockSpec((rows, 2 * tile), lambda i: (0, first + i)),
        pl.BlockSpec((rows, tile), lambda i: (0, H // 2 + first + i)),
        pl.BlockSpec((rows, tile), lambda i: (0, H // 2 + KV // 2 + first + i)),
        pl.BlockSpec((rows, tile), fixed),
        pl.BlockSpec((rows, tile), fixed),
        pl.BlockSpec((8, tile), fixed),
        pl.BlockSpec((rows, rows), fixed),
    ]


def attend(qkv, tables, first, count):
    rows = qkv.shape[0]
    wide = pl.BlockSpec((rows, 4 * HD), lambda i: (0, i))
    return pl.pallas_call(
        functools.partial(attend_kernel, rows // 2),
        grid=(count,),
        out_shape=[
            jax.ShapeDtypeStruct((rows, 4 * HD * count), jnp.bfloat16),
            jax.ShapeDtypeStruct((rows, 4 * HD * count), jnp.float32),
        ],
        in_specs=attention_specs(rows, first),
        out_specs=[wide, wide],
        compiler_params=pltpu.CompilerParams(vmem_limit_bytes=48 << 20),
        cost_estimate=pl.CostEstimate(flops=0, bytes_accessed=0, transcendentals=0),
        name="attend",
    )(qkv, qkv, qkv, *tables)


def attend_back(qkv, tables, logs, grad, first, count, before=()):
    rows = qkv.shape[0]
    tile = 2 * HD
    wide = pl.BlockSpec((rows, 2 * tile), lambda i: (0, i))
    taken = pl.BlockSpec((rows, 2 * tile), lambda i: (0, first + i))
    narrow = pl.BlockSpec((rows, tile), lambda i: (0, first + i))
    specs = attention_specs(rows, first) + [wide, taken]
    return pl.pallas_call(
        functools.partial(attend_back_kernel, rows // 2),
        grid=(count,),
        out_shape=[
            jax.ShapeDtypeStruct((rows, H * HD), jnp.bfloat16),
            jax.ShapeDtypeStruct((rows, KV * HD), jnp.bfloat16),
            jax.ShapeDtypeStruct((rows, KV * HD), jnp.bfloat16),
            jax.ShapeDtypeStruct((8, tile), jnp.float32),
        ],
        in_specs=specs + [pl.BlockSpec(memory_space=pl.ANY)] * len(before),
        input_output_aliases={len(specs) + i: i for i in range(len(before))},
        out_specs=[taken, narrow, narrow, pl.BlockSpec((8, tile), lambda i: (0, 0))],
        scratch_shapes=[
            pltpu.VMEM((2, rows, tile), jnp.float32),
            pltpu.VMEM((2, rows, tile), jnp.float32),
        ],
        compiler_params=pltpu.CompilerParams(vmem_limit_bytes=48 << 20),
        cost_estimate=pl.CostEstimate(flops=0, bytes_accessed=0, transcendentals=0),
        name="attend_back",
    )(qkv, qkv, qkv, *tables, logs, grad, *before)


def inner_back_kernel(d_ref, down_ref, gate_ref, up_ref, d_gate_ref, d_up_ref):
    d_inner = dot_back(d_ref[...], down_ref[...])
    gate = gate_ref[...]
    sigmoid = jax.nn.sigmoid(gate)
    d_gate = d_inner * up_ref[...] * sigmoid * (1.0 + gate * (1.0 - sigmoid))
    d_gate_ref[...] = d_gate.astype(jnp.bfloat16)
    d_up_ref[...] = (d_inner * gate * sigmoid).astype(jnp.bfloat16)


def inner_back(d_ffn, full_down, gate_proj, up_proj):
    (rows, width), units = d_ffn.shape, full_down.shape[0]
    tile = 512
    columns = pl.BlockSpec((rows, tile), lambda i: (0, i))
    shape = jax.ShapeDtypeStruct((rows, units), jnp.bfloat16)
    return pl.pallas_call(
        inner_back_kernel,
        grid=(units // tile,),
        out_shape=[shape, shape],
        in_specs=[
            pl.BlockSpec((rows, width), lambda i: (0, 0)),
            pl.BlockSpec((tile, width), lambda i: (i, 0)),
            columns,
            columns,
        ],
        out_specs=[columns, columns],
        compiler_params=pltpu.CompilerParams(vmem_limit_bytes=48 << 20),
        cost_estimate=pl.CostEstimate(flops=0, bytes_accessed=0, transcendentals=0),
        name="inner_back",
    )(d_ffn, full_down, gate_proj, up_proj)


def ffn_out_kernel(inner_ref, down_ref, hidden_ref, keep_ref, out_ref, total):
    step = pl.program_id(0)
    part = dot_plain(inner_ref[...], down_ref[...])

    @pl.when(step == 0)
    def _():
        total[...] = part

    @pl.when(step > 0)
    def _():
        total[...] += part

    @pl.when(step == pl.num_programs(0) - 1)
    def _():
        out_ref[...] = (hidden_ref[...] + keep_ref[...] * total[...]).astype(jnp.bfloat16)


def ffn_out(inner_low, full_down, hidden, keep_column):
    (rows, units), width = inner_low.shape, full_down.shape[1]
    tile = 512
    fixed = lambda i: (0, 0)
    return pl.pallas_call(
        ffn_out_kernel,
        grid=(units // tile,),
        out_shape=jax.ShapeDtypeStruct((rows, width), jnp.bfloat16),
        in_specs=[
            pl.BlockSpec((rows, tile), lambda i: (0, i)),
            pl.BlockSpec((tile, width), lambda i: (i, 0)),
            pl.BlockSpec((rows, width), fixed),
            pl.BlockSpec((rows, 1), fixed),
        ],
        out_specs=pl.BlockSpec((rows, width), fixed),
        scratch_shapes=[pltpu.VMEM((rows, width), jnp.float32)],
        compiler_params=pltpu.CompilerParams(vmem_limit_bytes=48 << 20),
        cost_estimate=pl.CostEstimate(flops=0, bytes_accessed=0, transcendentals=0),
        name="ffn_out",
    )(inner_low, full_down, hidden, keep_column)


def ffn_back_kernel(d_gate_ref, d_up_ref, gate_ref, up_ref, out_ref):
    part = dot_back(d_gate_ref[...], gate_ref[...]) + dot_back(d_up_ref[...], up_ref[...])

    @pl.when(pl.program_id(0) == 0)
    def _():
        out_ref[...] = part

    @pl.when(pl.program_id(0) > 0)
    def _():
        out_ref[...] += part


def ffn_back(d_gate, d_up, full_gate, full_up):
    (rows, units), width = d_gate.shape, full_gate.shape[0]
    tile = 512
    left = pl.BlockSpec((rows, tile), lambda i: (0, i))
    right = pl.BlockSpec((width, tile), lambda i: (0, i))
    return pl.pallas_call(
        ffn_back_kernel,
        grid=(units // tile,),
        out_shape=jax.ShapeDtypeStruct((rows, width), jnp.float32),
        in_specs=[left, left, right, right],
        out_specs=pl.BlockSpec((rows, width), lambda i: (0, 0)),
        compiler_params=pltpu.CompilerParams(vmem_limit_bytes=48 << 20),
        cost_estimate=pl.CostEstimate(flops=0, bytes_accessed=0, transcendentals=0),
        name="ffn_back",
    )(d_gate, d_up, full_gate, full_up)


class Links:
    def __init__(self, groups, shards):
        self.groups = groups
        self.shards = shards
        self.depth = shards // 2
        rep = lax.axis_index("rep")
        shard = lax.axis_index("shard")
        self.rep = rep
        self.z = shard // 2
        self.core = shard % 2
        self.index = jnp.stack([rep, self.z, self.core]).astype(jnp.int32)

    def across_core(self, value):
        return lax.ppermute(value, "shard", [(s, s ^ 1) for s in range(self.shards)])

    def across_x(self, value):
        return lax.ppermute(value, "rep", [(r, r ^ 1) for r in range(self.groups)])

    def across_y(self, value):
        return lax.ppermute(value, "rep", [(r, r ^ 2) for r in range(self.groups)])

    def along_z(self, value):
        pairs = [(s, (s + 2) % self.shards) for s in range(self.shards)]
        return lax.ppermute(value, "shard", pairs)

    def fits(self, rows):
        return self.groups == 4 and self.shards % 2 == 0 and rows % 64 == 0

    def gather_of(self, shard, widths):
        kind = Gather if self.fits(shard.shape[0]) else PlainGather
        return kind(self, shard, widths)

    def sum_of(self, pairs, extra=None, depth_first=False):
        kind = Sum if self.fits(pairs[0][0].shape[1] // self.shards) else PlainSum
        return kind(self, pairs, extra, depth_first)


def add(*values):
    return functools.reduce(jnp.add, [value.astype(jnp.float32) for value in values])


def advance(moves, *others):
    states = [(move.held, move.flying) for move in moves]
    states, others = lax.optimization_barrier((states, others))
    sends = []
    for move, (held, flying) in zip(moves, states):
        move.held, move.flying = held, flying
        move.held, move.sends = next(move.work)
        sends.append([value for _, value in move.sends])
    sends, others = lax.optimization_barrier((sends, others))
    for move, values in zip(moves, sends):
        move.flying = tuple(link(value) for (link, _), value in zip(move.sends, values))
    return others[0] if len(others) == 1 else others


def settle(moves, *others):
    states = [(move.held, move.flying) for move in moves]
    states, others = lax.optimization_barrier((states, others))
    for move, (held, flying) in zip(moves, states):
        move.held, move.flying = held, flying
    return others[0] if len(others) == 1 else others


class Moves:
    held = ()
    flying = ()

    def still(self):
        while True:
            yield (), ()

    def finish(self):
        for self.held, sends in self.work:
            self.flying = tuple(link(value) for link, value in sends)


class PlainGather(Moves):
    def __init__(self, links, shard, widths):
        self.shard, self.widths = shard, widths
        self.work = self.still()

    def result(self):
        whole = lax.all_gather(self.shard, "shard", axis=0, tiled=True)
        cuts = [sum(self.widths[:i]) for i in range(1, len(self.widths))]
        return jnp.split(whole, cuts, axis=1)


class PlainSum(Moves):
    def __init__(self, links, pairs, extra, depth_first):
        parts = [rows_product(left, right).astype(jnp.bfloat16) for left, right in pairs]
        self.low = jnp.concatenate(parts + ([] if extra is None else [extra]), axis=1)
        self.work = self.still()

    def result(self):
        owned = lax.psum_scatter(self.low, "shard", scatter_dimension=0, tiled=True)
        return lax.psum(owned, "rep").astype(jnp.float32)


class Gather(Moves):
    def __init__(self, links, shard, widths):
        self.links, self.shard, self.widths = links, shard, widths
        rows, self.columns = shard.shape
        self.part = rows // links.groups
        self.middle = self.columns // 256 * 128
        self.held = (lax.dynamic_slice_in_dim(shard, links.rep * self.part, self.part, axis=0),)
        self.work = self.stages()

    def stages(self):
        links, middle = self.links, self.middle
        moving, pieces = self.held[0], ()
        for step in range(links.depth - 1):
            moves = ((links.along_z, moving),)
            if step == 0:
                moves += ((links.across_core, self.shard),)
            yield pieces, moves
            moving = self.flying[0]
            pieces = self.held + self.flying
        first, other, *rest = pieces
        mine = jnp.concatenate([first, *rest], axis=0)
        yield (mine, other), (
            (links.across_x, mine),
            (links.across_y, mine),
            (links.across_core, mine),
        )
        from_x, from_y, _ = self.flying
        yield self.held + self.flying, (
            (links.across_y, from_x[:, :middle]),
            (links.across_x, from_y[:, middle:]),
            (links.across_core, from_x),
            (links.across_core, from_y),
        )
        yield self.held + self.flying, (
            (links.across_core, self.flying[0]),
            (links.across_core, self.flying[1]),
        )

    def result(self):
        self.finish()
        mine, other, from_x, from_y, mine_core, left, right, x_core, y_core = self.held
        here = (self.shard, mine, from_x, from_y, left, right)
        there = (other, mine_core, x_core, y_core, *self.flying)
        links = self.links
        return assemble(
            links.index, here, there, links.depth, self.part, self.middle, self.widths
        )


class Sum(Moves):
    def __init__(self, links, pairs, extra, depth_first):
        self.links = links
        self.part = pairs[0][0].shape[1] // links.shards // links.groups
        self.held = product(links.index, pairs, extra, links.depth)
        self.work = self.stages(depth_first)

    def result(self):
        self.finish()
        return place(self.links.index, self.flying + self.held, self.part)

    def stages(self, depth_first):
        links, part = self.links, self.part
        yield (self.held[1],), ((links.across_core, self.held[0]),)
        pair = self.held + self.flying
        if depth_first:
            yield from self.along(pair, links.groups * part)
            yield from self.across((self.held[0], self.flying[0]), 1)
            own, left, right = self.held + self.flying
            mine = jnp.concatenate(
                [add(own[:, : left.shape[1]], left), add(own[:, left.shape[1] :], right)], axis=1
            )
        else:
            yield from self.across(pair, links.depth)
            yield from self.along(self.held + self.flying, part)
            mine = add(self.held[0], self.flying[0])
        mine = mine.astype(jnp.bfloat16)
        middle = mine.shape[1] // 2
        yield (mine,), ((links.across_x, mine), (links.across_y, mine))
        from_x, from_y = self.flying
        yield self.held + (from_x, from_y), (
            (links.across_y, from_x[:, :middle]),
            (links.across_x, from_y[:, middle:]),
        )

    def across(self, pair, depth):
        links, part = self.links, self.part
        left, right = sum_first(links.index, pair, part, depth)
        yield pair, ((links.across_x, left), (links.across_y, right))
        left, right, own = sum_second(links.index, self.held, self.flying, part, depth)
        yield (own,), ((links.across_y, left), (links.across_x, right))

    def along(self, values, rows):
        links = self.links
        moving, *terms = ring_terms(links.index, values, rows, links.depth)
        yield tuple(terms), ((links.along_z, moving),)
        for _ in range(links.depth - 2):
            moving = add(self.held[0], self.flying[0]).astype(jnp.bfloat16)
            yield self.held[1:], ((links.along_z, moving),)


def sum_first_kernel(index_ref, *refs):
    keep, received = refs[0:3], refs[3:6]
    left_ref, right_ref = refs[6:]

    def total(place):
        return keep[place][...].astype(jnp.float32) + received[place][...].astype(jnp.float32)

    both = total(2).astype(jnp.bfloat16)
    middle = left_ref.shape[2]
    left_ref[0] = total(0).astype(jnp.bfloat16)
    left_ref[1] = both[:, :middle]
    right_ref[0] = total(1).astype(jnp.bfloat16)
    right_ref[1] = both[:, middle:]


def sum_first(index, pair, part, depth):
    columns = pair[0].shape[1]
    middle = columns // 2
    specs = [
        pl.BlockSpec((part, middle), lambda i, index: (4 * i + (index[0] ^ 1), 0)),
        pl.BlockSpec((part, middle), lambda i, index: (4 * i + (index[0] ^ 2), 1)),
        pl.BlockSpec((part, columns), lambda i, index: (4 * i + (index[0] ^ 3), 0)),
    ]
    half = pl.BlockSpec((2, part, middle), lambda i, index: (0, i, 0))
    shape = jax.ShapeDtypeStruct((2, depth * part, middle), jnp.bfloat16)
    return pl.pallas_call(
        sum_first_kernel,
        grid_spec=pltpu.PrefetchScalarGridSpec(
            num_scalar_prefetch=1, grid=(depth,), in_specs=specs * 2, out_specs=[half, half]
        ),
        out_shape=[shape, shape],
        compiler_params=pltpu.CompilerParams(vmem_limit_bytes=48 << 20),
        cost_estimate=pl.CostEstimate(flops=0, bytes_accessed=0, transcendentals=0),
        name="sum_first",
    )(index, *([pair[0]] * 3 + [pair[1]] * 3))


def sum_second_kernel(index_ref, *refs):
    keep, received = refs[0:3], refs[3:6]
    from_left, from_right, left_ref, right_ref, own_ref = refs[6:]
    middle = left_ref.shape[1]

    def total(place):
        return keep[place][...].astype(jnp.float32) + received[place][...].astype(jnp.float32)

    left_ref[...] = (total(0) + from_left[1].astype(jnp.float32)).astype(jnp.bfloat16)
    right_ref[...] = (total(1) + from_right[1].astype(jnp.float32)).astype(jnp.bfloat16)
    own = total(2)
    own_ref[:, :middle] = (own[:, :middle] + from_left[0].astype(jnp.float32)).astype(jnp.bfloat16)
    own_ref[:, middle:] = (own[:, middle:] + from_right[0].astype(jnp.float32)).astype(jnp.bfloat16)


def sum_second(index, pair, arrived, part, depth):
    columns = pair[0].shape[1]
    middle = columns // 2
    specs = [
        pl.BlockSpec((part, middle), lambda i, index: (4 * i + (index[0] ^ 2), 0)),
        pl.BlockSpec((part, middle), lambda i, index: (4 * i + (index[0] ^ 1), 1)),
        pl.BlockSpec((part, columns), lambda i, index: (4 * i + index[0], 0)),
    ]
    two = pl.BlockSpec((2, part, middle), lambda i, index: (0, i, 0))
    half = pl.BlockSpec((part, middle), lambda i, index: (i, 0))
    shape = jax.ShapeDtypeStruct((depth * part, middle), jnp.bfloat16)
    return pl.pallas_call(
        sum_second_kernel,
        grid_spec=pltpu.PrefetchScalarGridSpec(
            num_scalar_prefetch=1,
            grid=(depth,),
            in_specs=specs * 2 + [two, two],
            out_specs=[half, half, pl.BlockSpec((part, columns), lambda i, index: (i, 0))],
        ),
        out_shape=[shape, shape, jax.ShapeDtypeStruct((depth * part, columns), jnp.bfloat16)],
        compiler_params=pltpu.CompilerParams(vmem_limit_bytes=48 << 20),
        cost_estimate=pl.CostEstimate(flops=0, bytes_accessed=0, transcendentals=0),
        name="sum_second",
    )(index, *([pair[0]] * 3 + [pair[1]] * 3), *arrived)


def ring_terms_kernel(depth, index_ref, own_ref, *refs):
    others, outputs = refs[:-depth], refs[-depth:]
    own = own_ref[...].astype(jnp.float32)
    rest = [other[...].astype(jnp.float32) for other in others]
    total = own + (rest[0] if len(rest) == 1 else jnp.concatenate(rest, axis=1))
    for step in range(depth):

        @pl.when(pl.program_id(0) == step)
        def _(step=step):
            outputs[step][...] = total.astype(jnp.bfloat16)


def ring_terms(index, values, rows, depth):
    columns = values[0].shape[1]
    at = lambda i, index: (lax.rem(index[1] + 2 * depth - 1 - i, depth), 0)
    shape = jax.ShapeDtypeStruct((rows, columns), jnp.bfloat16)
    return pl.pallas_call(
        functools.partial(ring_terms_kernel, depth),
        grid_spec=pltpu.PrefetchScalarGridSpec(
            num_scalar_prefetch=1,
            grid=(depth,),
            in_specs=[pl.BlockSpec((rows, value.shape[1]), at) for value in values],
            out_specs=[pl.BlockSpec((rows, columns), lambda i, index: (0, 0))] * depth,
        ),
        out_shape=[shape] * depth,
        compiler_params=pltpu.CompilerParams(vmem_limit_bytes=48 << 20),
        cost_estimate=pl.CostEstimate(flops=0, bytes_accessed=0, transcendentals=0),
        name="ring_terms",
    )(index, *values)


def back_kernel(left_ref, right_ref, out_ref):
    out_ref[...] = dot_back(left_ref[...], right_ref[...]).astype(jnp.bfloat16)


def back_low(left, right):
    whole = pl.BlockSpec(memory_space=pltpu.VMEM)
    return pl.pallas_call(
        back_kernel,
        out_shape=jax.ShapeDtypeStruct((left.shape[0], right.shape[0]), jnp.bfloat16),
        in_specs=[whole, whole],
        out_specs=whole,
        compiler_params=pltpu.CompilerParams(vmem_limit_bytes=48 << 20),
        cost_estimate=pl.CostEstimate(flops=0, bytes_accessed=0, transcendentals=0),
        name="back_low",
    )(left, right)


def product_kernel(chunk, pairs, index_ref, *refs):
    extra_ref = refs[2 * pairs] if len(refs) > 2 * pairs + 2 else None
    send_ref, keep_ref = refs[-2:]
    rows = send_ref.shape[0]
    core = index_ref[2]

    def put(lanes, whole):
        low, high = whole[:rows], whole[rows:]
        send_ref[:, lanes] = jnp.where(core == 0, high, low).astype(jnp.bfloat16)
        keep_ref[:, lanes] = jnp.where(core == 0, low, high).astype(jnp.bfloat16)

    base = 0
    for pair in range(pairs):
        left_ref, right_ref = refs[2 * pair : 2 * pair + 2]
        left = left_ref[...]
        for start in range(0, right_ref.shape[1], chunk):
            put(
                slice(base + start, base + start + chunk),
                dot_rows(left, right_ref[:, start : start + chunk]),
            )
        base += right_ref.shape[1]
    if extra_ref is not None:
        put(slice(base, None), extra_ref[...].astype(jnp.float32))


def product(index, pairs, extra, depth):
    tokens, rows = pairs[0][0].shape[0], pairs[0][0].shape[1] // depth
    inputs, specs = [index], [pl.BlockSpec(memory_space=pltpu.SMEM)]
    columns = 0
    for left, right in pairs:
        inputs += [left, right]
        specs += [
            pl.BlockSpec((tokens, rows), lambda i: (0, i)),
            pl.BlockSpec((tokens, right.shape[1]), lambda i: (0, 0)),
        ]
        columns += right.shape[1]
    wide = columns
    if extra is not None:
        inputs.append(extra)
        specs.append(pl.BlockSpec((rows, extra.shape[1]), lambda i: (i, 0)))
        wide += extra.shape[1]
    half = pl.BlockSpec((rows // 2, wide), lambda i: (i, 0))
    shape = jax.ShapeDtypeStruct((depth * rows // 2, wide), jnp.bfloat16)
    return tuple(
        pl.pallas_call(
            functools.partial(product_kernel, 512, len(pairs)),
            grid=(depth,),
            out_shape=[shape, shape],
            in_specs=specs,
            out_specs=[half, half],
            compiler_params=pltpu.CompilerParams(vmem_limit_bytes=48 << 20),
            cost_estimate=pl.CostEstimate(flops=0, bytes_accessed=0, transcendentals=0),
            name="product",
        )(*inputs)
    )


def place_kernel(part, middle, index_ref, *refs):
    *far, mine, from_x, from_y, out_ref = refs
    rep = index_ref[0]

    def put(offset, lanes, value):
        start = pl.multiple_of((rep ^ offset) * part, 16)
        out_ref[pl.ds(start, part), lanes] = value[...].astype(jnp.float32)

    put(0, slice(None), mine)
    put(1, slice(None), from_x)
    put(2, slice(None), from_y)
    if len(far) == 1:
        put(3, slice(None), far[0])
    else:
        put(3, slice(0, middle), far[0])
        put(3, slice(middle, None), far[1])


def place(index, values, part):
    columns = values[-1].shape[1]
    middle = columns // 2
    whole = pl.BlockSpec(memory_space=pltpu.VMEM)
    return pl.pallas_call(
        functools.partial(place_kernel, part, middle),
        out_shape=jax.ShapeDtypeStruct((4 * part, columns), jnp.float32),
        in_specs=[pl.BlockSpec(memory_space=pltpu.SMEM)] + [whole] * len(values),
        out_specs=whole,
        compiler_params=pltpu.CompilerParams(vmem_limit_bytes=32 << 20),
        cost_estimate=pl.CostEstimate(flops=0, bytes_accessed=0, transcendentals=0),
        name="place",
    )(index, *values)


def assemble_kernel(depth, part, middle, widths, index_ref, *refs):
    sources = refs[:12]
    count = len(widths)
    outputs = refs[12:12 + count]
    held = refs[12 + count:12 + 2 * count]
    arrived, left_here = refs[12 + 2 * count:]
    rows = part * 4
    columns = sum(widths)
    rep, z, core = index_ref[0], index_ref[1], index_ref[2]
    blocks = []
    for step in range(depth):
        for side in range(2):
            own, mine, from_x, from_y, left, right = sources[6 * side:6 * side + 6]
            which = core if side == 0 else 1 - core
            base = pl.multiple_of((lax.rem(z + depth - step, depth) * 2 + which) * rows, rows)
            if step == 0:
                blocks.append((base, [(own, 0, rows, 0, 0, columns)]))
                continue
            start = (step - 1) * part
            moves = [
                (mine, start, part, rep * part, 0, columns),
                (from_x, start, part, (rep ^ 1) * part, 0, columns),
                (from_y, start, part, (rep ^ 2) * part, 0, columns),
                (left, start, part, (rep ^ 3) * part, 0, middle),
                (right, start, part, (rep ^ 3) * part, middle, columns),
            ]
            blocks.append((base, moves))
    used = 0
    plan = []
    for base, moves in blocks:
        copies = []
        for source, start, height, offset, first, last in moves:
            edge = 0
            for buffer, width in zip(held, widths):
                low, high = max(first, edge), min(last, edge + width)
                if low < high:
                    copies.append(
                        pltpu.make_async_copy(
                            source.at[pl.ds(start, height), pl.ds(low - first, high - low)],
                            buffer.at[
                                pl.ds(pl.multiple_of(base + offset, 16), height),
                                pl.ds(low - edge, high - low),
                            ],
                            arrived.at[used],
                        )
                    )
                    used += 1
                edge += width
        plan.append((base, copies))
    for _, copies in plan:
        for copy in copies:
            copy.start()
    stores = []
    for base, copies in plan:
        for copy in copies:
            copy.wait()
        for buffer, output in zip(held, outputs):
            place = pl.ds(base, rows)
            stores.append(
                pltpu.make_async_copy(
                    buffer.at[place, :], output.at[place, :], left_here.at[len(stores)]
                )
            )
            stores[-1].start()
    for store in stores:
        store.wait()


def assemble(index, here, there, depth, part, middle, widths):
    rows = here[0].shape[0] * 2 * depth
    total = sum(widths) * rows
    count = 2 * (1 + 5 * (depth - 1)) * len(widths)
    return pl.pallas_call(
        functools.partial(assemble_kernel, depth, part, middle, widths),
        out_shape=[jax.ShapeDtypeStruct((rows, width), jnp.bfloat16) for width in widths],
        in_specs=[pl.BlockSpec(memory_space=pltpu.SMEM)] + [pl.BlockSpec(memory_space=pl.ANY)] * 12,
        out_specs=[pl.BlockSpec(memory_space=pl.ANY)] * len(widths),
        scratch_shapes=[pltpu.VMEM((rows, width), jnp.bfloat16) for width in widths]
        + [
            pltpu.SemaphoreType.DMA((count,)),
            pltpu.SemaphoreType.DMA((2 * depth * len(widths),)),
        ],
        compiler_params=pltpu.CompilerParams(vmem_limit_bytes=2 * total + (8 << 20)),
        cost_estimate=pl.CostEstimate(flops=0, bytes_accessed=0, transcendentals=0),
        name="assemble",
    )(index, *here, *there)


def body(
    groups,
    shards,
    tokens,
    lengths,
    group_live,
    w_query,
    w_key,
    w_value,
    w_out,
    w_gate,
    w_up,
    w_down,
    g_attn,
    g_query,
    g_key,
    g_ffn,
    cotangent,
):
    links = Links(groups, shards)
    shard_rows = w_query.shape[0]
    width = HD * (H + 2 * KV)

    def column(values):
        return jnp.pad(values, (0, shard_rows - values.shape[0]))[:, None]

    gains = jnp.concatenate([column(g) for g in (g_attn, g_ffn, g_query, g_key)], axis=1)
    gains = jnp.pad(gains, ((0, 0), (0, 124)))
    packed = jnp.concatenate([w_query, w_key, w_value, w_out, gains], axis=1)
    first_move = links.gather_of(packed, (width, w_out.shape[1], 128))
    gate_move = links.gather_of(w_gate, (w_gate.shape[1],))
    up_move = links.gather_of(w_up, (w_up.shape[1],))
    down_move = links.gather_of(w_down, (w_down.shape[1],))
    for _ in range(3):
        advance([first_move])
    for _ in range(3):
        advance([first_move, gate_move])
    full_qkv, full_out, full_gains = first_move.result()
    full_qkv = advance([gate_move], full_qkv)
    full_qkv = advance([up_move], full_qkv)
    head_rows = g_query.shape[0]
    all_gains = full_gains[:, :4].astype(jnp.float32)
    gain_attn = all_gains[:, 0]
    gain_ffn = all_gains[:, 1]
    gain_query = all_gains[:, 2].reshape(shards, shard_rows)[:, :head_rows].reshape(HD)
    gain_key = all_gains[:, 3].reshape(shards, shard_rows)[:, :head_rows].reshape(HD)

    row_count = tokens.shape[0]
    x_float = tokens.astype(jnp.float32)
    row_index, segment, position, keep_mask = layout(lengths[0], group_live[0], row_count)
    allowed = (segment[:, None] == segment[None, :]) & (row_index[None, :] <= row_index[:, None])
    bias = jnp.where(allowed, 0.0, masked_score).astype(jnp.float32)
    gain_rows = jnp.stack([jnp.tile(gain_query, 2), jnp.tile(gain_key, 2)])
    tables = (*rotary_tables(position), jnp.pad(gain_rows, ((0, 6), (0, 0))), bias)
    unit_one, inverse_one = normalize(x_float)
    attn_input = (unit_one * gain_attn).astype(jnp.bfloat16)
    qkv = jnp.dot(attn_input, full_qkv, preferred_element_type=jnp.float32)
    parts, logs = [], []
    for first in range(KV // 2):
        part, log = attend(qkv, tables, first, 1)
        if first == 0:
            qkv, part = advance([up_move], qkv, part)
        if first == 1:
            qkv, part = advance([gate_move], qkv, part)
        if first == 2:
            qkv, part = advance([up_move], qkv, part)
        if first == 3:
            part = advance([gate_move], part)
            part = advance([up_move], part)
            part = advance([down_move], part)
        parts.append(part)
        logs.append(log)
    attended = jnp.concatenate(parts, axis=1)
    hidden = x_float + keep_mask[:, None] * jnp.dot(
        attended, full_out, preferred_element_type=jnp.float32
    )
    unit_two, inverse_two = normalize(hidden)
    ffn_input = (unit_two * gain_ffn).astype(jnp.bfloat16)
    (full_gate,) = gate_move.result()
    full_gate = advance([down_move], full_gate)
    gate_proj = jnp.dot(ffn_input, full_gate, preferred_element_type=jnp.float32)
    gate_proj = advance([down_move], gate_proj)
    gate_proj = advance([up_move], gate_proj)
    gate_proj = advance([up_move], gate_proj)
    gate_proj = advance([down_move], gate_proj)
    (full_up,) = up_move.result()
    up_proj = jnp.dot(ffn_input, full_up, preferred_element_type=jnp.float32)
    inner_low = (jax.nn.silu(gate_proj) * up_proj).astype(jnp.bfloat16)
    inner_low = advance([down_move], inner_low)

    d_final = cotangent.astype(jnp.float32)
    d_ffn = (keep_mask[:, None] * d_final).astype(jnp.bfloat16)
    down_sum = links.sum_of([(inner_low, d_ffn)])
    d_ffn, down_sum.held = advance([down_move], d_ffn, down_sum.held)
    (full_down,) = down_move.result()
    full_down = advance([down_sum], full_down)
    d_gate, d_up = inner_back(d_ffn, full_down, gate_proj, up_proj)
    d_gate, d_up = advance([down_sum], d_gate, d_up)
    gate_sum = links.sum_of([(ffn_input, d_gate)], depth_first=True)
    d_gate, d_up = advance([gate_sum], d_gate, d_up)
    up_sum = links.sum_of([(ffn_input, d_up)])
    d_gate, d_up = advance([up_sum], d_gate, d_up)
    d_gate, d_up = advance([gate_sum], d_gate, d_up)
    d_ffn_input = ffn_back(d_gate, d_up, full_gate, full_up)
    d_hidden_norm, grad_gain_ffn = norm_back(d_ffn_input, unit_two, inverse_two, gain_ffn)
    d_hidden = d_final + d_hidden_norm
    d_attn = (keep_mask[:, None] * d_hidden).astype(jnp.bfloat16)
    d_attn = advance([down_sum], d_attn)
    d_attn = advance([up_sum], d_attn)
    d_attended = back_low(d_attn, full_out)
    plans = ([gate_sum], [], [up_sum, down_sum], [gate_sum, down_sum])
    gain_sums, outputs = 0.0, ()
    for first in range(KV // 2):
        *outputs, gain_sum = attend_back(qkv, tables, logs[first], d_attended, first, 1, outputs)
        if plans[first]:
            d_attended, *outputs = advance(plans[first], d_attended, *outputs)
        gain_sums = gain_sums + gain_sum
    d_query, d_key, d_value = outputs
    grad_gain_query = gain_sums[0, :HD] + gain_sums[0, HD:]
    grad_gain_key = gain_sums[1, :HD] + gain_sums[1, HD:]
    d_attn_input = (
        back_product(d_query, full_qkv[:, : H * HD])
        + back_product(d_key, full_qkv[:, H * HD : (H + KV) * HD])
        + back_product(d_value, full_qkv[:, (H + KV) * HD :])
    )
    d_x_norm, grad_gain_attn = norm_back(d_attn_input, unit_one, inverse_one, gain_attn)
    grad_tokens = (d_hidden + d_x_norm).astype(jnp.bfloat16)

    def spread(values):
        blocks = jnp.pad(
            values.reshape(shards, head_rows), ((0, 0), (0, shard_rows - head_rows))
        )
        return blocks.reshape(shards * shard_rows)

    gain_grads = jnp.stack(
        [grad_gain_attn, grad_gain_ffn, spread(grad_gain_query), spread(grad_gain_key)], axis=1
    )
    gain_grads = jnp.pad(gain_grads, ((0, 0), (0, 252))).astype(jnp.bfloat16)
    gain_grads = settle([up_sum], gain_grads)
    qkv_sum = links.sum_of(
        [(attn_input, value) for value in (d_query, d_key, d_value)] + [(attended, d_attn)],
        gain_grads,
    )
    for plan in ([qkv_sum], [up_sum], [qkv_sum]):
        inner_low = advance(plan, inner_low)
    block_out = ffn_out(inner_low, full_down, hidden, keep_mask[:, None])
    plans = (
        [up_sum],
        [qkv_sum],
        [gate_sum],
        [down_sum],
        [up_sum],
        [qkv_sum],
        [gate_sum],
        [up_sum],
        [down_sum],
        [qkv_sum],
        [gate_sum],
        [up_sum],
        [qkv_sum],
        [gate_sum],
        [down_sum],
        [qkv_sum],
        [qkv_sum],
    )
    for plan in plans:
        block_out = advance(plan, block_out)
    owned = qkv_sum.result()
    grad_down, grad_gate, grad_up = down_sum.result(), gate_sum.result(), up_sum.result()
    last = width + w_out.shape[1]
    return (
        block_out,
        grad_tokens,
        owned[:, : H * HD],
        owned[:, H * HD : (H + KV) * HD],
        owned[:, (H + KV) * HD : width],
        owned[:, width : width + w_out.shape[1]],
        grad_gate,
        grad_up,
        grad_down,
        owned[:, last],
        owned[:head_rows, last + 2],
        owned[:head_rows, last + 3],
        owned[:, last + 1],
    )


def solution(mesh):
    in_specs = (
        P(("rep", "shard"), None),
        P(("rep", "shard"), None),
        P("rep"),
        P("shard", None),
        P("shard", None),
        P("shard", None),
        P("shard", None),
        P("shard", None),
        P("shard", None),
        P("shard", None),
        P("shard"),
        P("shard"),
        P("shard"),
        P("shard"),
        P(("rep", "shard"), None),
    )
    out_specs = (
        P(("rep", "shard"), None),
        P(("rep", "shard"), None),
        P("shard", None),
        P("shard", None),
        P("shard", None),
        P("shard", None),
        P("shard", None),
        P("shard", None),
        P("shard", None),
        P("shard"),
        P("shard"),
        P("shard"),
        P("shard"),
    )
    return jax.shard_map(
        functools.partial(body, mesh.shape["rep"], mesh.shape["shard"]),
        mesh=mesh,
        in_specs=in_specs,
        out_specs=out_specs,
        check_vma=False,
    )
```

```python
import functools

import jax
import jax.numpy as jnp
from jax import lax
from jax.experimental import pallas as pl
from jax.experimental.pallas import tpu as pltpu
from jax.sharding import PartitionSpec as P

H = 16
KV = 8
HD = 64


epsilon = 1e-05
theta_base = 1000000.0
masked_score = -1e30


def layout(seq_lengths, live_rows, row_count):
    row_index = jnp.arange(row_count, dtype=jnp.int32)
    seq_ends = jnp.cumsum(seq_lengths)
    passed_ends = row_index[:, None] >= seq_ends[None, :]
    segment = jnp.sum(passed_ends.astype(jnp.int32), axis=1, dtype=jnp.int32)
    begins = jnp.sum(jnp.where(passed_ends, seq_lengths[None, :], 0), axis=1, dtype=jnp.int32)
    live_mask = row_index < live_rows
    segment = jnp.where(live_mask, segment, -1)
    position = (row_index - begins).astype(jnp.float32)
    return (row_index, segment, position, live_mask.astype(jnp.float32))


def rotary_tables(position):
    half_width = HD // 2
    frequency = theta_base ** (-2.0 * jnp.arange(half_width, dtype=jnp.float32) / HD)
    angles = position[:, None] * frequency[None, :]
    cosine, sine = jnp.cos(angles), jnp.sin(angles)
    return (
        jnp.concatenate([cosine] * 4, axis=1),
        jnp.concatenate([-sine, sine, -sine, sine], axis=1),
    )


def normalize(values):
    inverse_rms = lax.rsqrt(jnp.mean(values * values, axis=-1, keepdims=True) + epsilon)
    return (values * inverse_rms, inverse_rms)


def norm_back(incoming, unit_values, inverse_rms, gain):
    grad_unit = incoming * gain
    grad_values = inverse_rms * (
        grad_unit - unit_values * jnp.mean(unit_values * grad_unit, axis=-1, keepdims=True)
    )
    grad_gain = jnp.sum((incoming * unit_values).reshape(-1, unit_values.shape[-1]), axis=0)
    return (grad_values, grad_gain)


def rows_product(left, right):
    return lax.dot_general(
        left, right, (((0,), (0,)), ((), ())), preferred_element_type=jnp.float32
    )


def back_product(left, right):
    return lax.dot_general(
        left, right, (((1,), (1,)), ((), ())), preferred_element_type=jnp.float32
    )


def lane_index(shape):
    return lax.broadcasted_iota(jnp.int32, shape, len(shape) - 1)


def head_mean(values):
    first = lane_index(values.shape) < HD
    low = jnp.sum(jnp.where(first, values, 0.0), axis=-1, keepdims=True)
    high = jnp.sum(jnp.where(first, 0.0, values), axis=-1, keepdims=True)
    return jnp.where(first, low, high) * (1.0 / HD)


def swap_halves(values):
    front = lane_index(values.shape) % HD < HD // 2
    return jnp.where(
        front, pltpu.roll(values, 2 * HD - HD // 2, 1), pltpu.roll(values, HD // 2, 1)
    )


def head_unit(raw):
    inverse = lax.rsqrt(head_mean(raw * raw) + epsilon)
    return raw * inverse, inverse


def head_norm_back(incoming, unit_values, inverse, gain):
    grad_unit = incoming * gain
    return inverse * (grad_unit - unit_values * head_mean(unit_values * grad_unit))


def pair_of(values, which):
    first = lane_index(values.shape) < HD
    kept = jnp.where(first, values, 0.0) if which == 0 else jnp.where(first, 0.0, values)
    moved = pltpu.roll(kept, HD, 1)
    pair = (kept, moved) if which == 0 else (moved, kept)
    return tuple(value.astype(jnp.bfloat16) for value in pair)


def dot_rows(left, right):
    return lax.dot_general(
        left, right, (((0,), (0,)), ((), ())), preferred_element_type=jnp.float32
    )


def dot_back(left, right):
    return lax.dot_general(
        left, right, (((1,), (1,)), ((), ())), preferred_element_type=jnp.float32
    )


def dot_plain(left, right):
    return lax.dot_general(
        left, right, (((1,), (0,)), ((), ())), preferred_element_type=jnp.float32
    )


def attend_kernel(block, q_ref, k_ref, v_ref, cos_ref, sin_ref, gain_ref, bias_ref, out_ref, log_ref):
    rows = q_ref.shape[0]
    tile = 2 * HD
    cosine, sine = cos_ref[...], sin_ref[...]
    first = lane_index((block, tile)) < HD

    def turned(raw, gain):
        unit_values, _ = head_unit(raw)
        scaled = unit_values * gain
        return cosine * scaled + sine * swap_halves(scaled)

    k_turned = turned(k_ref[...], gain_ref[1:2, :])
    v_values = v_ref[...]
    for which in range(2):
        lanes = slice(which * tile, (which + 1) * tile)
        query = (turned(q_ref[:, lanes], gain_ref[0:1, :]).astype(jnp.bfloat16)) * HD ** (-0.5)
        query = query.astype(jnp.bfloat16)
        keys = pair_of(k_turned, which)
        values = pair_of(v_values, which)
        for start in range(0, rows, block):
            stop = start + block
            bias = bias_ref[start:stop, :stop]
            result = jnp.zeros((block, tile), jnp.float32)
            logs = []
            for head in range(2):
                scores = dot_back(query[start:stop], keys[head][:stop]) + bias
                top = jnp.max(scores, axis=-1, keepdims=True)
                weights = jnp.exp(scores - top)
                totals = jnp.sum(weights, axis=-1, keepdims=True)
                low = (weights * (1.0 / totals)).astype(jnp.bfloat16)
                result += dot_plain(low, values[head][:stop])
                logs.append(top + jnp.log(totals))
            out_ref[start:stop, lanes] = result.astype(jnp.bfloat16)
            log_ref[start:stop, lanes] = jnp.where(first, logs[0], logs[1])


def attend_back_kernel(
    block,
    q_ref,
    k_ref,
    v_ref,
    cos_ref,
    sin_ref,
    gain_ref,
    bias_ref,
    log_ref,
    grad_ref,
    *refs,
):
    rows = q_ref.shape[0]
    tile = 2 * HD
    cosine, sine = cos_ref[...], sin_ref[...]
    dq_ref, dk_ref, dv_ref, gain_grad_ref, key_sum, value_sum = refs[-6:]
    query_gain, key_gain = gain_ref[0:1, :], gain_ref[1:2, :]
    first = lane_index((rows, tile)) < HD
    scale = HD ** (-0.5)

    @pl.when(pl.program_id(0) == 0)
    def _():
        gain_grad_ref[...] = jnp.zeros_like(gain_grad_ref)

    def turned(scaled):
        return cosine * scaled + sine * swap_halves(scaled)

    def back(incoming, unit_values, inverse, gain, row):
        flat = cosine * incoming - sine * swap_halves(incoming)
        gain_grad_ref[row:row + 1, :] += jnp.sum(flat * unit_values, axis=0, keepdims=True)
        return head_norm_back(flat, unit_values, inverse, gain).astype(jnp.bfloat16)

    k_unit, k_inverse = head_unit(k_ref[...])
    k_turned = turned(k_unit * key_gain)
    v_values = v_ref[...]
    key_parts, value_parts = [], []
    for which in range(2):
        lanes = slice(which * tile, (which + 1) * tile)
        q_unit, q_inverse = head_unit(q_ref[:, lanes])
        query = (turned(q_unit * query_gain)).astype(jnp.bfloat16)
        query = (query * scale).astype(jnp.bfloat16)
        keys = pair_of(k_turned, which)
        values = pair_of(v_values, which)
        key_sum[...] = jnp.zeros_like(key_sum)
        value_sum[...] = jnp.zeros_like(value_sum)
        d_query = []
        for start in range(0, rows, block):
            stop = start + block
            bias = bias_ref[start:stop, :stop]
            grad = grad_ref[start:stop, lanes]
            part = jnp.zeros((block, tile), jnp.float32)
            for head in range(2):
                column = which * tile + head * HD
                logs = log_ref[start:stop, column:column + 1]
                scores = dot_back(query[start:stop], keys[head][:stop]) + bias
                probability = jnp.exp(scores - logs)
                grad_prob = dot_back(grad, values[head][:stop])
                terms = jnp.sum(probability * grad_prob, axis=-1, keepdims=True)
                grad_scores = (probability * (grad_prob - terms)).astype(jnp.bfloat16)
                part += dot_plain(grad_scores, keys[head][:stop])
                key_sum[head, :stop, :] += dot_rows(grad_scores, query[start:stop])
                value_sum[head, :stop, :] += dot_rows(probability.astype(jnp.bfloat16), grad)
            d_query.append(part * scale)
        dq_ref[:, lanes] = back(
            jnp.concatenate(d_query, axis=0), q_unit, q_inverse, query_gain, 0
        )
        for total, parts in ((key_sum, key_parts), (value_sum, value_parts)):
            joined = jnp.where(first, total[0], total[1])
            parts.append(joined + pltpu.roll(joined, HD, 1))
    d_key = jnp.where(first, key_parts[0], key_parts[1])
    dk_ref[...] = back(d_key, k_unit, k_inverse, key_gain, 1)
    dv_ref[...] = jnp.where(first, value_parts[0], value_parts[1]).astype(jnp.bfloat16)


def attention_specs(rows, first=0):
    tile = 2 * HD
    fixed = lambda i: (0, 0)
    return [
        pl.BlockSpec((rows, 2 * tile), lambda i: (0, first + i)),
        pl.BlockSpec((rows, tile), lambda i: (0, H // 2 + first + i)),
        pl.BlockSpec((rows, tile), lambda i: (0, H // 2 + KV // 2 + first + i)),
        pl.BlockSpec((rows, tile), fixed),
        pl.BlockSpec((rows, tile), fixed),
        pl.BlockSpec((8, tile), fixed),
        pl.BlockSpec((rows, rows), fixed),
    ]


def attend(qkv, tables, first, count):
    rows = qkv.shape[0]
    wide = pl.BlockSpec((rows, 4 * HD), lambda i: (0, i))
    return pl.pallas_call(
        functools.partial(attend_kernel, rows // 2),
        grid=(count,),
        out_shape=[
            jax.ShapeDtypeStruct((rows, 4 * HD * count), jnp.bfloat16),
            jax.ShapeDtypeStruct((rows, 4 * HD * count), jnp.float32),
        ],
        in_specs=attention_specs(rows, first),
        out_specs=[wide, wide],
        compiler_params=pltpu.CompilerParams(vmem_limit_bytes=48 << 20),
        cost_estimate=pl.CostEstimate(flops=0, bytes_accessed=0, transcendentals=0),
        name="attend",
    )(qkv, qkv, qkv, *tables)


def attend_back(qkv, tables, logs, grad, first, count, before=()):
    rows = qkv.shape[0]
    tile = 2 * HD
    wide = pl.BlockSpec((rows, 2 * tile), lambda i: (0, i))
    taken = pl.BlockSpec((rows, 2 * tile), lambda i: (0, first + i))
    narrow = pl.BlockSpec((rows, tile), lambda i: (0, first + i))
    specs = attention_specs(rows, first) + [wide, taken]
    return pl.pallas_call(
        functools.partial(attend_back_kernel, rows // 2),
        grid=(count,),
        out_shape=[
            jax.ShapeDtypeStruct((rows, H * HD), jnp.bfloat16),
            jax.ShapeDtypeStruct((rows, KV * HD), jnp.bfloat16),
            jax.ShapeDtypeStruct((rows, KV * HD), jnp.bfloat16),
            jax.ShapeDtypeStruct((8, tile), jnp.float32),
        ],
        in_specs=specs + [pl.BlockSpec(memory_space=pl.ANY)] * len(before),
        input_output_aliases={len(specs) + i: i for i in range(len(before))},
        out_specs=[taken, narrow, narrow, pl.BlockSpec((8, tile), lambda i: (0, 0))],
        scratch_shapes=[
            pltpu.VMEM((2, rows, tile), jnp.float32),
            pltpu.VMEM((2, rows, tile), jnp.float32),
        ],
        compiler_params=pltpu.CompilerParams(vmem_limit_bytes=48 << 20),
        cost_estimate=pl.CostEstimate(flops=0, bytes_accessed=0, transcendentals=0),
        name="attend_back",
    )(qkv, qkv, qkv, *tables, logs, grad, *before)


def inner_back_kernel(d_ref, down_ref, gate_ref, up_ref, d_gate_ref, d_up_ref):
    d_inner = dot_back(d_ref[...], down_ref[...])
    gate = gate_ref[...]
    sigmoid = jax.nn.sigmoid(gate)
    d_gate = d_inner * up_ref[...] * sigmoid * (1.0 + gate * (1.0 - sigmoid))
    d_gate_ref[...] = d_gate.astype(jnp.bfloat16)
    d_up_ref[...] = (d_inner * gate * sigmoid).astype(jnp.bfloat16)


def inner_back(d_ffn, full_down, gate_proj, up_proj):
    (rows, width), units = d_ffn.shape, full_down.shape[0]
    tile = 512
    columns = pl.BlockSpec((rows, tile), lambda i: (0, i))
    shape = jax.ShapeDtypeStruct((rows, units), jnp.bfloat16)
    return pl.pallas_call(
        inner_back_kernel,
        grid=(units // tile,),
        out_shape=[shape, shape],
        in_specs=[
            pl.BlockSpec((rows, width), lambda i: (0, 0)),
            pl.BlockSpec((tile, width), lambda i: (i, 0)),
            columns,
            columns,
        ],
        out_specs=[columns, columns],
        compiler_params=pltpu.CompilerParams(vmem_limit_bytes=48 << 20),
        cost_estimate=pl.CostEstimate(flops=0, bytes_accessed=0, transcendentals=0),
        name="inner_back",
    )(d_ffn, full_down, gate_proj, up_proj)


def ffn_out_kernel(inner_ref, down_ref, hidden_ref, keep_ref, out_ref, total):
    step = pl.program_id(0)
    part = dot_plain(inner_ref[...], down_ref[...])

    @pl.when(step == 0)
    def _():
        total[...] = part

    @pl.when(step > 0)
    def _():
        total[...] += part

    @pl.when(step == pl.num_programs(0) - 1)
    def _():
        out_ref[...] = (hidden_ref[...] + keep_ref[...] * total[...]).astype(jnp.bfloat16)


def ffn_out(inner_low, full_down, hidden, keep_column):
    (rows, units), width = inner_low.shape, full_down.shape[1]
    tile = 512
    fixed = lambda i: (0, 0)
    return pl.pallas_call(
        ffn_out_kernel,
        grid=(units // tile,),
        out_shape=jax.ShapeDtypeStruct((rows, width), jnp.bfloat16),
        in_specs=[
            pl.BlockSpec((rows, tile), lambda i: (0, i)),
            pl.BlockSpec((tile, width), lambda i: (i, 0)),
            pl.BlockSpec((rows, width), fixed),
            pl.BlockSpec((rows, 1), fixed),
        ],
        out_specs=pl.BlockSpec((rows, width), fixed),
        scratch_shapes=[pltpu.VMEM((rows, width), jnp.float32)],
        compiler_params=pltpu.CompilerParams(vmem_limit_bytes=48 << 20),
        cost_estimate=pl.CostEstimate(flops=0, bytes_accessed=0, transcendentals=0),
        name="ffn_out",
    )(inner_low, full_down, hidden, keep_column)


def ffn_back_kernel(d_gate_ref, d_up_ref, gate_ref, up_ref, out_ref):
    part = dot_back(d_gate_ref[...], gate_ref[...]) + dot_back(d_up_ref[...], up_ref[...])

    @pl.when(pl.program_id(0) == 0)
    def _():
        out_ref[...] = part

    @pl.when(pl.program_id(0) > 0)
    def _():
        out_ref[...] += part


def ffn_back(d_gate, d_up, full_gate, full_up):
    (rows, units), width = d_gate.shape, full_gate.shape[0]
    tile = 512
    left = pl.BlockSpec((rows, tile), lambda i: (0, i))
    right = pl.BlockSpec((width, tile), lambda i: (0, i))
    return pl.pallas_call(
        ffn_back_kernel,
        grid=(units // tile,),
        out_shape=jax.ShapeDtypeStruct((rows, width), jnp.float32),
        in_specs=[left, left, right, right],
        out_specs=pl.BlockSpec((rows, width), lambda i: (0, 0)),
        compiler_params=pltpu.CompilerParams(vmem_limit_bytes=48 << 20),
        cost_estimate=pl.CostEstimate(flops=0, bytes_accessed=0, transcendentals=0),
        name="ffn_back",
    )(d_gate, d_up, full_gate, full_up)


class Links:
    def __init__(self, groups, shards):
        self.groups = groups
        self.shards = shards
        self.depth = shards // 2
        rep = lax.axis_index("rep")
        shard = lax.axis_index("shard")
        self.rep = rep
        self.z = shard // 2
        self.core = shard % 2
        self.index = jnp.stack([rep, self.z, self.core]).astype(jnp.int32)

    def across_core(self, value):
        return lax.ppermute(value, "shard", [(s, s ^ 1) for s in range(self.shards)])

    def across_x(self, value):
        return lax.ppermute(value, "rep", [(r, r ^ 1) for r in range(self.groups)])

    def across_y(self, value):
        return lax.ppermute(value, "rep", [(r, r ^ 2) for r in range(self.groups)])

    def along_z(self, value):
        pairs = [(s, (s + 2) % self.shards) for s in range(self.shards)]
        return lax.ppermute(value, "shard", pairs)

    def fits(self, rows):
        return self.groups == 4 and self.shards % 2 == 0 and rows % 64 == 0

    def gather_of(self, shard, widths):
        kind = Gather if self.fits(shard.shape[0]) else PlainGather
        return kind(self, shard, widths)

    def sum_of(self, pairs, extra=None, depth_first=False):
        kind = Sum if self.fits(pairs[0][0].shape[1] // self.shards) else PlainSum
        return kind(self, pairs, extra, depth_first)


def add(*values):
    return functools.reduce(jnp.add, [value.astype(jnp.float32) for value in values])


def advance(moves, *others):
    states = [(move.held, move.flying) for move in moves]
    states, others = lax.optimization_barrier((states, others))
    sends = []
    for move, (held, flying) in zip(moves, states):
        move.held, move.flying = held, flying
        move.held, move.sends = next(move.work)
        sends.append([value for _, value in move.sends])
    sends, others = lax.optimization_barrier((sends, others))
    for move, values in zip(moves, sends):
        move.flying = tuple(link(value) for (link, _), value in zip(move.sends, values))
    return others[0] if len(others) == 1 else others


def settle(moves, *others):
    states = [(move.held, move.flying) for move in moves]
    states, others = lax.optimization_barrier((states, others))
    for move, (held, flying) in zip(moves, states):
        move.held, move.flying = held, flying
    return others[0] if len(others) == 1 else others


class Moves:
    held = ()
    flying = ()

    def still(self):
        while True:
            yield (), ()

    def finish(self):
        for self.held, sends in self.work:
            self.flying = tuple(link(value) for link, value in sends)


class PlainGather(Moves):
    def __init__(self, links, shard, widths):
        self.shard, self.widths = shard, widths
        self.work = self.still()

    def result(self):
        whole = lax.all_gather(self.shard, "shard", axis=0, tiled=True)
        cuts = [sum(self.widths[:i]) for i in range(1, len(self.widths))]
        return jnp.split(whole, cuts, axis=1)


class PlainSum(Moves):
    def __init__(self, links, pairs, extra, depth_first):
        parts = [rows_product(left, right).astype(jnp.bfloat16) for left, right in pairs]
        self.low = jnp.concatenate(parts + ([] if extra is None else [extra]), axis=1)
        self.work = self.still()

    def result(self):
        owned = lax.psum_scatter(self.low, "shard", scatter_dimension=0, tiled=True)
        return lax.psum(owned, "rep").astype(jnp.float32)


class Gather(Moves):
    def __init__(self, links, shard, widths):
        self.links, self.shard, self.widths = links, shard, widths
        rows, self.columns = shard.shape
        self.part = rows // links.groups
        self.middle = self.columns // 256 * 128
        self.held = (lax.dynamic_slice_in_dim(shard, links.rep * self.part, self.part, axis=0),)
        self.work = self.stages()

    def stages(self):
        links, middle = self.links, self.middle
        moving, pieces = self.held[0], ()
        for step in range(links.depth - 1):
            moves = ((links.along_z, moving),)
            if step == 0:
                moves += ((links.across_core, self.shard),)
            yield pieces, moves
            moving = self.flying[0]
            pieces = self.held + self.flying
        first, other, *rest = pieces
        mine = jnp.concatenate([first, *rest], axis=0)
        yield (mine, other), (
            (links.across_x, mine),
            (links.across_y, mine),
            (links.across_core, mine),
        )
        from_x, from_y, _ = self.flying
        yield self.held + self.flying, (
            (links.across_y, from_x[:, :middle]),
            (links.across_x, from_y[:, middle:]),
            (links.across_core, from_x),
            (links.across_core, from_y),
        )
        yield self.held + self.flying, (
            (links.across_core, self.flying[0]),
            (links.across_core, self.flying[1]),
        )

    def result(self):
        self.finish()
        mine, other, from_x, from_y, mine_core, left, right, x_core, y_core = self.held
        here = (self.shard, mine, from_x, from_y, left, right)
        there = (other, mine_core, x_core, y_core, *self.flying)
        links = self.links
        return assemble(
            links.index, here, there, links.depth, self.part, self.middle, self.widths
        )


class Sum(Moves):
    def __init__(self, links, pairs, extra, depth_first):
        self.links = links
        self.part = pairs[0][0].shape[1] // links.shards // links.groups
        self.held = product(links.index, pairs, extra, links.depth)
        self.work = self.stages(depth_first)

    def result(self):
        self.finish()
        return place(self.links.index, self.flying + self.held, self.part)

    def stages(self, depth_first):
        links, part = self.links, self.part
        yield (self.held[1],), ((links.across_core, self.held[0]),)
        pair = self.held + self.flying
        if depth_first:
            yield from self.along(pair, links.groups * part)
            yield from self.across((self.held[0], self.flying[0]), 1)
            own, left, right = self.held + self.flying
            mine = jnp.concatenate(
                [add(own[:, : left.shape[1]], left), add(own[:, left.shape[1] :], right)], axis=1
            )
        else:
            yield from self.across(pair, links.depth)
            yield from self.along(self.held + self.flying, part)
            mine = add(self.held[0], self.flying[0])
        mine = mine.astype(jnp.bfloat16)
        middle = mine.shape[1] // 2
        yield (mine,), ((links.across_x, mine), (links.across_y, mine))
        from_x, from_y = self.flying
        yield self.held + (from_x, from_y), (
            (links.across_y, from_x[:, :middle]),
            (links.across_x, from_y[:, middle:]),
        )

    def across(self, pair, depth):
        links, part = self.links, self.part
        left, right = sum_first(links.index, pair, part, depth)
        yield pair, ((links.across_x, left), (links.across_y, right))
        left, right, own = sum_second(links.index, self.held, self.flying, part, depth)
        yield (own,), ((links.across_y, left), (links.across_x, right))

    def along(self, values, rows):
        links = self.links
        moving, *terms = ring_terms(links.index, values, rows, links.depth)
        yield tuple(terms), ((links.along_z, moving),)
        for _ in range(links.depth - 2):
            moving = add(self.held[0], self.flying[0]).astype(jnp.bfloat16)
            yield self.held[1:], ((links.along_z, moving),)


def sum_first_kernel(index_ref, *refs):
    keep, received = refs[0:3], refs[3:6]
    left_ref, right_ref = refs[6:]

    def total(place):
        return keep[place][...].astype(jnp.float32) + received[place][...].astype(jnp.float32)

    both = total(2).astype(jnp.bfloat16)
    middle = left_ref.shape[2]
    left_ref[0] = total(0).astype(jnp.bfloat16)
    left_ref[1] = both[:, :middle]
    right_ref[0] = total(1).astype(jnp.bfloat16)
    right_ref[1] = both[:, middle:]


def sum_first(index, pair, part, depth):
    columns = pair[0].shape[1]
    middle = columns // 2
    specs = [
        pl.BlockSpec((part, middle), lambda i, index: (4 * i + (index[0] ^ 1), 0)),
        pl.BlockSpec((part, middle), lambda i, index: (4 * i + (index[0] ^ 2), 1)),
        pl.BlockSpec((part, columns), lambda i, index: (4 * i + (index[0] ^ 3), 0)),
    ]
    half = pl.BlockSpec((2, part, middle), lambda i, index: (0, i, 0))
    shape = jax.ShapeDtypeStruct((2, depth * part, middle), jnp.bfloat16)
    return pl.pallas_call(
        sum_first_kernel,
        grid_spec=pltpu.PrefetchScalarGridSpec(
            num_scalar_prefetch=1, grid=(depth,), in_specs=specs * 2, out_specs=[half, half]
        ),
        out_shape=[shape, shape],
        compiler_params=pltpu.CompilerParams(vmem_limit_bytes=48 << 20),
        cost_estimate=pl.CostEstimate(flops=0, bytes_accessed=0, transcendentals=0),
        name="sum_first",
    )(index, *([pair[0]] * 3 + [pair[1]] * 3))


def sum_second_kernel(index_ref, *refs):
    keep, received = refs[0:3], refs[3:6]
    from_left, from_right, left_ref, right_ref, own_ref = refs[6:]
    middle = left_ref.shape[1]

    def total(place):
        return keep[place][...].astype(jnp.float32) + received[place][...].astype(jnp.float32)

    left_ref[...] = (total(0) + from_left[1].astype(jnp.float32)).astype(jnp.bfloat16)
    right_ref[...] = (total(1) + from_right[1].astype(jnp.float32)).astype(jnp.bfloat16)
    own = total(2)
    own_ref[:, :middle] = (own[:, :middle] + from_left[0].astype(jnp.float32)).astype(jnp.bfloat16)
    own_ref[:, middle:] = (own[:, middle:] + from_right[0].astype(jnp.float32)).astype(jnp.bfloat16)


def sum_second(index, pair, arrived, part, depth):
    columns = pair[0].shape[1]
    middle = columns // 2
    specs = [
        pl.BlockSpec((part, middle), lambda i, index: (4 * i + (index[0] ^ 2), 0)),
        pl.BlockSpec((part, middle), lambda i, index: (4 * i + (index[0] ^ 1), 1)),
        pl.BlockSpec((part, columns), lambda i, index: (4 * i + index[0], 0)),
    ]
    two = pl.BlockSpec((2, part, middle), lambda i, index: (0, i, 0))
    half = pl.BlockSpec((part, middle), lambda i, index: (i, 0))
    shape = jax.ShapeDtypeStruct((depth * part, middle), jnp.bfloat16)
    return pl.pallas_call(
        sum_second_kernel,
        grid_spec=pltpu.PrefetchScalarGridSpec(
            num_scalar_prefetch=1,
            grid=(depth,),
            in_specs=specs * 2 + [two, two],
            out_specs=[half, half, pl.BlockSpec((part, columns), lambda i, index: (i, 0))],
        ),
        out_shape=[shape, shape, jax.ShapeDtypeStruct((depth * part, columns), jnp.bfloat16)],
        compiler_params=pltpu.CompilerParams(vmem_limit_bytes=48 << 20),
        cost_estimate=pl.CostEstimate(flops=0, bytes_accessed=0, transcendentals=0),
        name="sum_second",
    )(index, *([pair[0]] * 3 + [pair[1]] * 3), *arrived)


def ring_terms_kernel(depth, index_ref, own_ref, *refs):
    others, outputs = refs[:-depth], refs[-depth:]
    own = own_ref[...].astype(jnp.float32)
    rest = [other[...].astype(jnp.float32) for other in others]
    total = own + (rest[0] if len(rest) == 1 else jnp.concatenate(rest, axis=1))
    for step in range(depth):

        @pl.when(pl.program_id(0) == step)
        def _(step=step):
            outputs[step][...] = total.astype(jnp.bfloat16)


def ring_terms(index, values, rows, depth):
    columns = values[0].shape[1]
    at = lambda i, index: (lax.rem(index[1] + 2 * depth - 1 - i, depth), 0)
    shape = jax.ShapeDtypeStruct((rows, columns), jnp.bfloat16)
    return pl.pallas_call(
        functools.partial(ring_terms_kernel, depth),
        grid_spec=pltpu.PrefetchScalarGridSpec(
            num_scalar_prefetch=1,
            grid=(depth,),
            in_specs=[pl.BlockSpec((rows, value.shape[1]), at) for value in values],
            out_specs=[pl.BlockSpec((rows, columns), lambda i, index: (0, 0))] * depth,
        ),
        out_shape=[shape] * depth,
        compiler_params=pltpu.CompilerParams(vmem_limit_bytes=48 << 20),
        cost_estimate=pl.CostEstimate(flops=0, bytes_accessed=0, transcendentals=0),
        name="ring_terms",
    )(index, *values)


def back_kernel(left_ref, right_ref, out_ref):
    out_ref[...] = dot_back(left_ref[...], right_ref[...]).astype(jnp.bfloat16)


def back_low(left, right):
    whole = pl.BlockSpec(memory_space=pltpu.VMEM)
    return pl.pallas_call(
        back_kernel,
        out_shape=jax.ShapeDtypeStruct((left.shape[0], right.shape[0]), jnp.bfloat16),
        in_specs=[whole, whole],
        out_specs=whole,
        compiler_params=pltpu.CompilerParams(vmem_limit_bytes=48 << 20),
        cost_estimate=pl.CostEstimate(flops=0, bytes_accessed=0, transcendentals=0),
        name="back_low",
    )(left, right)


def product_kernel(chunk, pairs, index_ref, *refs):
    extra_ref = refs[2 * pairs] if len(refs) > 2 * pairs + 2 else None
    send_ref, keep_ref = refs[-2:]
    rows = send_ref.shape[0]
    core = index_ref[2]

    def put(lanes, whole):
        low, high = whole[:rows], whole[rows:]
        send_ref[:, lanes] = jnp.where(core == 0, high, low).astype(jnp.bfloat16)
        keep_ref[:, lanes] = jnp.where(core == 0, low, high).astype(jnp.bfloat16)

    base = 0
    for pair in range(pairs):
        left_ref, right_ref = refs[2 * pair : 2 * pair + 2]
        left = left_ref[...]
        for start in range(0, right_ref.shape[1], chunk):
            put(
                slice(base + start, base + start + chunk),
                dot_rows(left, right_ref[:, start : start + chunk]),
            )
        base += right_ref.shape[1]
    if extra_ref is not None:
        put(slice(base, None), extra_ref[...].astype(jnp.float32))


def product(index, pairs, extra, depth):
    tokens, rows = pairs[0][0].shape[0], pairs[0][0].shape[1] // depth
    inputs, specs = [index], [pl.BlockSpec(memory_space=pltpu.SMEM)]
    columns = 0
    for left, right in pairs:
        inputs += [left, right]
        specs += [
            pl.BlockSpec((tokens, rows), lambda i: (0, i)),
            pl.BlockSpec((tokens, right.shape[1]), lambda i: (0, 0)),
        ]
        columns += right.shape[1]
    wide = columns
    if extra is not None:
        inputs.append(extra)
        specs.append(pl.BlockSpec((rows, extra.shape[1]), lambda i: (i, 0)))
        wide += extra.shape[1]
    half = pl.BlockSpec((rows // 2, wide), lambda i: (i, 0))
    shape = jax.ShapeDtypeStruct((depth * rows // 2, wide), jnp.bfloat16)
    return tuple(
        pl.pallas_call(
            functools.partial(product_kernel, 512, len(pairs)),
            grid=(depth,),
            out_shape=[shape, shape],
            in_specs=specs,
            out_specs=[half, half],
            compiler_params=pltpu.CompilerParams(vmem_limit_bytes=48 << 20),
            cost_estimate=pl.CostEstimate(flops=0, bytes_accessed=0, transcendentals=0),
            name="product",
        )(*inputs)
    )


def place_kernel(part, middle, index_ref, *refs):
    *far, mine, from_x, from_y, out_ref = refs
    rep = index_ref[0]

    def put(offset, lanes, value):
        start = pl.multiple_of((rep ^ offset) * part, 16)
        out_ref[pl.ds(start, part), lanes] = value[...].astype(jnp.float32)

    put(0, slice(None), mine)
    put(1, slice(None), from_x)
    put(2, slice(None), from_y)
    if len(far) == 1:
        put(3, slice(None), far[0])
    else:
        put(3, slice(0, middle), far[0])
        put(3, slice(middle, None), far[1])


def place(index, values, part):
    columns = values[-1].shape[1]
    middle = columns // 2
    whole = pl.BlockSpec(memory_space=pltpu.VMEM)
    return pl.pallas_call(
        functools.partial(place_kernel, part, middle),
        out_shape=jax.ShapeDtypeStruct((4 * part, columns), jnp.float32),
        in_specs=[pl.BlockSpec(memory_space=pltpu.SMEM)] + [whole] * len(values),
        out_specs=whole,
        compiler_params=pltpu.CompilerParams(vmem_limit_bytes=32 << 20),
        cost_estimate=pl.CostEstimate(flops=0, bytes_accessed=0, transcendentals=0),
        name="place",
    )(index, *values)


def assemble_kernel(depth, part, middle, widths, index_ref, *refs):
    sources = refs[:12]
    count = len(widths)
    outputs = refs[12:12 + count]
    held = refs[12 + count:12 + 2 * count]
    arrived, left_here = refs[12 + 2 * count:]
    rows = part * 4
    columns = sum(widths)
    rep, z, core = index_ref[0], index_ref[1], index_ref[2]
    blocks = []
    for step in range(depth):
        for side in range(2):
            own, mine, from_x, from_y, left, right = sources[6 * side:6 * side + 6]
            which = core if side == 0 else 1 - core
            base = pl.multiple_of((lax.rem(z + depth - step, depth) * 2 + which) * rows, rows)
            if step == 0:
                blocks.append((base, [(own, 0, rows, 0, 0, columns)]))
                continue
            start = (step - 1) * part
            moves = [
                (mine, start, part, rep * part, 0, columns),
                (from_x, start, part, (rep ^ 1) * part, 0, columns),
                (from_y, start, part, (rep ^ 2) * part, 0, columns),
                (left, start, part, (rep ^ 3) * part, 0, middle),
                (right, start, part, (rep ^ 3) * part, middle, columns),
            ]
            blocks.append((base, moves))
    used = 0
    plan = []
    for base, moves in blocks:
        copies = []
        for source, start, height, offset, first, last in moves:
            edge = 0
            for buffer, width in zip(held, widths):
                low, high = max(first, edge), min(last, edge + width)
                if low < high:
                    copies.append(
                        pltpu.make_async_copy(
                            source.at[pl.ds(start, height), pl.ds(low - first, high - low)],
                            buffer.at[
                                pl.ds(pl.multiple_of(base + offset, 16), height),
                                pl.ds(low - edge, high - low),
                            ],
                            arrived.at[used],
                        )
                    )
                    used += 1
                edge += width
        plan.append((base, copies))
    for _, copies in plan:
        for copy in copies:
            copy.start()
    stores = []
    for base, copies in plan:
        for copy in copies:
            copy.wait()
        for buffer, output in zip(held, outputs):
            place = pl.ds(base, rows)
            stores.append(
                pltpu.make_async_copy(
                    buffer.at[place, :], output.at[place, :], left_here.at[len(stores)]
                )
            )
            stores[-1].start()
    for store in stores:
        store.wait()


def assemble(index, here, there, depth, part, middle, widths):
    rows = here[0].shape[0] * 2 * depth
    total = sum(widths) * rows
    count = 2 * (1 + 5 * (depth - 1)) * len(widths)
    return pl.pallas_call(
        functools.partial(assemble_kernel, depth, part, middle, widths),
        out_shape=[jax.ShapeDtypeStruct((rows, width), jnp.bfloat16) for width in widths],
        in_specs=[pl.BlockSpec(memory_space=pltpu.SMEM)] + [pl.BlockSpec(memory_space=pl.ANY)] * 12,
        out_specs=[pl.BlockSpec(memory_space=pl.ANY)] * len(widths),
        scratch_shapes=[pltpu.VMEM((rows, width), jnp.bfloat16) for width in widths]
        + [
            pltpu.SemaphoreType.DMA((count,)),
            pltpu.SemaphoreType.DMA((2 * depth * len(widths),)),
        ],
        compiler_params=pltpu.CompilerParams(vmem_limit_bytes=2 * total + (8 << 20)),
        cost_estimate=pl.CostEstimate(flops=0, bytes_accessed=0, transcendentals=0),
        name="assemble",
    )(index, *here, *there)


def body(
    groups,
    shards,
    tokens,
    lengths,
    group_live,
    w_query,
    w_key,
    w_value,
    w_out,
    w_gate,
    w_up,
    w_down,
    g_attn,
    g_query,
    g_key,
    g_ffn,
    cotangent,
):
    links = Links(groups, shards)
    shard_rows = w_query.shape[0]
    width = HD * (H + 2 * KV)

    def column(values):
        return jnp.pad(values, (0, shard_rows - values.shape[0]))[:, None]

    gains = jnp.concatenate([column(g) for g in (g_attn, g_ffn, g_query, g_key)], axis=1)
    gains = jnp.pad(gains, ((0, 0), (0, 124)))
    packed = jnp.concatenate([w_query, w_key, w_value, w_out, gains], axis=1)
    first_move = links.gather_of(packed, (width, w_out.shape[1], 128))
    gate_move = links.gather_of(w_gate, (w_gate.shape[1],))
    up_move = links.gather_of(w_up, (w_up.shape[1],))
    down_move = links.gather_of(w_down, (w_down.shape[1],))
    for _ in range(3):
        advance([first_move])
    for _ in range(3):
        advance([first_move, gate_move])
    full_qkv, full_out, full_gains = first_move.result()
    full_qkv = advance([gate_move], full_qkv)
    full_qkv = advance([up_move], full_qkv)
    head_rows = g_query.shape[0]
    all_gains = full_gains[:, :4].astype(jnp.float32)
    gain_attn = all_gains[:, 0]
    gain_ffn = all_gains[:, 1]
    gain_query = all_gains[:, 2].reshape(shards, shard_rows)[:, :head_rows].reshape(HD)
    gain_key = all_gains[:, 3].reshape(shards, shard_rows)[:, :head_rows].reshape(HD)

    row_count = tokens.shape[0]
    x_float = tokens.astype(jnp.float32)
    row_index, segment, position, keep_mask = layout(lengths[0], group_live[0], row_count)
    allowed = (segment[:, None] == segment[None, :]) & (row_index[None, :] <= row_index[:, None])
    bias = jnp.where(allowed, 0.0, masked_score).astype(jnp.float32)
    gain_rows = jnp.stack([jnp.tile(gain_query, 2), jnp.tile(gain_key, 2)])
    tables = (*rotary_tables(position), jnp.pad(gain_rows, ((0, 6), (0, 0))), bias)
    unit_one, inverse_one = normalize(x_float)
    attn_input = (unit_one * gain_attn).astype(jnp.bfloat16)
    qkv = jnp.dot(attn_input, full_qkv, preferred_element_type=jnp.float32)
    parts, logs = [], []
    for first in range(KV // 2):
        part, log = attend(qkv, tables, first, 1)
        if first == 0:
            qkv, part = advance([up_move], qkv, part)
        if first == 1:
            qkv, part = advance([gate_move], qkv, part)
        if first == 2:
            qkv, part = advance([up_move], qkv, part)
        if first == 3:
            part = advance([gate_move], part)
            part = advance([up_move], part)
            part = advance([down_move], part)
        parts.append(part)
        logs.append(log)
    attended = jnp.concatenate(parts, axis=1)
    hidden = x_float + keep_mask[:, None] * jnp.dot(
        attended, full_out, preferred_element_type=jnp.float32
    )
    unit_two, inverse_two = normalize(hidden)
    ffn_input = (unit_two * gain_ffn).astype(jnp.bfloat16)
    (full_gate,) = gate_move.result()
    full_gate = advance([down_move], full_gate)
    gate_proj = jnp.dot(ffn_input, full_gate, preferred_element_type=jnp.float32)
    gate_proj = advance([down_move], gate_proj)
    gate_proj = advance([up_move], gate_proj)
    gate_proj = advance([up_move], gate_proj)
    gate_proj = advance([down_move], gate_proj)
    (full_up,) = up_move.result()
    up_proj = jnp.dot(ffn_input, full_up, preferred_element_type=jnp.float32)
    inner_low = (jax.nn.silu(gate_proj) * up_proj).astype(jnp.bfloat16)
    inner_low = advance([down_move], inner_low)

    d_final = cotangent.astype(jnp.float32)
    d_ffn = (keep_mask[:, None] * d_final).astype(jnp.bfloat16)
    down_sum = links.sum_of([(inner_low, d_ffn)])
    d_ffn, down_sum.held = advance([down_move], d_ffn, down_sum.held)
    (full_down,) = down_move.result()
    full_down = advance([down_sum], full_down)
    d_gate, d_up = inner_back(d_ffn, full_down, gate_proj, up_proj)
    d_gate, d_up = advance([down_sum], d_gate, d_up)
    gate_sum = links.sum_of([(ffn_input, d_gate)], depth_first=True)
    d_gate, d_up = advance([gate_sum], d_gate, d_up)
    up_sum = links.sum_of([(ffn_input, d_up)])
    d_gate, d_up = advance([up_sum], d_gate, d_up)
    d_gate, d_up = advance([gate_sum], d_gate, d_up)
    d_ffn_input = ffn_back(d_gate, d_up, full_gate, full_up)
    d_hidden_norm, grad_gain_ffn = norm_back(d_ffn_input, unit_two, inverse_two, gain_ffn)
    d_hidden = d_final + d_hidden_norm
    d_attn = (keep_mask[:, None] * d_hidden).astype(jnp.bfloat16)
    d_attn = advance([down_sum], d_attn)
    d_attn = advance([up_sum], d_attn)
    d_attended = back_low(d_attn, full_out)
    plans = ([gate_sum], [], [up_sum, down_sum], [gate_sum, down_sum])
    gain_sums, outputs = 0.0, ()
    for first in range(KV // 2):
        *outputs, gain_sum = attend_back(qkv, tables, logs[first], d_attended, first, 1, outputs)
        if plans[first]:
            d_attended, *outputs = advance(plans[first], d_attended, *outputs)
        gain_sums = gain_sums + gain_sum
    d_query, d_key, d_value = outputs
    grad_gain_query = gain_sums[0, :HD] + gain_sums[0, HD:]
    grad_gain_key = gain_sums[1, :HD] + gain_sums[1, HD:]
    d_attn_input = (
        back_product(d_query, full_qkv[:, : H * HD])
        + back_product(d_key, full_qkv[:, H * HD : (H + KV) * HD])
        + back_product(d_value, full_qkv[:, (H + KV) * HD :])
    )
    d_x_norm, grad_gain_attn = norm_back(d_attn_input, unit_one, inverse_one, gain_attn)
    grad_tokens = (d_hidden + d_x_norm).astype(jnp.bfloat16)

    def spread(values):
        blocks = jnp.pad(
            values.reshape(shards, head_rows), ((0, 0), (0, shard_rows - head_rows))
        )
        return blocks.reshape(shards * shard_rows)

    gain_grads = jnp.stack(
        [grad_gain_attn, grad_gain_ffn, spread(grad_gain_query), spread(grad_gain_key)], axis=1
    )
    gain_grads = jnp.pad(gain_grads, ((0, 0), (0, 252))).astype(jnp.bfloat16)
    gain_grads = settle([up_sum], gain_grads)
    qkv_sum = links.sum_of(
        [(attn_input, value) for value in (d_query, d_key, d_value)] + [(attended, d_attn)],
        gain_grads,
    )
    for plan in ([qkv_sum], [up_sum], [qkv_sum]):
        inner_low = advance(plan, inner_low)
    block_out = ffn_out(inner_low, full_down, hidden, keep_mask[:, None])
    plans = (
        [up_sum],
        [qkv_sum],
        [gate_sum],
        [up_sum],
        [qkv_sum],
        [gate_sum],
        [up_sum],
        [qkv_sum],
        [down_sum],
        [gate_sum],
        [up_sum],
        [qkv_sum],
        [down_sum],
        [gate_sum],
        [qkv_sum],
        [down_sum],
        [qkv_sum],
    )
    for plan in plans:
        block_out = advance(plan, block_out)
    owned = qkv_sum.result()
    grad_down, grad_gate, grad_up = down_sum.result(), gate_sum.result(), up_sum.result()
    last = width + w_out.shape[1]
    return (
        block_out,
        grad_tokens,
        owned[:, : H * HD],
        owned[:, H * HD : (H + KV) * HD],
        owned[:, (H + KV) * HD : width],
        owned[:, width : width + w_out.shape[1]],
        grad_gate,
        grad_up,
        grad_down,
        owned[:, last],
        owned[:head_rows, last + 2],
        owned[:head_rows, last + 3],
        owned[:, last + 1],
    )


def solution(mesh):
    in_specs = (
        P(("rep", "shard"), None),
        P(("rep", "shard"), None),
        P("rep"),
        P("shard", None),
        P("shard", None),
        P("shard", None),
        P("shard", None),
        P("shard", None),
        P("shard", None),
        P("shard", None),
        P("shard"),
        P("shard"),
        P("shard"),
        P("shard"),
        P(("rep", "shard"), None),
    )
    out_specs = (
        P(("rep", "shard"), None),
        P(("rep", "shard"), None),
        P("shard", None),
        P("shard", None),
        P("shard", None),
        P("shard", None),
        P("shard", None),
        P("shard", None),
        P("shard", None),
        P("shard"),
        P("shard"),
        P("shard"),
        P("shard"),
    )
    return jax.shard_map(
        functools.partial(body, mesh.shape["rep"], mesh.shape["shard"]),
        mesh=mesh,
        in_specs=in_specs,
        out_specs=out_specs,
        check_vma=False,
    )
```
